256 devices in a mesh: ctx: 64 (over y, x, z_lo, core), head: 4 (over z_hi).
Axes of the slice: x: 4, y: 4, z: 8 (z_hi: 4, z_lo: 2; z = z_hi * 2 + z_lo), core: 2. Of those that a mesh axis runs over, the one named last changes fastest.
Arguments:
- placement: int32 [128], replicated, may hold values from 0 to 127, each once
- queries: bfloat16 [12288, 2048], P('ctx', 'head'), may hold values from -5 to 5
- keys: bfloat16 [12288, 512], P('ctx', 'head'), may hold values from -5 to 5
- values: bfloat16 [12288, 512], P('ctx', 'head'), may hold values from -6 to 6
- cotangent: bfloat16 [12288, 4096], P('ctx', 'head'), may hold values from -6 to 6
- out_weight: bfloat16 [2048, 4096], P('head'), may hold values from -0.125 to 0.125
Outputs:
- query_grad: bfloat16 [12288, 2048], P('ctx', 'head')
- key_gradient: bfloat16 [12288, 512], P('ctx', 'head')
- value_gradient: bfloat16 [12288, 512], P('ctx', 'head')
The draws below stay inside these ranges and needn't reach their ends.
Inputs may be any that keep to these rules, and one draw needn't show every extreme that they name: `placement`: every span number appears exactly once.
All inputs are finite; a program needn't handle non-finite values.
Results may differ from the reference program's by a relative error of at most 0.011.
Values may be sent and summed in bfloat16 or wider, within the bound.
A program may use at most 128 MiB of HBM per device.

```python
import math
import jax
import jax.numpy as jnp
from jax import lax

D = 4096
QUERY_HEADS = 16
KEY_VALUE_HEADS = 4
HEAD_SIZE = 128
BLOCK = 32
TOK_DEV = 192
SEQUENCE_TOKENS = 12288
N_CTX = 64


def draw_queries(key, part):
    key = jax.random.fold_in(key, 3)
    first_key = jax.random.fold_in(key, 0)
    rank_four_shape = (SEQUENCE_TOKENS, KEY_VALUE_HEADS, QUERY_HEADS // KEY_VALUE_HEADS, HEAD_SIZE)
    sampled_draws = jax.random.normal(first_key, rank_four_shape, jnp.float32)
    return jnp.clip(sampled_draws, -5.0, 5.0).reshape(SEQUENCE_TOKENS, QUERY_HEADS * HEAD_SIZE).astype(jnp.bfloat16)


def draw_keys(key, part):
    key = jax.random.fold_in(key, 5)
    first_key = jax.random.fold_in(key, 0)
    rank_three_shape = (SEQUENCE_TOKENS, KEY_VALUE_HEADS, HEAD_SIZE)
    sampled_draws = jax.random.normal(first_key, rank_three_shape, jnp.float32)
    return jnp.clip(sampled_draws, -5.0, 5.0).reshape(SEQUENCE_TOKENS, KEY_VALUE_HEADS * HEAD_SIZE).astype(jnp.bfloat16)


def block_levels(own_key, shape, shards, smallest, largest):
    factor_of, own = 1.0, jax.random.fold_in(own_key, 6)
    for axis_at, parts in shards:
        draws = jnp.exp(jax.random.uniform(jax.random.fold_in(own, axis_at), (parts,), jnp.float32, smallest / len(shards), largest / len(shards)))
        factor_of = factor_of * jnp.repeat(draws, shape[axis_at] // parts).reshape([-1 if axis == axis_at else 1 for axis in range(len(shape))])
    return factor_of


def noise(stream_key, dims, spread, most, shards=(), kind=jnp.bfloat16):
    result = jax.random.normal(stream_key, dims, jnp.float32) * spread
    if len(shards) > 0:
        result = block_levels(stream_key, dims, shards, -0.22, 0.18) * result
    return jnp.clip(result, min=-most, max=most).astype(kind)


def setup_inputs(seed: int = 0) -> dict:
    arg_keys = jax.random.split(jax.random.key(seed), 7)
    return {
        "placement": jax.random.permutation(arg_keys[0], 2 * N_CTX).astype(jnp.int32),
        "queries": draw_queries(jax.random.fold_in(arg_keys[6], 71), 0),
        "keys": draw_keys(jax.random.fold_in(arg_keys[6], 71), 0),
        "values": noise(arg_keys[3], (SEQUENCE_TOKENS, KEY_VALUE_HEADS * HEAD_SIZE), 1.0, 6.0, ((0, 64), (1, 4))),
        "cotangent": noise(arg_keys[4], (SEQUENCE_TOKENS, D), 1.0, 6.0, ((0, 64), (1, 4))),
        "out_weight": noise(arg_keys[5], (QUERY_HEADS * HEAD_SIZE, D), (QUERY_HEADS * HEAD_SIZE) ** -0.5, 0.125, ((0, 4),)),
    }


def reference(placement, queries, keys, values, cotangent, out_weight):
    count_of_tokens = queries.shape[0]
    span_rows = TOK_DEV // 2
    group_width = QUERY_HEADS // KEY_VALUE_HEADS
    score_scale = 1.0 / math.sqrt(HEAD_SIZE)
    row_index = jnp.arange(count_of_tokens, dtype=jnp.int32)
    position = placement[row_index // span_rows] * span_rows + row_index % span_rows
    block_of = (position // BLOCK).astype(jnp.int32)
    grad_out = jnp.dot(cotangent, out_weight.T, preferred_element_type=jnp.float32).astype(jnp.bfloat16)
    query_heads = queries.reshape(count_of_tokens, QUERY_HEADS, HEAD_SIZE).transpose(1, 0, 2)
    grad_heads = grad_out.reshape(count_of_tokens, QUERY_HEADS, HEAD_SIZE).transpose(1, 0, 2)
    heads_of_keys = keys.reshape(count_of_tokens, KEY_VALUE_HEADS, HEAD_SIZE).transpose(1, 0, 2)
    heads_of_values = values.reshape(count_of_tokens, KEY_VALUE_HEADS, HEAD_SIZE).transpose(1, 0, 2)
    block_count = count_of_tokens // TOK_DEV

    def one_head(head_inputs):
        query_head, grad_head, head_index = head_inputs
        key_head = heads_of_keys[head_index // group_width]
        value_head = heads_of_values[head_index // group_width]

        def block_step(carry, block_inputs):
            key_acc, value_acc = carry
            query_block, grad_block, query_blocks = block_inputs
            logits = jnp.dot(query_block, key_head.T, preferred_element_type=jnp.float32) * score_scale
            visible = block_of[None, :] <= query_blocks[:, None]
            logits = jnp.where(visible, logits, -jnp.inf)
            log_total = jax.nn.logsumexp(logits, axis=1)
            weights = jnp.where(visible, jnp.exp(logits - log_total[:, None]), 0.0)
            rounded = weights.astype(jnp.bfloat16)
            output = jnp.dot(rounded, value_head, preferred_element_type=jnp.float32)
            row_delta = lax.optimization_barrier(jnp.sum(grad_block.astype(jnp.float32) * output, axis=1))
            grad_probs = jnp.dot(grad_block, value_head.T, preferred_element_type=jnp.float32)
            grad_logits = (weights * (grad_probs - row_delta[:, None])).astype(jnp.bfloat16)
            query_part = jnp.dot(grad_logits, key_head, preferred_element_type=jnp.float32) * score_scale
            key_acc = key_acc + jnp.dot(grad_logits.T, query_block, preferred_element_type=jnp.float32) * score_scale
            value_acc = value_acc + jnp.dot(rounded.T, grad_block, preferred_element_type=jnp.float32)
            return ((key_acc, value_acc), query_part)
        initial = (jnp.zeros((count_of_tokens, HEAD_SIZE), jnp.float32), jnp.zeros((count_of_tokens, HEAD_SIZE), jnp.float32))
        (key_acc, value_acc), query_parts = lax.scan(block_step, initial, (query_head.reshape(block_count, TOK_DEV, HEAD_SIZE), grad_head.reshape(block_count, TOK_DEV, HEAD_SIZE), block_of.reshape(block_count, TOK_DEV)))
        return (query_parts.reshape(count_of_tokens, HEAD_SIZE), key_acc, value_acc)
    head_ids = jnp.arange(QUERY_HEADS, dtype=jnp.int32)
    query_parts, key_portions, value_portions = lax.map(one_head, (query_heads, grad_heads, head_ids))
    query_grad = query_parts.transpose(1, 0, 2).reshape(count_of_tokens, QUERY_HEADS * HEAD_SIZE).astype(jnp.bfloat16)
    key_gradient = key_portions.reshape(KEY_VALUE_HEADS, group_width, count_of_tokens, HEAD_SIZE).sum(axis=1)
    value_gradient = value_portions.reshape(KEY_VALUE_HEADS, group_width, count_of_tokens, HEAD_SIZE).sum(axis=1)
    key_gradient = key_gradient.transpose(1, 0, 2).reshape(count_of_tokens, KEY_VALUE_HEADS * HEAD_SIZE).astype(jnp.bfloat16)
    value_gradient = value_gradient.transpose(1, 0, 2).reshape(count_of_tokens, KEY_VALUE_HEADS * HEAD_SIZE).astype(jnp.bfloat16)
    return (query_grad, key_gradient, value_gradient)
```

```python
import functools
import math
import jax, jax.numpy as jnp
from jax import lax
from jax.experimental import pallas as pl
from jax.experimental.pallas import tpu as pltpu
from jax.sharding import PartitionSpec as P

SPAN = 96
C2 = math.log2(math.e) / math.sqrt(128.0)
NEG = -1e30
NQ = 8
NK = 32
CH = 512
TL = 128


def dot(a, b, ca, cb):
    return lax.dot_general(a, b, (((ca,), (cb,)), ((), ())), preferred_element_type=jnp.float32)


def sort_slots(place, part, before, order, inv):
    def clear(s, _):
        inv[s] = -1
        return 0
    lax.fori_loop(0, 128, clear, 0)
    def put(s, _):
        g = (s // 2) * 8 + part * 2 + s % 2
        inv[place[g]] = s
        return 0
    lax.fori_loop(0, NK, put, 0)
    def scan(p, count):
        before[p] = count
        order[count] = inv[p]
        return count + (inv[p] >= 0).astype(jnp.int32)
    lax.fori_loop(0, 128, scan, 0)


def slot_limits(place, before, inv, plane, t):
    span = place[plane * 8 + t]
    full = before[span] * SPAN
    own = (inv[span] >= 0).astype(jnp.int32)
    end = full + own * SPAN
    col = lax.broadcasted_iota(jnp.int32, (1, 4 * SPAN), 1)
    sub = (col % SPAN) // 32 + 1
    limit = full + own * 32 * sub
    return full, end, limit


def heads_down(ref, t):
    rows = pl.ds(pl.multiple_of(t * SPAN, SPAN), SPAN)
    return jnp.concatenate([ref[rows, h * 128:(h + 1) * 128] for h in range(4)], axis=0)


def fwd_kernel(where, place, q_ref, k_ref, v_ref, o_ref, m_ref, l_ref, ks, vs, vt, before, order, inv):
    plane, part = where()
    sort_slots(place, part, before, order, inv)
    def gather(r, _):
        src = pl.ds(pl.multiple_of(order[r] * SPAN, SPAN), SPAN)
        dst = pl.ds(pl.multiple_of(r * SPAN, SPAN), SPAN)
        ks[dst, :] = k_ref[src, :]
        vs[dst, :] = v_ref[src, :]
        return 0
    lax.fori_loop(0, NK, gather, 0)
    for i in range(NK * SPAN // 512):
        vt[:, i * 512:(i + 1) * 512] = vs[i * 512:(i + 1) * 512, :].T

    def one_slot(t, _):
        full, end, limit = slot_limits(place, before, inv, plane, t)
        qc = heads_down(q_ref, t)
        o_ref[t] = jnp.zeros((128, 384), jnp.float32)

        def step(base, rows, carry, masked):
            m, l = carry
            base = pl.multiple_of(base, TL)
            s = dot(ks[pl.ds(base, rows), :], qc, 1, 1) * C2
            if masked:
                idx = base + lax.broadcasted_iota(jnp.int32, (rows, 384), 0)
                s = jnp.where(idx < limit, s, NEG)
            m2 = jnp.maximum(m, jnp.max(s, axis=0, keepdims=True))
            a = jnp.exp2(m - m2)
            p = jnp.exp2(s - m2)
            if masked:
                p = jnp.where(idx < limit, p, 0.0)
            l2 = l * a + jnp.sum(p, axis=0, keepdims=True)
            o_ref[t] = o_ref[t] * a + dot(vt[:, pl.ds(base, rows)], p.astype(jnp.bfloat16), 1, 0)
            return m2, l2

        init = (jnp.full((1, 384), NEG, jnp.float32), jnp.zeros((1, 384), jnp.float32))
        nf = full // CH
        carry = lax.fori_loop(0, nf, lambda i, c: step(i * CH, CH, c, False), init)
        nt = full // TL
        carry = lax.fori_loop(nf * (CH // TL), nt, lambda i, c: step(i * TL, TL, c, False), carry)
        m, l = lax.fori_loop(nt, (end + TL - 1) // TL, lambda i, c: step(i * TL, TL, c, True), carry)
        m_ref[t] = m
        l_ref[t] = l
        return 0
    lax.fori_loop(0, NQ, one_slot, 0)


def bwd_kernel(where, place, q_ref, g_ref, k_ref, v_ref, ls_ref, de_ref, dq_ref, dk_ref, dv_ref,
               ks, vs, kt, dks, dvs, dqt, before, order, inv):
    plane, part = where()
    sort_slots(place, part, before, order, inv)
    def gather(r, _):
        src = pl.ds(pl.multiple_of(order[r] * SPAN, SPAN), SPAN)
        dst = pl.ds(pl.multiple_of(r * SPAN, SPAN), SPAN)
        ks[dst, :] = k_ref[src, :]
        vs[dst, :] = v_ref[src, :]
        dks[dst, :] = jnp.zeros((SPAN, 128), jnp.float32)
        dvs[dst, :] = jnp.zeros((SPAN, 128), jnp.float32)
        return 0
    lax.fori_loop(0, NK, gather, 0)
    for i in range(NK * SPAN // 512):
        kt[:, i * 512:(i + 1) * 512] = ks[i * 512:(i + 1) * 512, :].T

    def one_slot(t, _):
        full, end, limit = slot_limits(place, before, inv, plane, t)
        qc = heads_down(q_ref, t)
        gc = heads_down(g_ref, t)
        ls = ls_ref[t]
        de = de_ref[t]
        dqt[...] = jnp.zeros((128, 384), jnp.float32)

        def step(base, rows, masked):
            base = pl.multiple_of(base, TL)
            at = pl.ds(base, rows)
            s = dot(ks[at, :], qc, 1, 1)
            dp = dot(vs[at, :], gc, 1, 1)
            p = jnp.exp2(s * C2 - ls)
            if masked:
                idx = base + lax.broadcasted_iota(jnp.int32, (rows, 384), 0)
                p = jnp.where(idx < limit, p, 0.0)
            ds = (p * (dp - de)).astype(jnp.bfloat16)
            dvs[at, :] += dot(p.astype(jnp.bfloat16), gc, 1, 0)
            dks[at, :] += dot(ds, qc, 1, 0)
            dqt[...] += dot(kt[:, at], ds, 1, 0)

        def full_step(i, c):
            step(i * CH, CH, False)
            return c
        def tail_step(i, c):
            step(i * TL, TL, False)
            return c
        def masked_step(i, c):
            step(i * TL, TL, True)
            return c
        nf = full // CH
        lax.fori_loop(0, nf, full_step, 0)
        nt = full // TL
        lax.fori_loop(nf * (CH // TL), nt, tail_step, 0)
        lax.fori_loop(nt, (end + TL - 1) // TL, masked_step, 0)
        dq = dqt[...].T * (1.0 / math.sqrt(128.0))
        rows = pl.ds(pl.multiple_of(t * SPAN, SPAN), SPAN)
        for h in range(4):
            dq_ref[rows, h * 128:(h + 1) * 128] = dq[h * SPAN:(h + 1) * SPAN].astype(jnp.bfloat16)
        return 0
    lax.fori_loop(0, NQ, one_slot, 0)
    def scatter(r, _):
        src = pl.ds(pl.multiple_of(r * SPAN, SPAN), SPAN)
        dst = pl.ds(pl.multiple_of(order[r] * SPAN, SPAN), SPAN)
        dk_ref[dst, :] = (dks[src, :] * (1.0 / math.sqrt(128.0))).astype(jnp.bfloat16)
        dv_ref[dst, :] = dvs[src, :].astype(jnp.bfloat16)
        return 0
    lax.fori_loop(0, NK, scatter, 0)

VM = pl.BlockSpec(memory_space=pltpu.VMEM)
SM = pl.BlockSpec(memory_space=pltpu.SMEM)
INTS = [pltpu.SMEM((128,), jnp.int32), pltpu.SMEM((NK + 1,), jnp.int32), pltpu.SMEM((128,), jnp.int32)]
LIM = 48 * 1024 * 1024


def fwd(where, place, q, k, v):

    return pl.pallas_call(
        functools.partial(fwd_kernel, where),
        out_shape=(jax.ShapeDtypeStruct((NQ, 128, 384), jnp.float32), jax.ShapeDtypeStruct((NQ, 1, 384), jnp.float32), jax.ShapeDtypeStruct((NQ, 1, 384), jnp.float32)),
        in_specs=[SM, VM, VM, VM], out_specs=(VM, VM, VM),
        scratch_shapes=[pltpu.VMEM((3072, 128), jnp.bfloat16), pltpu.VMEM((3072, 128), jnp.bfloat16), pltpu.VMEM((128, 3072), jnp.bfloat16)] + INTS,
        compiler_params=pltpu.CompilerParams(vmem_limit_bytes=LIM), name="fwd_k",
    )(place, q, k, v)


def bwd(where, place, q, g, k, v, ls, de):

    return pl.pallas_call(
        functools.partial(bwd_kernel, where),
        out_shape=(jax.ShapeDtypeStruct((768, 512), jnp.bfloat16), jax.ShapeDtypeStruct((3072, 128), jnp.bfloat16), jax.ShapeDtypeStruct((3072, 128), jnp.bfloat16)),
        in_specs=[SM] + [VM] * 6, out_specs=(VM, VM, VM),
        scratch_shapes=[pltpu.VMEM((3072, 128), jnp.bfloat16), pltpu.VMEM((3072, 128), jnp.bfloat16), pltpu.VMEM((128, 3072), jnp.bfloat16),
            pltpu.VMEM((3072, 128), jnp.float32), pltpu.VMEM((3072, 128), jnp.float32), pltpu.VMEM((128, 384), jnp.float32)] + INTS,
        compiler_params=pltpu.CompilerParams(vmem_limit_bytes=LIM), name="bwd_k",
    )(place, q, g, k, v, ls, de)

MESH = pl.DeviceIdType.MESH
LO, HI = pl.ds(0, SPAN), pl.ds(SPAN, SPAN)
ALL = pl.ds(0, 2 * SPAN)
OFFSETS = (0, -1, 1, 2)


def coords():
    me = lax.axis_index("ctx")
    return me // 16, (me // 4) % 4, (me // 2) % 2, me % 2


def device(y, x, z, c):
    return {"ctx": ((y + 4) % 4 * 4 + (x + 4) % 4) * 4 + z * 2 + c}


def greet():
    y, x, z, c = coords()
    barrier = pltpu.get_barrier_semaphore()
    near = [(y, x + 1, z, c), (y, x - 1, z, c), (y + 1, x, z, c), (y - 1, x, z, c), (y, x, 1 - z, c), (y, x, z, 1 - c)]
    for n in near:
        pl.semaphore_signal(barrier, inc=1, device_id=device(*n), device_id_type=MESH)
    pl.semaphore_wait(barrier, len(near))


def remote(src, dst, send, recv, n, to):
    return pltpu.make_async_remote_copy(
        src_ref=src, dst_ref=dst, send_sem=send.at[n], recv_sem=recv.at[n], device_id=device(*to), device_id_type=MESH
    )


def group_share(own, out, send, recv):
    y, x, z, c = coords()
    core, chip = (y, x, z, 1 - c), (y, x, 1 - z, c)
    mine, far = z * 2 + c, (1 - z) * 2 + c

    def cp(src, block, n, to):
        return remote(src, out.at[block], send, recv, n, to)

    to_chip, to_core = cp(own, mine, 0, chip), cp(own, mine, 1, core)
    onward = cp(out.at[far], far, 2, core)
    from_chip, from_core = cp(out.at[far], far, 0, chip), cp(out.at[z * 2 + 1 - c], z * 2 + 1 - c, 1, core)
    from_far = cp(out.at[(1 - z) * 2 + 1 - c], (1 - z) * 2 + 1 - c, 2, core)
    return (to_chip, to_core, onward), (from_chip, from_core, from_far)


def plane_gather(own, out, x_first, send, recv):
    y, x, z, c = coords()

    def place(da, db):
        dy, dx = (db, da) if x_first else (da, db)
        return (y + dy, x + dx, z, c)

    def block(da, db):
        yy, xx, _, _ = place(da, db)
        return (yy + 4) % 4, (xx + 4) % 4

    def cp(n, sa, sb, rows, to, src=None):
        yy, xx = block(sa, sb)
        ref = out.at[yy, xx, rows]
        return remote(ref if src is None else src, ref, send, recv, n, place(*to))

    sends, recvs = {}, {}
    for d, half in ((1, LO), (-1, HI)):
        i = (1 - d) // 2
        sends["a", d] = cp(i, 0, 0, ALL, (d, 0), own)
        recvs["a", d] = cp(i, -d, 0, ALL, (d, 0))
        sends["aa", d] = cp(2 + i, -d, 0, half, (d, 0))
        recvs["aa", d] = cp(2 + i, -2 * d, 0, half, (d, 0))
        for k, e in enumerate(OFFSETS):
            sends["b", e, d] = cp(4 + 4 * k + i, e, 0, ALL, (0, d), own if e == 0 else None)
            recvs["b", e, d] = cp(4 + 4 * k + i, e, -d, ALL, (0, d))
            sends["bb", e, d] = cp(6 + 4 * k + i, e, -d, half, (0, d))
            recvs["bb", e, d] = cp(6 + 4 * k + i, e, -2 * d, half, (0, d))
    return sends, recvs


def share_kernel(q_ref, k_ref, v_ref, qa, ka, va, qs, qr, ks, kr, vs, vr):
    y, x, z, c = coords()
    greet()
    planes = [plane_gather(k_ref, ka, True, ks, kr), plane_gather(v_ref, va, False, vs, vr)]
    q_send, q_recv = group_share(q_ref, qa, qs, qr)
    q_send[0].start()
    for s, _ in planes:
        for d in (1, -1):
            s["a", d].start()
    for s, _ in planes:
        for d in (1, -1):
            s["b", 0, d].start()
    q_send[1].start()
    qa[z * 2 + c] = q_ref[...]
    ka[y, x] = k_ref[...]
    va[y, x] = v_ref[...]
    for d in (1, -1):
        for s, r in planes:
            r["a", d].wait_recv()
            s["aa", d].start()
            s["b", -d, 1].start()
            s["b", -d, -1].start()
    for d in (1, -1):
        for s, r in planes:
            r["b", 0, d].wait_recv()
            s["bb", 0, d].start()
    for s, r in planes:
        r["aa", 1].wait_recv()
        r["aa", -1].wait_recv()
        s["b", 2, 1].start()
        s["b", 2, -1].start()
    q_recv[0].wait_recv()
    q_send[2].start()
    for e in (-1, 1, 2):
        for d in (1, -1):
            for s, r in planes:
                r["b", e, d].wait_recv()
                s["bb", e, d].start()
    for e in OFFSETS:
        for d in (1, -1):
            for s, r in planes:
                r["bb", e, d].wait_recv()
    q_recv[1].wait_recv()
    q_recv[2].wait_recv()
    for s, _ in planes:
        for copy in s.values():
            copy.wait_send()
    for copy in q_send:
        copy.wait_send()


def stats_kernel(g_ref, o_ref, m_ref, l_ref, ga, ls_ref, de_ref, part, stats, gs, gr, ss, sr):
    y, x, z, c = coords()
    mine = z * 2 + c
    greet_group()
    g_send, g_recv = group_share(g_ref, ga, gs, gr)
    g_send[0].start()
    g_send[1].start()
    ga[mine] = g_ref[...]

    def inner(block):
        for s in range(2):
            rows = ga[block, s * SPAN:(s + 1) * SPAN, :]
            down = jnp.concatenate([rows[:, h * 128:(h + 1) * 128] for h in range(4)], axis=0)
            down = down.astype(jnp.float32).T
            part[block * 2 + s] = jnp.sum(down * o_ref[block * 2 + s], axis=0, keepdims=True)

    inner(mine)
    g_recv[0].wait_recv()
    g_send[2].start()
    inner((1 - z) * 2 + c)
    g_recv[1].wait_recv()
    inner(z * 2 + 1 - c)
    g_recv[2].wait_recv()
    inner((1 - z) * 2 + 1 - c)
    for t in range(NQ):
        stats[mine, t:t + 1, :] = m_ref[t]
        stats[mine, NQ + t:NQ + t + 1, :] = l_ref[t]
        stats[mine, 2 * NQ + t:2 * NQ + t + 1, :] = part[t]
    others = [(z, 1 - c), (1 - z, c), (1 - z, 1 - c)]
    sent = [remote(stats.at[mine], stats.at[mine], ss, sr, n, (y, x, zz, cc)) for n, (zz, cc) in enumerate(others)]
    came = [remote(stats.at[zz * 2 + cc], stats.at[zz * 2 + cc], ss, sr, n, (y, x, zz, cc)) for n, (zz, cc) in enumerate(others)]
    for copy in sent:
        copy.start()
    for copy in came:
        copy.wait_recv()
    tops = [stats[j, 0:NQ, :] for j in range(4)]
    top = jnp.maximum(jnp.maximum(tops[0], tops[1]), jnp.maximum(tops[2], tops[3]))
    scales = [jnp.exp2(m - top) for m in tops]
    total = sum(scales[j] * stats[j, NQ:2 * NQ, :] for j in range(4))
    delta = sum(scales[j] * stats[j, 2 * NQ:3 * NQ, :] for j in range(4)) / total
    level = top + jnp.log(total) * math.log2(math.e)
    for t in range(NQ):
        ls_ref[t] = level[t:t + 1, :]
        de_ref[t] = delta[t:t + 1, :]
    for copy in sent:
        copy.wait_send()
    for copy in g_send:
        copy.wait_send()


def greet_group():
    y, x, z, c = coords()
    barrier = pltpu.get_barrier_semaphore()
    near = [(y, x, 1 - z, c), (y, x, z, 1 - c), (y, x, 1 - z, 1 - c)]
    for n in near:
        pl.semaphore_signal(barrier, inc=1, device_id=device(*n), device_id_type=MESH)
    pl.semaphore_wait(barrier, len(near))


def f32(a):
    return a.astype(jnp.float32)


def plane_reduce(src, out, x_first, far1, near1, stage1, acc, far2, near2, stage2, send, recv):
    y, x, z, c = coords()
    first = x if x_first else y
    second = y if x_first else x

    def to1(d):
        return (y, x + d, z, c) if x_first else (y + d, x, z, c)

    def to2(d):
        return (y + d, x, z, c) if x_first else (y, x + d, z, c)

    def line(d, rows):
        i = (first + d + 4) % 4
        return src.at[:, i, rows] if x_first else src.at[i, :, rows]

    def load(d):
        i = (first + d + 4) % 4
        return src[:, i] if x_first else src[i]

    def cp(s, t, n, to):
        return remote(s, t, send, recv, n, to)

    halves = ((0, 1, LO, HI, slice(0, SPAN), slice(SPAN, 2 * SPAN)), (1, -1, HI, LO, slice(SPAN, 2 * SPAN), slice(0, SPAN)))
    sends = []

    def go(copy):
        copy.start()
        sends.append(copy)

    def step0():
        for i, d, half, other, _, _ in halves:
            go(cp(line(2, half), far1.at[i], i, to1(d)))
        for i, d, half, other, _, _ in halves:
            go(cp(line(d, other), near1.at[i, :, other], 2 + i, to1(d)))

    def step1():
        for i, d, half, other, hs, _ in halves:
            cp(far1.at[i], far1.at[i], i, to1(d)).wait_recv()
            stage1[i] = (f32(load(d)[:, hs]) + f32(far1[i])).astype(jnp.bfloat16)
            go(cp(stage1.at[i], near1.at[i, :, half], 4 + i, to1(d)))

    def step2():
        for i, d, half, other, _, _ in halves:
            cp(near1.at[i, :, other], near1.at[i, :, other], 2 + i, to1(d)).wait_recv()
            cp(near1.at[i, :, half], near1.at[i, :, half], 4 + i, to1(d)).wait_recv()
        acc[...] = (f32(load(0)) + f32(near1[0]) + f32(near1[1])).astype(jnp.bfloat16)
        for i, d, half, other, _, _ in halves:
            go(cp(acc.at[(second + 2) % 4, half], far2.at[i], 6 + i, to2(d)))
        for i, d, half, other, _, _ in halves:
            go(cp(acc.at[(second + d + 4) % 4, other], near2.at[i, other], 8 + i, to2(d)))

    def step3():
        for i, d, half, other, hs, _ in halves:
            cp(far2.at[i], far2.at[i], 6 + i, to2(d)).wait_recv()
            stage2[i] = (f32(acc[(second + d + 4) % 4, hs]) + f32(far2[i])).astype(jnp.bfloat16)
            go(cp(stage2.at[i], near2.at[i, half], 10 + i, to2(d)))

    def step4():
        for i, d, half, other, _, _ in halves:
            cp(near2.at[i, other], near2.at[i, other], 8 + i, to2(d)).wait_recv()
            cp(near2.at[i, half], near2.at[i, half], 10 + i, to2(d)).wait_recv()
        out[...] = (f32(acc[second]) + f32(near2[0]) + f32(near2[1])).astype(jnp.bfloat16)

    def finish():
        for copy in sends:
            copy.wait_send()

    return [step0, step1, step2, step3, step4, finish]


def reduce_kernel(dq_ref, dk_ref, dv_ref, qo, ko, vo, q1, q2, qstage, qs, qr, *rest):
    y, x, z, c = coords()
    greet()
    core, chip = (y, x, z, 1 - c), (y, x, 1 - z, c)
    k_steps = plane_reduce(dk_ref, ko, False, *rest[:9])
    v_steps = plane_reduce(dv_ref, vo, True, *rest[9:])
    other = remote(dq_ref.at[(1 - z) * 2 + 1 - c], q1.at[1 - z], qs, qr, 0, core)
    same = remote(dq_ref.at[z * 2 + 1 - c], q1.at[z], qs, qr, 1, core)
    across = remote(qstage, q2, qs, qr, 2, chip)
    k_steps[0]()
    v_steps[0]()
    other.start()
    same.start()
    other.wait_recv()
    qstage[...] = (f32(dq_ref[(1 - z) * 2 + c]) + f32(q1[1 - z])).astype(jnp.bfloat16)
    across.start()
    for k_step, v_step in list(zip(k_steps, v_steps))[1:5]:
        k_step()
        v_step()
    same.wait_recv()
    across.wait_recv()
    qo[...] = (f32(dq_ref[z * 2 + c]) + f32(q1[z]) + f32(q2[...])).astype(jnp.bfloat16)
    k_steps[5]()
    v_steps[5]()
    for copy in (other, same, across):
        copy.wait_send()


def sems(n):
    return [pltpu.SemaphoreType.DMA((n,)), pltpu.SemaphoreType.DMA((n,))]


def bf16(*shape):
    return jax.ShapeDtypeStruct(shape, jnp.bfloat16)


def single(*shape):
    return jax.ShapeDtypeStruct(shape, jnp.float32)


def remote_params(n):
    return pltpu.CompilerParams(collective_id=n, has_side_effects=True, vmem_limit_bytes=LIM)


def share(q, k, v):
    return pl.pallas_call(
        share_kernel,
        out_shape=(bf16(4, 192, 512), bf16(4, 4, 192, 128), bf16(4, 4, 192, 128)),
        in_specs=[VM] * 3, out_specs=(VM,) * 3,
        scratch_shapes=sems(3) + sems(20) + sems(20),
        compiler_params=remote_params(0), name="share_k",
    )(q, k, v)


def stats(g, o, m, l):
    return pl.pallas_call(
        stats_kernel,
        out_shape=(bf16(4, 192, 512), single(NQ, 1, 384), single(NQ, 1, 384)),
        in_specs=[VM] * 4, out_specs=(VM,) * 3,
        scratch_shapes=[pltpu.VMEM((NQ, 1, 384), jnp.float32), pltpu.VMEM((4, 3 * NQ, 384), jnp.float32)] + sems(3) + sems(3),
        compiler_params=remote_params(1), name="stats_k",
    )(g, o, m, l)


def reduce(dq, dk, dv):
    def vm(*shape):
        return pltpu.VMEM(shape, jnp.bfloat16)
    plane = [vm(2, 4, SPAN, 128), vm(2, 4, 2 * SPAN, 128), vm(2, 4, SPAN, 128), vm(4, 2 * SPAN, 128),
             vm(2, SPAN, 128), vm(2, 2 * SPAN, 128), vm(2, SPAN, 128)] + sems(12)
    return pl.pallas_call(
        reduce_kernel,
        out_shape=(bf16(192, 512), bf16(192, 128), bf16(192, 128)),
        in_specs=[VM] * 3, out_specs=(VM,) * 3,
        scratch_shapes=[vm(2, 192, 512), vm(192, 512), vm(192, 512)] + sems(3) + plane + plane,
        compiler_params=remote_params(2), name="reduce_k",
    )(dq, dk, dv)


def where():
    y, x, z, c = coords()
    return y * 4 + x, z * 2 + c


def local(placement, queries, keys, values, cotangent, out_weight):
    whole = lax.all_gather(cotangent, "head", axis=1, tiled=True)
    q_all, k_all, v_all = share(queries, keys, values)
    q_all = q_all.reshape(768, 512)
    k_all = k_all.reshape(3072, 128)
    v_all = v_all.reshape(3072, 128)
    o, m, l = fwd(where, placement, q_all, k_all, v_all)
    grad = lax.dot_general(whole, out_weight, (((1,), (1,)), ((), ())), preferred_element_type=jnp.float32).astype(jnp.bfloat16)
    g_all, ls, de = stats(grad, o, m, l)
    dq, dk, dv = bwd(where, placement, q_all, g_all.reshape(768, 512), k_all, v_all, ls, de)
    return reduce(dq.reshape(4, 192, 512), dk.reshape(4, 4, 192, 128), dv.reshape(4, 4, 192, 128))


def solution(mesh):
    in_specs = (P(), P("ctx", "head"), P("ctx", "head"), P("ctx", "head"), P("ctx", "head"), P("head", None))
    out_specs = (P("ctx", "head"), P("ctx", "head"), P("ctx", "head"))
    return jax.shard_map(local, mesh=mesh, in_specs=in_specs, out_specs=out_specs, check_vma=False)
```

```python
import functools
import math

import jax
import jax.numpy as jnp
from jax import lax
from jax.experimental import pallas as pl
from jax.experimental.pallas import tpu as pltpu
from jax.sharding import PartitionSpec as P

SPAN = 96
SCALE = 1.0 / math.sqrt(128.0)
C2 = math.log2(math.e) * SCALE
NEG = -1e30
NQ = 8
NK = 32
CH = 512
DEEP = 3
COLS = 4 * SPAN
PAIR_A, PAIR_B, PAIR_C, PAIR_F, ONE_T, ONE_C, FULL, OWN, ORDER, PAIRS, ONES = 0, 32, 64, 96, 128, 160, 192, 200, 208, 248, 249
TABLE = 256


def dot(a, b, ca, cb):
    return lax.dot_general(a, b, (((ca,), (cb,)), ((), ())), preferred_element_type=jnp.float32)


def int_of(flag):
    return jnp.where(flag, 1, 0).astype(jnp.int32)


def make_table(keys, plane, tab, rank):
    for r in range(NK):
        tab[ORDER + r] = keys[2, r]
    spans = [keys[3, plane * 8 + t] for t in range(NQ)]
    for t in range(NQ):
        tab[FULL + t] = keys[0, spans[t]] * SPAN
        tab[OWN + t] = int_of(keys[1, spans[t]] >= 0)
        rank[sum(int_of(spans[u] < spans[t]) for u in range(NQ) if u != t)] = t

    def pair(i, counts):
        pairs, ones = counts
        a, b = rank[2 * i], rank[2 * i + 1]
        full = tab[FULL + a]
        chunks_a = (full + tab[OWN + a] * SPAN + CH - 1) // CH
        chunks_b = (tab[FULL + b] + tab[OWN + b] * SPAN + CH - 1) // CH

        def put_pair(c, _):
            tab[PAIR_A + pairs + c] = a
            tab[PAIR_B + pairs + c] = b
            tab[PAIR_C + pairs + c] = c
            tab[PAIR_F + pairs + c] = int_of((c + 1) * CH > full)
            return 0
        lax.fori_loop(0, chunks_a, put_pair, 0)

        def put_one(c, _):
            tab[ONE_T + ones + c - chunks_a] = b
            tab[ONE_C + ones + c - chunks_a] = c
            return 0
        lax.fori_loop(chunks_a, chunks_b, put_one, 0)
        return pairs + chunks_a, ones + jnp.maximum(chunks_b - chunks_a, 0)
    pairs, ones = lax.fori_loop(0, NQ // 2, pair, (jnp.int32(0), jnp.int32(0)))
    tab[PAIRS] = pairs
    tab[ONES] = ones
    tab[PAIR_A + pairs] = 0
    tab[PAIR_B + pairs] = 1
    tab[PAIR_C + pairs] = 0
    tab[PAIR_F + pairs] = 0


def limits(tab, slots):
    col = lax.broadcasted_iota(jnp.int32, (1, COLS), 1)
    sub = 32 * ((col % SPAN) // 32 + 1)
    return jnp.concatenate([tab[FULL + t] + tab[OWN + t] * sub for t in slots], axis=1)


def visible(tab, slots, chunk):
    idx = lax.broadcasted_iota(jnp.int32, (CH, COLS * len(slots)), 0)
    return idx < limits(tab, slots) - chunk * CH


def side(ref, slots, axis):
    return jnp.concatenate([ref[t] for t in slots], axis=axis) if len(slots) > 1 else ref[slots[0]]


def rows_of(chunk):
    return pl.ds(pl.multiple_of(chunk * CH, CH), CH)


def fwd_kernel(where, keys, qd, k_ref, v_ref, o_ref, m_ref, l_ref, ks, vs, tab, pairs_p, ones_p, pairs_m, ones_m,
               vt, s0, s1, x0, x1, rank, p0, p1, po, sems):
    plane, _ = where()
    make_table(keys, plane, tab, rank)

    def sort(r, _):
        src = pl.ds(pl.multiple_of(tab[ORDER + r] * SPAN, SPAN), SPAN)
        dst = pl.ds(pl.multiple_of(r * SPAN, SPAN), SPAN)
        ks[dst, :] = k_ref[src, :]
        vs[dst, :] = v_ref[src, :]
        return 0
    lax.fori_loop(0, NK, sort, 0)
    for i in range(NK * SPAN // 512):
        vt[:, i * 512:(i + 1) * 512] = vs[i * 512:(i + 1) * 512, :].T
    o_ref[...] = jnp.zeros_like(o_ref)
    m_ref[...] = jnp.full(m_ref.shape, NEG, jnp.float32)
    l_ref[...] = jnp.zeros_like(l_ref)

    def scores(slots, chunk):
        return dot(ks[rows_of(chunk), :], side(qd, slots, 0), 1, 1) * C2

    def accumulate(slots, chunk, s, top, keep, kept_m, n):
        m = side(m_ref, slots, 1)
        m2 = jnp.maximum(m, top)
        a = jnp.exp2(m - m2)
        p = jnp.exp2(s - m2)
        l2 = side(l_ref, slots, 1) * a + jnp.sum(p, axis=0, keepdims=True)
        pb = p.astype(jnp.bfloat16)
        keep[...] = pb
        kept_m[n] = m2
        o = dot(vt[:, rows_of(chunk)], pb, 1, 0)
        for i, t in enumerate(slots):
            at = slice(i * COLS, (i + 1) * COLS)
            m_ref[t] = m2[:, at]
            l_ref[t] = l2[:, at]
            o_ref[t] = o_ref[t] * a[:, at] + o[:, at]

    def item(n):
        return [tab[PAIR_A + n], tab[PAIR_B + n]], tab[PAIR_C + n]

    def produce(n, buf, top):
        slots, chunk = item(n)
        s = scores(slots, chunk)
        buf[...] = s
        top[...] = jnp.max(s, axis=0, keepdims=True)

    def fix(n, buf, top):
        @pl.when(tab[PAIR_F + n] == 1)
        def _():
            slots, chunk = item(n)
            s = jnp.where(visible(tab, slots, chunk), buf[...], NEG)
            buf[...] = s
            top[...] = jnp.max(s, axis=0, keepdims=True)

    def save(n, keep, i):
        return pltpu.make_async_copy(keep, pairs_p.at[n], sems.at[i])

    def consume(n, buf, top, keep, i):
        slots, chunk = item(n)
        accumulate(slots, chunk, buf[...], top[...], keep, pairs_m, n)
        save(n, keep, i).start()

    count = tab[PAIRS]

    @pl.when(count > 0)
    def _():
        produce(0, s0, x0)
        fix(0, s0, x0)

    def two(i, _):
        @pl.when(i > 0)
        def _():
            save(0, p0, 0).wait()
        produce(2 * i + 1, s1, x1)
        consume(2 * i, s0, x0, p0, 0)
        fix(2 * i + 1, s1, x1)

        @pl.when(i > 0)
        def _():
            save(0, p1, 1).wait()
        produce(2 * i + 2, s0, x0)
        consume(2 * i + 1, s1, x1, p1, 1)
        fix(2 * i + 2, s0, x0)
        return 0
    lax.fori_loop(0, count // 2, two, 0)

    @pl.when(count // 2 > 0)
    def _():
        save(0, p0, 0).wait()
        save(0, p1, 1).wait()

    @pl.when(count % 2 == 1)
    def _():
        consume(count - 1, s0, x0, p0, 0)

    def save_one(n):
        return pltpu.make_async_copy(po, ones_p.at[n], sems.at[2])

    def one(n, _):
        slots, chunk = [tab[ONE_T + n]], tab[ONE_C + n]
        s = jnp.where(visible(tab, slots, chunk), scores(slots, chunk), NEG)

        @pl.when(n > 0)
        def _():
            save_one(0).wait()
        accumulate(slots, chunk, s, jnp.max(s, axis=0, keepdims=True), po, ones_m, n)
        save_one(n).start()
        return 0
    lax.fori_loop(0, tab[ONES], one, 0)

    @pl.when(tab[ONES] > 0)
    def _():
        save_one(0).wait()

    @pl.when(count % 2 == 1)
    def _():
        save(0, p0, 0).wait()


def bwd_kernel(tab, qd, gt, vs, kt, ls_ref, de_ref, pairs_p, ones_p, pairs_m, ones_m, dq_ref, dk_ref, dv_ref,
               dks, dvs, dqt, p_ring, o_ring, sems):
    pairs, ones = tab[PAIRS], tab[ONES]

    def load(src, n, ring, first):
        return pltpu.make_async_copy(src.at[n], ring.at[n % DEEP], sems.at[first + n % DEEP])

    for i in range(DEEP - 1):
        @pl.when(pairs > i)
        def _():
            load(pairs_p, i, p_ring, 0).start()
    for i in range(DEEP - 1):
        @pl.when(ones > i)
        def _():
            load(ones_p, i, o_ring, DEEP).start()
    dks[...] = jnp.zeros_like(dks)
    dvs[...] = jnp.zeros_like(dvs)
    dqt[...] = jnp.zeros_like(dqt)

    def step(slots, chunk, p_ref, m):
        at = rows_of(chunk)
        part = jnp.exp2(m - side(ls_ref, slots, 1))
        gs = (side(gt, slots, 1).astype(jnp.float32) * part).astype(jnp.bfloat16)
        p = p_ref[...]
        dp = dot(vs[at, :], gs, 1, 0)
        ds = p * (dp - side(de_ref, slots, 1) * part).astype(jnp.bfloat16)
        dvs[at, :] += dot(p, gs, 1, 1)
        dks[at, :] += dot(ds, side(qd, slots, 0), 1, 0)
        dq = dot(kt[:, at], ds, 1, 0)
        for i, t in enumerate(slots):
            dqt[t] += dq[:, i * COLS:(i + 1) * COLS]

    def run(src, count, first, ring, body):
        def visit(n, _):
            @pl.when(n + DEEP - 1 < count)
            def _():
                load(src, n + DEEP - 1, ring, first).start()
            load(src, n, ring, first).wait()
            body(n, ring.at[n % DEEP])
            return 0
        lax.fori_loop(0, count, visit, 0)

    run(pairs_p, pairs, 0, p_ring,
        lambda n, buf: step([tab[PAIR_A + n], tab[PAIR_B + n]], tab[PAIR_C + n], buf, pairs_m[n]))
    run(ones_p, ones, DEEP, o_ring, lambda n, buf: step([tab[ONE_T + n]], tab[ONE_C + n], buf, ones_m[n]))

    for t in range(NQ):
        dq_ref[t] = (dqt[t].T * SCALE).astype(jnp.bfloat16)

    def scatter(r, _):
        src = pl.ds(pl.multiple_of(r * SPAN, SPAN), SPAN)
        dst = pl.ds(pl.multiple_of(tab[ORDER + r] * SPAN, SPAN), SPAN)
        dk_ref[dst, :] = (dks[src, :] * SCALE).astype(jnp.bfloat16)
        dv_ref[dst, :] = dvs[src, :].astype(jnp.bfloat16)
        return 0
    lax.fori_loop(0, NK, scatter, 0)


VM = pl.BlockSpec(memory_space=pltpu.VMEM)
SM = pl.BlockSpec(memory_space=pltpu.SMEM)
ANY = pl.BlockSpec(memory_space=pl.ANY)
LIM = 28 * 1024 * 1024
KEYS = NK * SPAN


def bf16(*shape):
    return jax.ShapeDtypeStruct(shape, jnp.bfloat16)


def single(*shape):
    return jax.ShapeDtypeStruct(shape, jnp.float32)


def vm(*shape):
    return pltpu.VMEM(shape, jnp.bfloat16)


def vm32(*shape):
    return pltpu.VMEM(shape, jnp.float32)


def cost(flops, nbytes):
    return pl.CostEstimate(flops=flops, bytes_accessed=nbytes, transcendentals=0)


def fwd(where, keys, q, k, v):
    return pl.pallas_call(
        functools.partial(fwd_kernel, where),
        out_shape=(single(NQ, 128, COLS), single(NQ, 1, COLS), single(NQ, 1, COLS), bf16(KEYS, 128), bf16(KEYS, 128),
                   jax.ShapeDtypeStruct((TABLE,), jnp.int32), bf16(24, CH, 2 * COLS), bf16(24, CH, COLS),
                   single(24, 1, 2 * COLS), single(24, 1, COLS)),
        in_specs=[SM, VM, VM, VM], out_specs=(VM,) * 5 + (SM, ANY, ANY, VM, VM),
        scratch_shapes=[vm(128, KEYS), vm32(CH, 2 * COLS), vm32(CH, 2 * COLS), vm32(1, 2 * COLS), vm32(1, 2 * COLS),
                        pltpu.SMEM((NQ,), jnp.int32), vm(CH, 2 * COLS), vm(CH, 2 * COLS), vm(CH, COLS),
                        pltpu.SemaphoreType.DMA((3,))],
        compiler_params=pltpu.CompilerParams(vmem_limit_bytes=LIM), cost_estimate=cost(10**10, 8 * 10**6), name="fwd_k",
    )(keys, q, k, v)


def bwd(tab, q, g, v, kt, ls, de, pp, po, mp, mo):
    return pl.pallas_call(
        bwd_kernel,
        out_shape=(bf16(NQ, COLS, 128), bf16(KEYS, 128), bf16(KEYS, 128)),
        in_specs=[SM] + [VM] * 6 + [ANY, ANY, VM, VM], out_specs=(VM, VM, VM),
        scratch_shapes=[vm32(KEYS, 128), vm32(KEYS, 128), vm32(NQ, 128, COLS), vm(DEEP, CH, 2 * COLS),
                        vm(DEEP, CH, COLS), pltpu.SemaphoreType.DMA((2 * DEEP,))],
        compiler_params=pltpu.CompilerParams(vmem_limit_bytes=LIM), cost_estimate=cost(2 * 10**10, 8 * 10**6), name="bwd_k",
    )(tab, q, g, v, kt, ls, de, pp, po, mp, mo)

MESH = pl.DeviceIdType.MESH
LO, HI = pl.ds(0, SPAN), pl.ds(SPAN, SPAN)
ALL = pl.ds(0, 2 * SPAN)
OFFSETS = (0, -1, 1, 2)


def coords():
    me = lax.axis_index("ctx")
    return me // 16, (me // 4) % 4, (me // 2) % 2, me % 2


def device(y, x, z, c):
    return {"ctx": ((y + 4) % 4 * 4 + (x + 4) % 4) * 4 + z * 2 + c}


def head_at(d):
    return {"head": (lax.axis_index("head") + d + 4) % 4}


def greet(heads):
    y, x, z, c = coords()
    barrier = pltpu.get_barrier_semaphore()
    near = [(y, x, 1 - z, c), (y, x, z, 1 - c)]
    for d in (1, -1, 2):
        near += [(y, x + d, z, c), (y + d, x, z, c)]
    ids = [device(*n) for n in near]
    if heads:
        ids += [head_at(1), head_at(-1)]
    for n in ids:
        pl.semaphore_signal(barrier, inc=1, device_id=n, device_id_type=MESH)
    pl.semaphore_wait(barrier, len(ids))


def remote(src, dst, send, recv, n, to):
    return pltpu.make_async_remote_copy(
        src_ref=src, dst_ref=dst, send_sem=send.at[n], recv_sem=recv.at[n], device_id=device(*to), device_id_type=MESH
    )


def group_share(own, out, pick, send, recv, first):
    y, x, z, c = coords()
    core, chip = (y, x, z, 1 - c), (y, x, 1 - z, c)
    mine, far, beside, across = z * 2 + c, (1 - z) * 2 + c, z * 2 + 1 - c, (1 - z) * 2 + 1 - c

    def cp(src, block, n, to):
        return remote(pick(src.at[block]), pick(out.at[block]), send, recv, first + n, to)

    sends = cp(own, mine, 0, chip), cp(own, mine, 1, core), cp(out, far, 2, core)
    recvs = cp(out, far, 0, chip), cp(out, beside, 1, core), cp(out, across, 2, core)
    return sends, recvs


def plane_gather(out, send, recv, x_first):
    y, x, z, c = coords()

    def place(da, db):
        dy, dx = (db, da) if x_first else (da, db)
        return (y + dy, x + dx, z, c)

    def block(da, db):
        yy, xx, _, _ = place(da, db)
        return (yy + 4) % 4, (xx + 4) % 4

    def cp(n, sa, sb, rows, to):
        yy, xx = block(sa, sb)
        ref = out.at[yy, xx, rows]
        return remote(ref, ref, send, recv, n, place(*to))

    sends, recvs = {}, {}
    for i, d in enumerate((1, -1, 2)):
        sends["a", d] = cp(i, 0, 0, ALL, (d, 0))
        recvs["a", d] = cp(i, -d, 0, ALL, (d, 0))
    for d, half in ((1, LO), (-1, HI)):
        i = (1 - d) // 2
        for k, e in enumerate(OFFSETS):
            sends["b", e, d] = cp(4 + 4 * k + i, e, 0, ALL, (0, d))
            recvs["b", e, d] = cp(4 + 4 * k + i, e, -d, ALL, (0, d))
            sends["bb", e, d] = cp(6 + 4 * k + i, e, -d, half, (0, d))
            recvs["bb", e, d] = cp(6 + 4 * k + i, e, -2 * d, half, (0, d))
    return sends, recvs


def key_order(place, part):
    slot = lax.broadcasted_iota(jnp.int32, (128, 128), 0)
    lane = lax.broadcasted_iota(jnp.int32, (128, 128), 1)
    across = jnp.broadcast_to(f32(place), (128, 128))
    down = across.T
    position = f32(lane)
    own = jnp.where((slot % 8) // 2 == part, 1.0, 0.0)
    name = f32(slot // 8 * 2 + slot % 2)
    before = jnp.sum(jnp.where(down < position, own, 0.0), axis=0, keepdims=True)
    held = jnp.sum(jnp.where(down == position, own * (name + 1.0), 0.0), axis=0, keepdims=True) - 1.0
    own_lane = jnp.where((lane % 8) // 2 == part, 1.0, 0.0)
    rank = jnp.sum(jnp.where(across < down, own_lane, 0.0), axis=1, keepdims=True)
    order = jnp.sum(jnp.where(rank == position, own * name, 0.0), axis=0, keepdims=True)
    return jnp.concatenate([before, held, order, f32(place)], axis=0).astype(jnp.int32)


def order_kernel(place, keys):
    _, _, z, c = coords()
    keys[...] = key_order(place[...], z * 2 + c)


def share_kernel(_, q_ref, k_ref, v_ref, c_ref, qa, ka, va, up, down, here, qs, qr, ks, kr, vs, vr, cs, cr):
    y, x, z, c = coords()
    mine = z * 2 + c
    lo, hi = c_ref.at[LO], c_ref.at[HI]
    loads = [pltpu.make_async_copy(k_ref, ka.at[y, x], here.at[0]), pltpu.make_async_copy(v_ref, va.at[y, x], here.at[1])]
    for s in range(2):
        for h in range(4):
            loads.append(pltpu.make_async_copy(
                q_ref.at[s * SPAN:(s + 1) * SPAN, h * 128:(h + 1) * 128], qa.at[mine, s, h * SPAN:(h + 1) * SPAN],
                here.at[2 + s * 4 + h]))
    loads += [pltpu.make_async_copy(hi, up.at[0], here.at[10]), pltpu.make_async_copy(lo, down.at[0], here.at[11])]
    for load in loads:
        load.start()
    greet(True)
    to_up = pltpu.make_async_remote_copy(
        src_ref=lo, dst_ref=up.at[1], send_sem=cs.at[0], recv_sem=cr.at[0], device_id=head_at(1), device_id_type=MESH)
    to_down = pltpu.make_async_remote_copy(
        src_ref=hi, dst_ref=down.at[1], send_sem=cs.at[1], recv_sem=cr.at[1], device_id=head_at(-1), device_id_type=MESH)
    planes = [plane_gather(ka, ks, kr, True), plane_gather(va, vs, vr, False)]
    q_send, q_recv = group_share(qa, qa, lambda ref: ref, qs, qr, 0)
    for load in loads[:2]:
        load.wait()
    for s, _ in planes:
        for d in (1, -1, 2):
            s["a", d].start()
    for s, _ in planes:
        for d in (1, -1):
            s["b", 0, d].start()
    for load in loads[2:]:
        load.wait()
    q_send[0].start()
    q_send[1].start()
    to_up.start()
    to_down.start()
    for d, e in ((1, -1), (-1, 1)):
        for s, r in planes:
            r["a", d].wait_recv()
            s["b", e, 1].start()
            s["b", e, -1].start()
    for d in (1, -1):
        for s, r in planes:
            r["b", 0, d].wait_recv()
            s["bb", 0, d].start()
    for s, r in planes:
        r["a", 2].wait_recv()
        s["b", 2, 1].start()
        s["b", 2, -1].start()
    q_recv[0].wait_recv()
    q_send[2].start()
    for e in (-1, 1, 2):
        for d in (1, -1):
            for s, r in planes:
                r["b", e, d].wait_recv()
                s["bb", e, d].start()
    for e in OFFSETS:
        for d in (1, -1):
            for s, r in planes:
                r["bb", e, d].wait_recv()
    q_recv[1].wait_recv()
    q_recv[2].wait_recv()
    for s, _ in planes:
        for copy in s.values():
            copy.wait_send()
    for copy in q_send:
        copy.wait_send()
    to_up.wait()
    to_down.wait()


def stats_kernel(up, down, from_low, from_high, w_ref, o_ref, m_ref, l_ref, k_ref, gt, ls_ref, de_ref, kt, ga, part, levels, deltas, gs, gr, ss, sr):
    y, x, z, c = coords()
    mine = z * 2 + c
    head = lax.axis_index("head")
    greet_group()

    others = [(z, 1 - c), (1 - z, c), (1 - z, 1 - c)]

    def spread(ref, first):
        sent = [remote(ref.at[mine], ref.at[mine], ss, sr, first + n, (y, x, zz, cc)) for n, (zz, cc) in enumerate(others)]
        came = [remote(ref.at[zz * 2 + cc], ref.at[zz * 2 + cc], ss, sr, first + n, (y, x, zz, cc))
                for n, (zz, cc) in enumerate(others)]
        return sent, came

    for t in range(NQ):
        levels[mine, t:t + 1, :] = m_ref[t]
        levels[mine, NQ + t:NQ + t + 1, :] = l_ref[t]
    levels_sent, levels_came = spread(levels, 0)
    for copy in levels_sent:
        copy.start()

    def term(block, d):
        cols = pl.ds(pl.multiple_of((head + d + 4) % 4 * 1024, 1024), 1024)
        return dot(block, w_ref[:, cols], 1, 1)

    def whole(low, high):
        return jnp.concatenate([low, high], axis=0)

    grad = term(whole(down[0], up[0]), 0) + term(whole(up[1], from_low[0]), -1)
    grad += term(whole(from_high[0], down[1]), 1) + term(whole(from_low[1], from_high[1]), 2)
    grad = grad.astype(jnp.bfloat16)
    shares = [group_share(ga, ga, lambda ref, s=s: ref.at[s], gs, gr, 3 * s) for s in range(2)]
    for s in range(2):
        ga[mine, s] = jnp.concatenate([grad[s * SPAN:(s + 1) * SPAN, h * 128:(h + 1) * 128] for h in range(4)], axis=0)
        shares[s][0][0].start()
        shares[s][0][1].start()

    def inner(block, s):
        t = block * 2 + s
        down = ga[block, s].T
        gt[t] = down
        part[t] = jnp.sum(f32(down) * o_ref[t], axis=0, keepdims=True)

    for i in range(NK * SPAN // 512):
        kt[:, i * 512:(i + 1) * 512] = k_ref[i * 512:(i + 1) * 512, :].T
    for s in range(2):
        inner(mine, s)
    for s in range(2):
        shares[s][1][1].wait_recv()
        inner(z * 2 + 1 - c, s)
    for s in range(2):
        shares[s][1][0].wait_recv()
        shares[s][0][2].start()
        inner((1 - z) * 2 + c, s)
    for s in range(2):
        shares[s][1][2].wait_recv()
        inner((1 - z) * 2 + 1 - c, s)
    for t in range(NQ):
        deltas[mine, t:t + 1, :] = part[t]
    deltas_sent, deltas_came = spread(deltas, 3)
    for copy in deltas_sent:
        copy.start()
    for copy in levels_came:
        copy.wait_recv()
    tops = [levels[j, 0:NQ, :] for j in range(4)]
    top = jnp.maximum(jnp.maximum(tops[0], tops[1]), jnp.maximum(tops[2], tops[3]))
    scales = [jnp.exp2(m - top) for m in tops]
    total = sum(scales[j] * levels[j, NQ:2 * NQ, :] for j in range(4))
    level = top + jnp.log(total) * math.log2(math.e)
    for copy in deltas_came:
        copy.wait_recv()
    delta = sum(scales[j] * deltas[j] for j in range(4)) / total
    for t in range(NQ):
        ls_ref[t] = level[t:t + 1, :]
        de_ref[t] = delta[t:t + 1, :]
    for copy in levels_sent + deltas_sent:
        copy.wait_send()
    for s in range(2):
        for copy in shares[s][0]:
            copy.wait_send()


def greet_group():
    y, x, z, c = coords()
    barrier = pltpu.get_barrier_semaphore()
    near = [(y, x, 1 - z, c), (y, x, z, 1 - c), (y, x, 1 - z, 1 - c)]
    for n in near:
        pl.semaphore_signal(barrier, inc=1, device_id=device(*n), device_id_type=MESH)
    pl.semaphore_wait(barrier, len(near))


def f32(a):
    return a.astype(jnp.float32)


def plane_reduce(src, out, x_first, far1, near1, stage1, acc, near2, send, recv):
    y, x, z, c = coords()
    first = x if x_first else y
    second = y if x_first else x

    def to1(d):
        return (y, x + d, z, c) if x_first else (y + d, x, z, c)

    def to2(d):
        return (y + d, x, z, c) if x_first else (y, x + d, z, c)

    def line(d, rows):
        i = (first + d + 4) % 4
        return src.at[:, i, rows] if x_first else src.at[i, :, rows]

    def load(d):
        i = (first + d + 4) % 4
        return src[:, i] if x_first else src[i]

    def cp(s, t, n, to):
        return remote(s, t, send, recv, n, to)

    halves = ((0, 1, LO, HI, slice(0, SPAN), slice(SPAN, 2 * SPAN)), (1, -1, HI, LO, slice(SPAN, 2 * SPAN), slice(0, SPAN)))
    sends = []

    def go(copy):
        copy.start()
        sends.append(copy)

    def step0():
        for i, d, half, other, _, _ in halves:
            go(cp(line(2, half), far1.at[i], i, to1(d)))
        for i, d, half, other, _, _ in halves:
            go(cp(line(d, other), near1.at[i, :, other], 2 + i, to1(d)))

    def step1():
        for i, d, half, other, hs, _ in halves:
            cp(far1.at[i], far1.at[i], i, to1(d)).wait_recv()
            stage1[i] = (f32(load(d)[:, hs]) + f32(far1[i])).astype(jnp.bfloat16)
            go(cp(stage1.at[i], near1.at[i, :, half], 4 + i, to1(d)))

    def step2():
        for i, d, half, other, _, _ in halves:
            cp(near1.at[i, :, other], near1.at[i, :, other], 2 + i, to1(d)).wait_recv()
            cp(near1.at[i, :, half], near1.at[i, :, half], 4 + i, to1(d)).wait_recv()
        acc[...] = (f32(load(0)) + f32(near1[0]) + f32(near1[1])).astype(jnp.bfloat16)
        for i, d in enumerate((2, 1, -1)):
            go(cp(acc.at[(second + d + 4) % 4], near2.at[i], 6 + i, to2(d)))

    def step3():
        for i, d in enumerate((2, 1, -1)):
            cp(near2.at[i], near2.at[i], 6 + i, to2(d)).wait_recv()
        out[...] = (f32(acc[second]) + f32(near2[0]) + f32(near2[1]) + f32(near2[2])).astype(jnp.bfloat16)

    def finish():
        for copy in sends:
            copy.wait_send()

    return [step0, step1, step2, step3, finish]


def reduce_kernel(dq_ref, dk_ref, dv_ref, qo, ko, vo, q1, q2, qstage, qs, qr, *rest):
    y, x, z, c = coords()
    greet(False)
    core, chip = (y, x, z, 1 - c), (y, x, 1 - z, c)
    k_steps = plane_reduce(dk_ref, ko, False, *rest[:7])
    v_steps = plane_reduce(dv_ref, vo, True, *rest[7:])
    other = remote(dq_ref.at[(1 - z) * 2 + 1 - c], q1.at[1 - z], qs, qr, 0, core)
    same = remote(dq_ref.at[z * 2 + 1 - c], q1.at[z], qs, qr, 1, core)
    across = remote(qstage, q2, qs, qr, 2, chip)
    k_steps[0]()
    v_steps[0]()
    other.start()
    same.start()
    other.wait_recv()
    qstage[...] = (f32(dq_ref[(1 - z) * 2 + c]) + f32(q1[1 - z])).astype(jnp.bfloat16)
    across.start()
    for k_step, v_step in list(zip(k_steps, v_steps))[1:4]:
        k_step()
        v_step()
    same.wait_recv()
    across.wait_recv()
    total = (f32(dq_ref[z * 2 + c]) + f32(q1[z]) + f32(q2[...])).astype(jnp.bfloat16)
    for s in range(2):
        for h in range(4):
            qo[s * SPAN:(s + 1) * SPAN, h * 128:(h + 1) * 128] = total[s, h * SPAN:(h + 1) * SPAN]
    k_steps[4]()
    v_steps[4]()
    for copy in (other, same, across):
        copy.wait_send()


def sems(n):
    return [pltpu.SemaphoreType.DMA((n,)), pltpu.SemaphoreType.DMA((n,))]


def remote_params(n, limit=LIM):
    return pltpu.CompilerParams(collective_id=n, has_side_effects=True, vmem_limit_bytes=limit)


def key_table(place):
    return pl.pallas_call(
        order_kernel, out_shape=jax.ShapeDtypeStruct((4, 128), jnp.int32), in_specs=[VM], out_specs=VM,
        compiler_params=pltpu.CompilerParams(vmem_limit_bytes=LIM), cost_estimate=cost(10**10, 10**6), name="order_k",
    )(place)


def finish_kernel(*refs):
    sems = refs[-1]
    copies = [pltpu.make_async_copy(refs[i], refs[3 + i], sems.at[i]) for i in range(3)]
    for copy in copies:
        copy.start()
    for copy in copies:
        copy.wait()


def finish(*args):
    return pl.pallas_call(
        finish_kernel, out_shape=tuple(bf16(*a.shape) for a in args), in_specs=[VM] * 3, out_specs=(ANY,) * 3,
        scratch_shapes=[pltpu.SemaphoreType.DMA((3,))],
        compiler_params=pltpu.CompilerParams(vmem_limit_bytes=LIM), cost_estimate=cost(10**6, 10**6), name="finish_k",
    )(*args)


def share(*args):
    return pl.pallas_call(
        share_kernel,
        out_shape=(bf16(4, 2, COLS, 128), bf16(4, 4, 192, 128), bf16(4, 4, 192, 128), bf16(2, SPAN, 1024), bf16(2, SPAN, 1024)),
        in_specs=[ANY] * 5, out_specs=(VM,) * 5,
        scratch_shapes=[pltpu.SemaphoreType.DMA((12,))] + sems(3) + sems(20) + sems(20) + sems(2),
        compiler_params=remote_params(0), cost_estimate=cost(10**10, 8 * 10**6), name="share_k",
    )(*args)


def stats(*args):
    return pl.pallas_call(
        stats_kernel,
        out_shape=(bf16(NQ, 128, COLS), single(NQ, 1, COLS), single(NQ, 1, COLS), bf16(128, KEYS)),
        in_specs=[VM] * 9, out_specs=(VM,) * 4,
        scratch_shapes=[vm(4, 2, COLS, 128), vm32(NQ, 1, COLS), vm32(4, 2 * NQ, COLS), vm32(4, NQ, COLS)] + sems(6) + sems(6),
        compiler_params=remote_params(1), cost_estimate=cost(10**9, 8 * 10**6), name="stats_k",
    )(*args)


def reduce(dq, dk, dv):
    plane = [vm(2, 4, SPAN, 128), vm(2, 4, 2 * SPAN, 128), vm(2, 4, SPAN, 128), vm(4, 2 * SPAN, 128),
             vm(3, 2 * SPAN, 128)] + sems(9)
    return pl.pallas_call(
        reduce_kernel,
        out_shape=(bf16(192, 512), bf16(192, 128), bf16(192, 128)),
        in_specs=[VM] * 3, out_specs=(VM,) * 3,
        scratch_shapes=[vm(2, 2, COLS, 128), vm(2, COLS, 128), vm(2, COLS, 128)] + sems(3) + plane + plane,
        compiler_params=remote_params(2), name="reduce_k",
    )(dq, dk, dv)


def where():
    y, x, z, c = coords()
    return y * 4 + x, z * 2 + c


def local(placement, queries, keys, values, cotangent, out_weight):
    order = key_table(placement.reshape(1, 128))
    q_all, k_all, v_all, up, down = share(order, queries, keys, values, cotangent)
    from_low = lax.ppermute(up, "head", [(i, (i + 1) % 4) for i in range(4)])
    from_high = lax.ppermute(down, "head", [(i, (i + 3) % 4) for i in range(4)])
    q_all = q_all.reshape(NQ, COLS, 128)
    o, m, l, ks, vs, tab, *kept = fwd(where, order, q_all, k_all.reshape(KEYS, 128), v_all.reshape(KEYS, 128))
    gt, ls, de, kt = stats(up, down, from_low, from_high, out_weight, o, m, l, ks)
    dq, dk, dv = bwd(tab, q_all, gt, vs, kt, ls, de, *kept)
    return finish(*reduce(dq.reshape(4, 2, COLS, 128), dk.reshape(4, 4, 192, 128), dv.reshape(4, 4, 192, 128)))


def solution(mesh):
    in_specs = (P(), P("ctx", "head"), P("ctx", "head"), P("ctx", "head"), P("ctx", "head"), P("head", None))
    out_specs = (P("ctx", "head"), P("ctx", "head"), P("ctx", "head"))
    return jax.shard_map(local, mesh=mesh, in_specs=in_specs, out_specs=out_specs, check_vma=False)
```

```python
import functools
import math

import jax
import jax.numpy as jnp
from jax import lax
from jax.experimental import pallas as pl
from jax.experimental.pallas import tpu as pltpu
from jax.sharding import PartitionSpec as P

SPAN = 96
SCALE = 1.0 / math.sqrt(128.0)
C2 = math.log2(math.e) * SCALE
NEG = -1e30
NQ = 8
NK = 32
CH = 512
BLOCKS = NQ * NK * SPAN // CH
COLS = 4 * SPAN
PAIR_A, PAIR_B, PAIR_C, PAIR_F, ONE_T, ONE_C, FULL, OWN, ORDER, PAIRS, ONES = 0, 32, 64, 96, 128, 160, 192, 200, 208, 248, 249
TABLE = 256


def dot(a, b, ca, cb):
    return lax.dot_general(a, b, (((ca,), (cb,)), ((), ())), preferred_element_type=jnp.float32)


def int_of(flag):
    return jnp.where(flag, 1, 0).astype(jnp.int32)


def make_table(keys, plane, tab, rank):
    for r in range(NK):
        tab[ORDER + r] = keys[2, r]
    spans = [keys[3, plane * 8 + t] for t in range(NQ)]
    for t in range(NQ):
        tab[FULL + t] = keys[0, spans[t]] * SPAN
        tab[OWN + t] = int_of(keys[1, spans[t]] >= 0)
        rank[sum(int_of(spans[u] < spans[t]) for u in range(NQ) if u != t)] = t

    def pair(i, counts):
        pairs, ones = counts
        a, b = rank[2 * i], rank[2 * i + 1]
        full = tab[FULL + a]
        chunks_a = (full + tab[OWN + a] * SPAN + CH - 1) // CH
        chunks_b = (tab[FULL + b] + tab[OWN + b] * SPAN + CH - 1) // CH

        def put_pair(c, _):
            tab[PAIR_A + pairs + c] = a
            tab[PAIR_B + pairs + c] = b
            tab[PAIR_C + pairs + c] = c
            tab[PAIR_F + pairs + c] = int_of((c + 1) * CH > full)
            return 0
        lax.fori_loop(0, chunks_a, put_pair, 0)

        def put_one(c, _):
            tab[ONE_T + ones + c - chunks_a] = b
            tab[ONE_C + ones + c - chunks_a] = c
            return 0
        lax.fori_loop(chunks_a, chunks_b, put_one, 0)
        return pairs + chunks_a, ones + jnp.maximum(chunks_b - chunks_a, 0)
    pairs, ones = lax.fori_loop(0, NQ // 2, pair, (jnp.int32(0), jnp.int32(0)))
    tab[PAIRS] = pairs
    tab[ONES] = ones
    tab[PAIR_A + pairs] = 0
    tab[PAIR_B + pairs] = 1
    tab[PAIR_C + pairs] = 0
    tab[PAIR_F + pairs] = 0


def limits(tab, slots):
    col = lax.broadcasted_iota(jnp.int32, (1, COLS), 1)
    sub = 32 * ((col % SPAN) // 32 + 1)
    return jnp.concatenate([tab[FULL + t] + tab[OWN + t] * sub for t in slots], axis=1)


def visible(tab, slots, chunk):
    idx = lax.broadcasted_iota(jnp.int32, (CH, COLS * len(slots)), 0)
    return idx < limits(tab, slots) - chunk * CH


def side(ref, slots, axis):
    return jnp.concatenate([ref[t] for t in slots], axis=axis) if len(slots) > 1 else ref[slots[0]]


def rows_of(chunk):
    return pl.ds(pl.multiple_of(chunk * CH, CH), CH)


def fwd_kernel(where, keys, qd, k_ref, v_ref, o_ref, m_ref, l_ref, ks, vs, tab, kept, pairs_m, ones_m,
               vt, s0, s1, x0, x1, rank):
    plane, _ = where()
    make_table(keys, plane, tab, rank)

    def sort(r, _):
        src = pl.ds(pl.multiple_of(tab[ORDER + r] * SPAN, SPAN), SPAN)
        dst = pl.ds(pl.multiple_of(r * SPAN, SPAN), SPAN)
        ks[dst, :] = k_ref[src, :]
        vs[dst, :] = v_ref[src, :]
        return 0
    lax.fori_loop(0, NK, sort, 0)
    for i in range(NK * SPAN // 512):
        vt[:, i * 512:(i + 1) * 512] = vs[i * 512:(i + 1) * 512, :].T
    o_ref[...] = jnp.zeros_like(o_ref)
    m_ref[...] = jnp.full(m_ref.shape, NEG, jnp.float32)
    l_ref[...] = jnp.zeros_like(l_ref)

    def scores(slots, chunk):
        return dot(ks[rows_of(chunk), :], side(qd, slots, 0), 1, 1) * C2

    def accumulate(slots, chunk, s, top, block, kept_m, n):
        m = side(m_ref, slots, 1)
        m2 = jnp.maximum(m, top)
        a = jnp.exp2(m - m2)
        p = jnp.exp2(s - m2)
        l2 = side(l_ref, slots, 1) * a + jnp.sum(p, axis=0, keepdims=True)
        pb = p.astype(jnp.bfloat16)
        kept_m[n] = m2
        o = dot(vt[:, rows_of(chunk)], pb, 1, 0)
        for i, t in enumerate(slots):
            at = slice(i * COLS, (i + 1) * COLS)
            kept[block + i] = pb[:, at]
            m_ref[t] = m2[:, at]
            l_ref[t] = l2[:, at]
            o_ref[t] = o_ref[t] * a[:, at] + o[:, at]

    def item(n):
        return [tab[PAIR_A + n], tab[PAIR_B + n]], tab[PAIR_C + n]

    def produce(n, buf, top):
        slots, chunk = item(n)
        s = scores(slots, chunk)
        buf[...] = s
        top[...] = jnp.max(s, axis=0, keepdims=True)

    def fix(n, buf, top):
        @pl.when(tab[PAIR_F + n] == 1)
        def _():
            slots, chunk = item(n)
            s = jnp.where(visible(tab, slots, chunk), buf[...], NEG)
            buf[...] = s
            top[...] = jnp.max(s, axis=0, keepdims=True)

    def consume(n, buf, top):
        slots, chunk = item(n)
        accumulate(slots, chunk, buf[...], top[...], 2 * n, pairs_m, n)

    count = tab[PAIRS]

    @pl.when(count > 0)
    def _():
        produce(0, s0, x0)
        fix(0, s0, x0)

    def two(i, _):
        produce(2 * i + 1, s1, x1)
        consume(2 * i, s0, x0)
        fix(2 * i + 1, s1, x1)
        produce(2 * i + 2, s0, x0)
        consume(2 * i + 1, s1, x1)
        fix(2 * i + 2, s0, x0)
        return 0
    lax.fori_loop(0, count // 2, two, 0)

    @pl.when(count % 2 == 1)
    def _():
        consume(count - 1, s0, x0)

    def one(n, _):
        slots, chunk = [tab[ONE_T + n]], tab[ONE_C + n]
        s = jnp.where(visible(tab, slots, chunk), scores(slots, chunk), NEG)
        accumulate(slots, chunk, s, jnp.max(s, axis=0, keepdims=True), 2 * count + n, ones_m, n)
        return 0
    lax.fori_loop(0, tab[ONES], one, 0)


def bwd_kernel(tab, qd, gt, vs, kt, ls_ref, de_ref, kept, pairs_m, ones_m, dq_ref, dk_ref, dv_ref, dks, dvs, dqt):
    pairs, ones = tab[PAIRS], tab[ONES]
    dks[...] = jnp.zeros_like(dks)
    dvs[...] = jnp.zeros_like(dvs)
    dqt[...] = jnp.zeros_like(dqt)

    def step(slots, chunk, block, m):
        at = rows_of(chunk)
        part = jnp.exp2(m - side(ls_ref, slots, 1))
        gs = (side(gt, slots, 1).astype(jnp.float32) * part).astype(jnp.bfloat16)
        p = side(kept, [block + i for i in range(len(slots))], 1)
        dp = dot(vs[at, :], gs, 1, 0)
        ds = p * (dp - side(de_ref, slots, 1) * part).astype(jnp.bfloat16)
        dvs[at, :] += dot(p, gs, 1, 1)
        dks[at, :] += dot(ds, side(qd, slots, 0), 1, 0)
        dq = dot(kt[:, at], ds, 1, 0)
        for i, t in enumerate(slots):
            dqt[t] += dq[:, i * COLS:(i + 1) * COLS]

    def pair(n, _):
        step([tab[PAIR_A + n], tab[PAIR_B + n]], tab[PAIR_C + n], 2 * n, pairs_m[n])
        return 0
    lax.fori_loop(0, pairs, pair, 0)

    def one(n, _):
        step([tab[ONE_T + n]], tab[ONE_C + n], 2 * pairs + n, ones_m[n])
        return 0
    lax.fori_loop(0, ones, one, 0)

    for t in range(NQ):
        dq_ref[t] = (dqt[t].T * SCALE).astype(jnp.bfloat16)

    def scatter(r, _):
        src = pl.ds(pl.multiple_of(r * SPAN, SPAN), SPAN)
        dst = pl.ds(pl.multiple_of(tab[ORDER + r] * SPAN, SPAN), SPAN)
        dk_ref[dst, :] = (dks[src, :] * SCALE).astype(jnp.bfloat16)
        dv_ref[dst, :] = dvs[src, :].astype(jnp.bfloat16)
        return 0
    lax.fori_loop(0, NK, scatter, 0)


VM = pl.BlockSpec(memory_space=pltpu.VMEM)
SM = pl.BlockSpec(memory_space=pltpu.SMEM)
ANY = pl.BlockSpec(memory_space=pl.ANY)
LIM = 18 * 1024 * 1024
LOW = 16 * 1024 * 1024
KEYS = NK * SPAN


def bf16(*shape):
    return jax.ShapeDtypeStruct(shape, jnp.bfloat16)


def single(*shape):
    return jax.ShapeDtypeStruct(shape, jnp.float32)


def vm(*shape):
    return pltpu.VMEM(shape, jnp.bfloat16)


def vm32(*shape):
    return pltpu.VMEM(shape, jnp.float32)


def cost(flops, nbytes):
    return pl.CostEstimate(flops=flops, bytes_accessed=nbytes, transcendentals=0)


def fwd(where, keys, q, k, v):
    return pl.pallas_call(
        functools.partial(fwd_kernel, where),
        out_shape=(single(NQ, 128, COLS), single(NQ, 1, COLS), single(NQ, 1, COLS), bf16(KEYS, 128), bf16(KEYS, 128),
                   jax.ShapeDtypeStruct((TABLE,), jnp.int32), vm(BLOCKS, CH, COLS), single(24, 1, 2 * COLS), single(24, 1, COLS)),
        in_specs=[SM, VM, VM, VM], out_specs=(VM,) * 5 + (SM, VM, VM, VM),
        scratch_shapes=[vm(128, KEYS), vm32(CH, 2 * COLS), vm32(CH, 2 * COLS), vm32(1, 2 * COLS), vm32(1, 2 * COLS),
                        pltpu.SMEM((NQ,), jnp.int32)],
        compiler_params=pltpu.CompilerParams(vmem_limit_bytes=LIM), cost_estimate=cost(10**10, 8 * 10**6), name="fwd_k",
    )(keys, q, k, v)


def bwd(tab, q, g, v, kt, ls, de, kept, pairs_m, ones_m):
    return pl.pallas_call(
        bwd_kernel,
        out_shape=(bf16(NQ, COLS, 128), bf16(KEYS, 128), bf16(KEYS, 128)),
        in_specs=[SM] + [VM] * 9, out_specs=(VM, VM, VM),
        scratch_shapes=[vm32(KEYS, 128), vm32(KEYS, 128), vm32(NQ, 128, COLS)],
        compiler_params=pltpu.CompilerParams(vmem_limit_bytes=LIM), cost_estimate=cost(2 * 10**10, 8 * 10**6), name="bwd_k",
    )(tab, q, g, v, kt, ls, de, kept, pairs_m, ones_m)

MESH = pl.DeviceIdType.MESH
LO, HI = pl.ds(0, SPAN), pl.ds(SPAN, SPAN)
ALL = pl.ds(0, 2 * SPAN)
OFFSETS = (0, -1, 1, 2)


def coords():
    me = lax.axis_index("ctx")
    return me // 16, (me // 4) % 4, (me // 2) % 2, me % 2


def device(y, x, z, c):
    return {"ctx": ((y + 4) % 4 * 4 + (x + 4) % 4) * 4 + z * 2 + c}


def head_at(d):
    return {"head": (lax.axis_index("head") + d + 4) % 4}


def greet(heads):
    y, x, z, c = coords()
    barrier = pltpu.get_barrier_semaphore()
    near = [(y, x, 1 - z, c), (y, x, z, 1 - c)]
    for d in (1, -1, 2):
        near += [(y, x + d, z, c), (y + d, x, z, c)]
    ids = [device(*n) for n in near]
    if heads:
        ids += [head_at(1), head_at(-1)]
    for n in ids:
        pl.semaphore_signal(barrier, inc=1, device_id=n, device_id_type=MESH)
    pl.semaphore_wait(barrier, len(ids))


def remote(src, dst, send, recv, n, to):
    return pltpu.make_async_remote_copy(
        src_ref=src, dst_ref=dst, send_sem=send.at[n], recv_sem=recv.at[n], device_id=device(*to), device_id_type=MESH
    )


def group_share(own, out, pick, send, recv, first):
    y, x, z, c = coords()
    core, chip = (y, x, z, 1 - c), (y, x, 1 - z, c)
    mine, far, beside, across = z * 2 + c, (1 - z) * 2 + c, z * 2 + 1 - c, (1 - z) * 2 + 1 - c

    def cp(src, block, n, to):
        return remote(pick(src.at[block]), pick(out.at[block]), send, recv, first + n, to)

    sends = cp(own, mine, 0, chip), cp(own, mine, 1, core), cp(out, far, 2, core)
    recvs = cp(out, far, 0, chip), cp(out, beside, 1, core), cp(out, across, 2, core)
    return sends, recvs


def plane_gather(out, send, recv, x_first):
    y, x, z, c = coords()

    def place(da, db):
        dy, dx = (db, da) if x_first else (da, db)
        return (y + dy, x + dx, z, c)

    def block(da, db):
        yy, xx, _, _ = place(da, db)
        return (yy + 4) % 4, (xx + 4) % 4

    def cp(n, sa, sb, rows, to):
        yy, xx = block(sa, sb)
        ref = out.at[yy, xx, rows]
        return remote(ref, ref, send, recv, n, place(*to))

    sends, recvs = {}, {}
    for i, d in enumerate((1, -1, 2)):
        sends["a", d] = cp(i, 0, 0, ALL, (d, 0))
        recvs["a", d] = cp(i, -d, 0, ALL, (d, 0))
    for d, half in ((1, LO), (-1, HI)):
        i = (1 - d) // 2
        for k, e in enumerate(OFFSETS):
            sends["b", e, d] = cp(4 + 4 * k + i, e, 0, ALL, (0, d))
            recvs["b", e, d] = cp(4 + 4 * k + i, e, -d, ALL, (0, d))
            sends["bb", e, d] = cp(6 + 4 * k + i, e, -d, half, (0, d))
            recvs["bb", e, d] = cp(6 + 4 * k + i, e, -2 * d, half, (0, d))
    return sends, recvs


def key_order(place, part):
    slot = lax.broadcasted_iota(jnp.int32, (128, 128), 0)
    lane = lax.broadcasted_iota(jnp.int32, (128, 128), 1)
    across = jnp.broadcast_to(f32(place), (128, 128))
    down = across.T
    position = f32(lane)
    own = jnp.where((slot % 8) // 2 == part, 1.0, 0.0)
    name = f32(slot // 8 * 2 + slot % 2)
    before = jnp.sum(jnp.where(down < position, own, 0.0), axis=0, keepdims=True)
    held = jnp.sum(jnp.where(down == position, own * (name + 1.0), 0.0), axis=0, keepdims=True) - 1.0
    own_lane = jnp.where((lane % 8) // 2 == part, 1.0, 0.0)
    rank = jnp.sum(jnp.where(across < down, own_lane, 0.0), axis=1, keepdims=True)
    order = jnp.sum(jnp.where(rank == position, own * name, 0.0), axis=0, keepdims=True)
    return jnp.concatenate([before, held, order, f32(place)], axis=0).astype(jnp.int32)


def order_kernel(place, keys):
    _, _, z, c = coords()
    keys[...] = key_order(place[...], z * 2 + c)


def share_kernel(q_ref, k_ref, v_ref, c_ref, qa, ka, va, up, down, here, qs, qr, ks, kr, vs, vr, cs, cr):
    y, x, z, c = coords()
    mine = z * 2 + c
    lo, hi = c_ref.at[LO], c_ref.at[HI]
    loads = [pltpu.make_async_copy(k_ref, ka.at[y, x], here.at[0]), pltpu.make_async_copy(v_ref, va.at[y, x], here.at[1])]
    for s in range(2):
        for h in range(4):
            loads.append(pltpu.make_async_copy(
                q_ref.at[s * SPAN:(s + 1) * SPAN, h * 128:(h + 1) * 128], qa.at[mine, s, h * SPAN:(h + 1) * SPAN],
                here.at[2 + s * 4 + h]))
    loads += [pltpu.make_async_copy(hi, up.at[0], here.at[10]), pltpu.make_async_copy(lo, down.at[0], here.at[11])]
    for load in loads:
        load.start()
    greet(True)
    to_up = pltpu.make_async_remote_copy(
        src_ref=lo, dst_ref=up.at[1], send_sem=cs.at[0], recv_sem=cr.at[0], device_id=head_at(1), device_id_type=MESH)
    to_down = pltpu.make_async_remote_copy(
        src_ref=hi, dst_ref=down.at[1], send_sem=cs.at[1], recv_sem=cr.at[1], device_id=head_at(-1), device_id_type=MESH)
    planes = [plane_gather(ka, ks, kr, True), plane_gather(va, vs, vr, False)]
    q_send, q_recv = group_share(qa, qa, lambda ref: ref, qs, qr, 0)
    for load in loads[:2]:
        load.wait()
    for s, _ in planes:
        for d in (1, -1, 2):
            s["a", d].start()
    for s, _ in planes:
        for d in (1, -1):
            s["b", 0, d].start()
    for load in loads[2:]:
        load.wait()
    q_send[0].start()
    q_send[1].start()
    to_up.start()
    to_down.start()
    for d, e in ((1, -1), (-1, 1)):
        for s, r in planes:
            r["a", d].wait_recv()
            s["b", e, 1].start()
            s["b", e, -1].start()
    for d in (1, -1):
        for s, r in planes:
            r["b", 0, d].wait_recv()
            s["bb", 0, d].start()
    for s, r in planes:
        r["a", 2].wait_recv()
        s["b", 2, 1].start()
        s["b", 2, -1].start()
    q_recv[0].wait_recv()
    q_send[2].start()
    for e in (-1, 1, 2):
        for d in (1, -1):
            for s, r in planes:
                r["b", e, d].wait_recv()
                s["bb", e, d].start()
    for e in OFFSETS:
        for d in (1, -1):
            for s, r in planes:
                r["bb", e, d].wait_recv()
    q_recv[1].wait_recv()
    q_recv[2].wait_recv()
    for s, _ in planes:
        for copy in s.values():
            copy.wait_send()
    for copy in q_send:
        copy.wait_send()
    to_up.wait()
    to_down.wait()


def stats_kernel(up, down, from_low, from_high, w_ref, o_ref, m_ref, l_ref, k_ref, _, gt, ls_ref, de_ref, kt, ga, part, levels, deltas, gs, gr, ss, sr):
    y, x, z, c = coords()
    mine = z * 2 + c
    head = lax.axis_index("head")
    greet_group()

    others = [(z, 1 - c), (1 - z, c), (1 - z, 1 - c)]

    def spread(ref, first):
        sent = [remote(ref.at[mine], ref.at[mine], ss, sr, first + n, (y, x, zz, cc)) for n, (zz, cc) in enumerate(others)]
        came = [remote(ref.at[zz * 2 + cc], ref.at[zz * 2 + cc], ss, sr, first + n, (y, x, zz, cc))
                for n, (zz, cc) in enumerate(others)]
        return sent, came

    for t in range(NQ):
        levels[mine, t:t + 1, :] = m_ref[t]
        levels[mine, NQ + t:NQ + t + 1, :] = l_ref[t]
    levels_sent, levels_came = spread(levels, 0)
    for copy in levels_sent:
        copy.start()

    def term(block, d):
        cols = pl.ds(pl.multiple_of((head + d + 4) % 4 * 1024, 1024), 1024)
        return dot(block, w_ref[:, cols], 1, 1)

    def whole(low, high):
        return jnp.concatenate([low, high], axis=0)

    grad = term(whole(down[0], up[0]), 0) + term(whole(up[1], from_low[0]), -1)
    grad += term(whole(from_high[0], down[1]), 1) + term(whole(from_low[1], from_high[1]), 2)
    grad = grad.astype(jnp.bfloat16)
    shares = [group_share(ga, ga, lambda ref, s=s: ref.at[s], gs, gr, 3 * s) for s in range(2)]
    for s in range(2):
        ga[mine, s] = jnp.concatenate([grad[s * SPAN:(s + 1) * SPAN, h * 128:(h + 1) * 128] for h in range(4)], axis=0)
        shares[s][0][0].start()
        shares[s][0][1].start()

    def inner(block, s):
        t = block * 2 + s
        down = ga[block, s].T
        gt[t] = down
        part[t] = jnp.sum(f32(down) * o_ref[t], axis=0, keepdims=True)

    for i in range(NK * SPAN // 512):
        kt[:, i * 512:(i + 1) * 512] = k_ref[i * 512:(i + 1) * 512, :].T
    for s in range(2):
        inner(mine, s)
    for s in range(2):
        shares[s][1][1].wait_recv()
        inner(z * 2 + 1 - c, s)
    for s in range(2):
        shares[s][1][0].wait_recv()
        shares[s][0][2].start()
        inner((1 - z) * 2 + c, s)
    for s in range(2):
        shares[s][1][2].wait_recv()
        inner((1 - z) * 2 + 1 - c, s)
    for t in range(NQ):
        deltas[mine, t:t + 1, :] = part[t]
    deltas_sent, deltas_came = spread(deltas, 3)
    for copy in deltas_sent:
        copy.start()
    for copy in levels_came:
        copy.wait_recv()
    tops = [levels[j, 0:NQ, :] for j in range(4)]
    top = jnp.maximum(jnp.maximum(tops[0], tops[1]), jnp.maximum(tops[2], tops[3]))
    scales = [jnp.exp2(m - top) for m in tops]
    total = sum(scales[j] * levels[j, NQ:2 * NQ, :] for j in range(4))
    level = top + jnp.log(total) * math.log2(math.e)
    for copy in deltas_came:
        copy.wait_recv()
    delta = sum(scales[j] * deltas[j] for j in range(4)) / total
    for t in range(NQ):
        ls_ref[t] = level[t:t + 1, :]
        de_ref[t] = delta[t:t + 1, :]
    for copy in levels_sent + deltas_sent:
        copy.wait_send()
    for s in range(2):
        for copy in shares[s][0]:
            copy.wait_send()


def greet_group():
    y, x, z, c = coords()
    barrier = pltpu.get_barrier_semaphore()
    near = [(y, x, 1 - z, c), (y, x, z, 1 - c), (y, x, 1 - z, 1 - c)]
    for n in near:
        pl.semaphore_signal(barrier, inc=1, device_id=device(*n), device_id_type=MESH)
    pl.semaphore_wait(barrier, len(near))


def f32(a):
    return a.astype(jnp.float32)


def plane_reduce(src, out, x_first, far1, near1, stage1, acc, near2, send, recv):
    y, x, z, c = coords()
    first = x if x_first else y
    second = y if x_first else x

    def to1(d):
        return (y, x + d, z, c) if x_first else (y + d, x, z, c)

    def to2(d):
        return (y + d, x, z, c) if x_first else (y, x + d, z, c)

    def line(d, rows):
        i = (first + d + 4) % 4
        return src.at[:, i, rows] if x_first else src.at[i, :, rows]

    def load(d):
        i = (first + d + 4) % 4
        return src[:, i] if x_first else src[i]

    def cp(s, t, n, to):
        return remote(s, t, send, recv, n, to)

    halves = ((0, 1, LO, HI, slice(0, SPAN), slice(SPAN, 2 * SPAN)), (1, -1, HI, LO, slice(SPAN, 2 * SPAN), slice(0, SPAN)))
    sends = []

    def go(copy):
        copy.start()
        sends.append(copy)

    def step0():
        for i, d, half, other, _, _ in halves:
            go(cp(line(2, half), far1.at[i], i, to1(d)))
        for i, d, half, other, _, _ in halves:
            go(cp(line(d, other), near1.at[i, :, other], 2 + i, to1(d)))

    def step1():
        for i, d, half, other, hs, _ in halves:
            cp(far1.at[i], far1.at[i], i, to1(d)).wait_recv()
            stage1[i] = (f32(load(d)[:, hs]) + f32(far1[i])).astype(jnp.bfloat16)
            go(cp(stage1.at[i], near1.at[i, :, half], 4 + i, to1(d)))

    def step2():
        for i, d, half, other, _, _ in halves:
            cp(near1.at[i, :, other], near1.at[i, :, other], 2 + i, to1(d)).wait_recv()
            cp(near1.at[i, :, half], near1.at[i, :, half], 4 + i, to1(d)).wait_recv()
        acc[...] = (f32(load(0)) + f32(near1[0]) + f32(near1[1])).astype(jnp.bfloat16)
        for i, d in enumerate((2, 1, -1)):
            go(cp(acc.at[(second + d + 4) % 4], near2.at[i], 6 + i, to2(d)))

    def step3():
        for i, d in enumerate((2, 1, -1)):
            cp(near2.at[i], near2.at[i], 6 + i, to2(d)).wait_recv()
        out[...] = (f32(acc[second]) + f32(near2[0]) + f32(near2[1]) + f32(near2[2])).astype(jnp.bfloat16)

    def finish():
        for copy in sends:
            copy.wait_send()

    return [step0, step1, step2, step3, finish]


def reduce_kernel(dq_ref, dk_ref, dv_ref, qo, ko, vo, q1, q2, qstage, qs, qr, *rest):
    y, x, z, c = coords()
    greet(False)
    core, chip = (y, x, z, 1 - c), (y, x, 1 - z, c)
    k_steps = plane_reduce(dk_ref, ko, False, *rest[:7])
    v_steps = plane_reduce(dv_ref, vo, True, *rest[7:])
    other = remote(dq_ref.at[(1 - z) * 2 + 1 - c], q1.at[1 - z], qs, qr, 0, core)
    same = remote(dq_ref.at[z * 2 + 1 - c], q1.at[z], qs, qr, 1, core)
    across = remote(qstage, q2, qs, qr, 2, chip)
    k_steps[0]()
    v_steps[0]()
    other.start()
    same.start()
    other.wait_recv()
    qstage[...] = (f32(dq_ref[(1 - z) * 2 + c]) + f32(q1[1 - z])).astype(jnp.bfloat16)
    across.start()
    for k_step, v_step in list(zip(k_steps, v_steps))[1:4]:
        k_step()
        v_step()
    same.wait_recv()
    across.wait_recv()
    total = (f32(dq_ref[z * 2 + c]) + f32(q1[z]) + f32(q2[...])).astype(jnp.bfloat16)
    for s in range(2):
        for h in range(4):
            qo[s * SPAN:(s + 1) * SPAN, h * 128:(h + 1) * 128] = total[s, h * SPAN:(h + 1) * SPAN]
    k_steps[4]()
    v_steps[4]()
    for copy in (other, same, across):
        copy.wait_send()


def sems(n):
    return [pltpu.SemaphoreType.DMA((n,)), pltpu.SemaphoreType.DMA((n,))]


def remote_params(n, limit=LOW):
    return pltpu.CompilerParams(collective_id=n, has_side_effects=True, vmem_limit_bytes=limit)


def key_table(place):
    return pl.pallas_call(
        order_kernel, out_shape=jax.ShapeDtypeStruct((4, 128), jnp.int32), in_specs=[VM], out_specs=VM,
        compiler_params=pltpu.CompilerParams(vmem_limit_bytes=LIM), cost_estimate=cost(10**10, 10**6), name="order_k",
    )(place)


def finish_kernel(*refs):
    sems = refs[-1]
    copies = [pltpu.make_async_copy(refs[i], refs[3 + i], sems.at[i]) for i in range(3)]
    for copy in copies:
        copy.start()
    for copy in copies:
        copy.wait()


def finish(*args):
    return pl.pallas_call(
        finish_kernel, out_shape=tuple(bf16(*a.shape) for a in args), in_specs=[VM] * 3, out_specs=(ANY,) * 3,
        scratch_shapes=[pltpu.SemaphoreType.DMA((3,))],
        compiler_params=pltpu.CompilerParams(vmem_limit_bytes=LIM), cost_estimate=cost(10**6, 10**6), name="finish_k",
    )(*args)


def share(*args):
    return pl.pallas_call(
        share_kernel,
        out_shape=(bf16(4, 2, COLS, 128), bf16(4, 4, 192, 128), bf16(4, 4, 192, 128), bf16(2, SPAN, 1024), bf16(2, SPAN, 1024)),
        in_specs=[ANY] * 4, out_specs=(VM,) * 5,
        scratch_shapes=[pltpu.SemaphoreType.DMA((12,))] + sems(3) + sems(20) + sems(20) + sems(2),
        compiler_params=remote_params(0), cost_estimate=cost(10**10, 8 * 10**6), name="share_k",
    )(*[pltpu.with_memory_space_constraint(a, pltpu.HBM) for a in args])


def stats(*args):
    return pl.pallas_call(
        stats_kernel,
        out_shape=(bf16(NQ, 128, COLS), single(NQ, 1, COLS), single(NQ, 1, COLS), bf16(128, KEYS)),
        in_specs=[VM] * 10, out_specs=(VM,) * 4,
        scratch_shapes=[vm(4, 2, COLS, 128), vm32(NQ, 1, COLS), vm32(4, 2 * NQ, COLS), vm32(4, NQ, COLS)] + sems(6) + sems(6),
        compiler_params=remote_params(1), cost_estimate=cost(10**9, 8 * 10**6), name="stats_k",
    )(*args)


def reduce(dq, dk, dv):
    plane = [vm(2, 4, SPAN, 128), vm(2, 4, 2 * SPAN, 128), vm(2, 4, SPAN, 128), vm(4, 2 * SPAN, 128),
             vm(3, 2 * SPAN, 128)] + sems(9)
    return pl.pallas_call(
        reduce_kernel,
        out_shape=(bf16(192, 512), bf16(192, 128), bf16(192, 128)),
        in_specs=[VM] * 3, out_specs=(VM,) * 3,
        scratch_shapes=[vm(2, 2, COLS, 128), vm(2, COLS, 128), vm(2, COLS, 128)] + sems(3) + plane + plane,
        compiler_params=remote_params(2), name="reduce_k",
    )(dq, dk, dv)


def where():
    y, x, z, c = coords()
    return y * 4 + x, z * 2 + c


def local(placement, queries, keys, values, cotangent, out_weight):
    order = key_table(placement.reshape(1, 128))
    q_all, k_all, v_all, up, down = share(queries, keys, values, cotangent)
    from_low = lax.ppermute(up, "head", [(i, (i + 1) % 4) for i in range(4)])
    from_high = lax.ppermute(down, "head", [(i, (i + 3) % 4) for i in range(4)])
    q_all = q_all.reshape(NQ, COLS, 128)
    o, m, l, ks, vs, tab, kept, pairs_m, ones_m = fwd(where, order, q_all, k_all.reshape(KEYS, 128), v_all.reshape(KEYS, 128))
    kept = pltpu.with_memory_space_constraint(kept, pltpu.VMEM)
    gt, ls, de, kt = stats(up, down, from_low, from_high, out_weight, o, m, l, ks, kept)
    dq, dk, dv = bwd(tab, q_all, gt, vs, kt, ls, de, kept, pairs_m, ones_m)
    return finish(*reduce(dq.reshape(4, 2, COLS, 128), dk.reshape(4, 4, 192, 128), dv.reshape(4, 4, 192, 128)))


def solution(mesh):
    in_specs = (P(), P("ctx", "head"), P("ctx", "head"), P("ctx", "head"), P("ctx", "head"), P("head", None))
    out_specs = (P("ctx", "head"), P("ctx", "head"), P("ctx", "head"))
    return jax.shard_map(local, mesh=mesh, in_specs=in_specs, out_specs=out_specs, check_vma=False)
```

```python
import functools
import math

import jax
import jax.numpy as jnp
from jax import lax
from jax.experimental import pallas as pl
from jax.experimental.pallas import tpu as pltpu
from jax.sharding import PartitionSpec as P

SPAN = 96
SCALE = 1.0 / math.sqrt(128.0)
C2 = math.log2(math.e) * SCALE
NEG = -1e30
NQ = 8
NK = 32
CH = 512
COLS = 4 * SPAN
PAIR_A, PAIR_B, PAIR_C, PAIR_F, ONE_T, ONE_C, FULL, OWN, ORDER, PAIRS, ONES = 0, 32, 64, 96, 128, 160, 192, 200, 208, 248, 249
TABLE = 256


def dot(a, b, ca, cb):
    return lax.dot_general(a, b, (((ca,), (cb,)), ((), ())), preferred_element_type=jnp.float32)


def int_of(flag):
    return jnp.where(flag, 1, 0).astype(jnp.int32)


def make_table(keys, plane, tab, rank):
    for r in range(NK):
        tab[ORDER + r] = keys[2, r]
    spans = [keys[3, plane * 8 + t] for t in range(NQ)]
    for t in range(NQ):
        tab[FULL + t] = keys[0, spans[t]] * SPAN
        tab[OWN + t] = int_of(keys[1, spans[t]] >= 0)
        rank[sum(int_of(spans[u] < spans[t]) for u in range(NQ) if u != t)] = t

    def pair(i, counts):
        pairs, ones = counts
        a, b = rank[2 * i], rank[2 * i + 1]
        full = tab[FULL + a]
        chunks_a = (full + tab[OWN + a] * SPAN + CH - 1) // CH
        chunks_b = (tab[FULL + b] + tab[OWN + b] * SPAN + CH - 1) // CH

        def put_pair(c, _):
            tab[PAIR_A + pairs + c] = a
            tab[PAIR_B + pairs + c] = b
            tab[PAIR_C + pairs + c] = c
            tab[PAIR_F + pairs + c] = int_of((c + 1) * CH > full)
            return 0
        lax.fori_loop(0, chunks_a, put_pair, 0)

        def put_one(c, _):
            tab[ONE_T + ones + c - chunks_a] = b
            tab[ONE_C + ones + c - chunks_a] = c
            return 0
        lax.fori_loop(chunks_a, chunks_b, put_one, 0)
        return pairs + chunks_a, ones + jnp.maximum(chunks_b - chunks_a, 0)
    pairs, ones = lax.fori_loop(0, NQ // 2, pair, (jnp.int32(0), jnp.int32(0)))
    tab[PAIRS] = pairs
    tab[ONES] = ones
    tab[PAIR_A + pairs] = 0
    tab[PAIR_B + pairs] = 1
    tab[PAIR_C + pairs] = 0
    tab[PAIR_F + pairs] = 0


def limits(tab, slots):
    col = lax.broadcasted_iota(jnp.int32, (1, COLS), 1)
    sub = 32 * ((col % SPAN) // 32 + 1)
    return jnp.concatenate([tab[FULL + t] + tab[OWN + t] * sub for t in slots], axis=1)


def visible(tab, slots, chunk):
    idx = lax.broadcasted_iota(jnp.int32, (CH, COLS * len(slots)), 0)
    return idx < limits(tab, slots) - chunk * CH


def side(ref, slots, axis):
    return jnp.concatenate([ref[t] for t in slots], axis=axis) if len(slots) > 1 else ref[slots[0]]


def rows_of(chunk):
    return pl.ds(pl.multiple_of(chunk * CH, CH), CH)


def fwd_kernel(where, keys, qd, k_ref, v_ref, o_ref, m_ref, l_ref, ks, vs, tab, kept, pairs_m, ones_m,
               vt, s0, s1, x0, x1, rank):
    plane, _ = where()
    make_table(keys, plane, tab, rank)

    def sort(r, _):
        src = pl.ds(pl.multiple_of(tab[ORDER + r] * SPAN, SPAN), SPAN)
        dst = pl.ds(pl.multiple_of(r * SPAN, SPAN), SPAN)
        ks[dst, :] = k_ref[src, :]
        vs[dst, :] = v_ref[src, :]
        return 0
    lax.fori_loop(0, NK, sort, 0)
    for i in range(NK * SPAN // 512):
        vt[:, i * 512:(i + 1) * 512] = vs[i * 512:(i + 1) * 512, :].T

    def clear(t, _):
        first = (tab[FULL + t] + tab[OWN + t] * SPAN + CH - 1) // CH

        def unseen(chunk, _):
            kept[t, rows_of(chunk), :] = jnp.zeros((CH, COLS), jnp.bfloat16)
            return 0
        return lax.fori_loop(first, KEYS // CH, unseen, 0)
    lax.fori_loop(0, NQ, clear, 0)
    o_ref[...] = jnp.zeros_like(o_ref)
    m_ref[...] = jnp.full(m_ref.shape, NEG, jnp.float32)
    l_ref[...] = jnp.zeros_like(l_ref)

    def scores(slots, chunk):
        return dot(ks[rows_of(chunk), :], side(qd, slots, 0), 1, 1) * C2

    def accumulate(slots, chunk, s, top, kept_m, n):
        m = side(m_ref, slots, 1)
        m2 = jnp.maximum(m, top)
        a = jnp.exp2(m - m2)
        p = jnp.exp2(s - m2)
        l2 = side(l_ref, slots, 1) * a + jnp.sum(p, axis=0, keepdims=True)
        pb = p.astype(jnp.bfloat16)
        kept_m[n] = m2
        o = dot(vt[:, rows_of(chunk)], pb, 1, 0)
        for i, t in enumerate(slots):
            at = slice(i * COLS, (i + 1) * COLS)
            kept[t, rows_of(chunk), :] = pb[:, at]
            m_ref[t] = m2[:, at]
            l_ref[t] = l2[:, at]
            o_ref[t] = o_ref[t] * a[:, at] + o[:, at]

    def item(n):
        return [tab[PAIR_A + n], tab[PAIR_B + n]], tab[PAIR_C + n]

    def produce(n, buf, top):
        slots, chunk = item(n)
        s = scores(slots, chunk)
        buf[...] = s
        top[...] = jnp.max(s, axis=0, keepdims=True)

    def fix(n, buf, top):
        @pl.when(tab[PAIR_F + n] == 1)
        def _():
            slots, chunk = item(n)
            s = jnp.where(visible(tab, slots, chunk), buf[...], NEG)
            buf[...] = s
            top[...] = jnp.max(s, axis=0, keepdims=True)

    def consume(n, buf, top):
        slots, chunk = item(n)
        accumulate(slots, chunk, buf[...], top[...], pairs_m, n)

    count = tab[PAIRS]

    @pl.when(count > 0)
    def _():
        produce(0, s0, x0)
        fix(0, s0, x0)

    def two(i, _):
        produce(2 * i + 1, s1, x1)
        consume(2 * i, s0, x0)
        fix(2 * i + 1, s1, x1)
        produce(2 * i + 2, s0, x0)
        consume(2 * i + 1, s1, x1)
        fix(2 * i + 2, s0, x0)
        return 0
    lax.fori_loop(0, count // 2, two, 0)

    @pl.when(count % 2 == 1)
    def _():
        consume(count - 1, s0, x0)

    def one(n, _):
        slots, chunk = [tab[ONE_T + n]], tab[ONE_C + n]
        s = jnp.where(visible(tab, slots, chunk), scores(slots, chunk), NEG)
        accumulate(slots, chunk, s, jnp.max(s, axis=0, keepdims=True), ones_m, n)
        return 0
    lax.fori_loop(0, tab[ONES], one, 0)


def bwd_kernel(tab, qd, gt, vs, ls_ref, de_ref, kept, pairs_m, ones_m, ds_ref, dk_ref, dv_ref, dks, dvs):
    pairs, ones = tab[PAIRS], tab[ONES]
    dks[...] = jnp.zeros_like(dks)
    dvs[...] = jnp.zeros_like(dvs)

    def step(slots, chunk, m):
        at = rows_of(chunk)
        part = jnp.exp2(m - side(ls_ref, slots, 1))
        gs = (side(gt, slots, 1).astype(jnp.float32) * part).astype(jnp.bfloat16)
        p = jnp.concatenate([kept[t, at, :] for t in slots], axis=1)
        dp = dot(vs[at, :], gs, 1, 0)
        ds = p * (dp - side(de_ref, slots, 1) * part).astype(jnp.bfloat16)
        dvs[at, :] += dot(p, gs, 1, 1)
        dks[at, :] += dot(ds, side(qd, slots, 0), 1, 0)
        for i, t in enumerate(slots):
            ds_ref[t, at, :] = ds[:, i * COLS:(i + 1) * COLS]

    def pair(n, _):
        step([tab[PAIR_A + n], tab[PAIR_B + n]], tab[PAIR_C + n], pairs_m[n])
        return 0
    lax.fori_loop(0, pairs, pair, 0)

    def one(n, _):
        step([tab[ONE_T + n]], tab[ONE_C + n], ones_m[n])
        return 0
    lax.fori_loop(0, ones, one, 0)

    def scatter(r, _):
        src = pl.ds(pl.multiple_of(r * SPAN, SPAN), SPAN)
        dst = pl.ds(pl.multiple_of(tab[ORDER + r] * SPAN, SPAN), SPAN)
        dk_ref[dst, :] = (dks[src, :] * SCALE).astype(jnp.bfloat16)
        dv_ref[dst, :] = dvs[src, :].astype(jnp.bfloat16)
        return 0
    lax.fori_loop(0, NK, scatter, 0)


VM = pl.BlockSpec(memory_space=pltpu.VMEM)
SM = pl.BlockSpec(memory_space=pltpu.SMEM)
ANY = pl.BlockSpec(memory_space=pl.ANY)
LIM = 18 * 1024 * 1024
LOW = 16 * 1024 * 1024
KEYS = NK * SPAN


def bf16(*shape):
    return jax.ShapeDtypeStruct(shape, jnp.bfloat16)


def single(*shape):
    return jax.ShapeDtypeStruct(shape, jnp.float32)


def vm(*shape):
    return pltpu.VMEM(shape, jnp.bfloat16)


def vm32(*shape):
    return pltpu.VMEM(shape, jnp.float32)


def cost(flops, nbytes):
    return pl.CostEstimate(flops=flops, bytes_accessed=nbytes, transcendentals=0)


def fwd(where, keys, q, k, v):
    return pl.pallas_call(
        functools.partial(fwd_kernel, where),
        out_shape=(single(NQ, 128, COLS), single(NQ, 1, COLS), single(NQ, 1, COLS), bf16(KEYS, 128), bf16(KEYS, 128),
                   jax.ShapeDtypeStruct((TABLE,), jnp.int32), vm(NQ, KEYS, COLS), single(24, 1, 2 * COLS), single(24, 1, COLS)),
        in_specs=[SM, VM, VM, VM], out_specs=(VM,) * 5 + (SM, VM, VM, VM),
        scratch_shapes=[vm(128, KEYS), vm32(CH, 2 * COLS), vm32(CH, 2 * COLS), vm32(1, 2 * COLS), vm32(1, 2 * COLS),
                        pltpu.SMEM((NQ,), jnp.int32)],
        compiler_params=pltpu.CompilerParams(vmem_limit_bytes=LIM), cost_estimate=cost(10**10, 8 * 10**6), name="fwd_k",
    )(keys, q, k, v)


def bwd(tab, q, g, v, ls, de, kept, pairs_m, ones_m):
    return pl.pallas_call(
        bwd_kernel,
        out_shape=(vm(NQ, KEYS, COLS), bf16(KEYS, 128), bf16(KEYS, 128)),
        in_specs=[SM] + [VM] * 8, out_specs=(VM, VM, VM), input_output_aliases={6: 0},
        scratch_shapes=[vm32(KEYS, 128), vm32(KEYS, 128)],
        compiler_params=pltpu.CompilerParams(vmem_limit_bytes=LIM), cost_estimate=cost(2 * 10**10, 8 * 10**6), name="bwd_k",
    )(tab, q, g, v, ls, de, kept, pairs_m, ones_m)

MESH = pl.DeviceIdType.MESH
LO, HI = pl.ds(0, SPAN), pl.ds(SPAN, SPAN)
ALL = pl.ds(0, 2 * SPAN)
OFFSETS = (0, -1, 1, 2)


def coords():
    me = lax.axis_index("ctx")
    return me // 16, (me // 4) % 4, (me // 2) % 2, me % 2


def device(y, x, z, c):
    return {"ctx": ((y + 4) % 4 * 4 + (x + 4) % 4) * 4 + z * 2 + c}


def head_at(d):
    return {"head": (lax.axis_index("head") + d + 4) % 4}


def greet(heads):
    y, x, z, c = coords()
    barrier = pltpu.get_barrier_semaphore()
    near = [(y, x, 1 - z, c), (y, x, z, 1 - c)]
    for d in (1, -1, 2):
        near += [(y, x + d, z, c), (y + d, x, z, c)]
    ids = [device(*n) for n in near]
    if heads:
        ids += [head_at(1), head_at(-1)]
    for n in ids:
        pl.semaphore_signal(barrier, inc=1, device_id=n, device_id_type=MESH)
    pl.semaphore_wait(barrier, len(ids))


def remote(src, dst, send, recv, n, to):
    return pltpu.make_async_remote_copy(
        src_ref=src, dst_ref=dst, send_sem=send.at[n], recv_sem=recv.at[n], device_id=device(*to), device_id_type=MESH
    )


def group_share(own, out, pick, send, recv, first):
    y, x, z, c = coords()
    core, chip = (y, x, z, 1 - c), (y, x, 1 - z, c)
    mine, far, beside, across = z * 2 + c, (1 - z) * 2 + c, z * 2 + 1 - c, (1 - z) * 2 + 1 - c

    def cp(src, block, n, to):
        return remote(pick(src.at[block]), pick(out.at[block]), send, recv, first + n, to)

    sends = cp(own, mine, 0, chip), cp(own, mine, 1, core), cp(out, far, 2, core)
    recvs = cp(out, far, 0, chip), cp(out, beside, 1, core), cp(out, across, 2, core)
    return sends, recvs


def plane_gather(out, send, recv, x_first):
    y, x, z, c = coords()

    def place(da, db):
        dy, dx = (db, da) if x_first else (da, db)
        return (y + dy, x + dx, z, c)

    def block(da, db):
        yy, xx, _, _ = place(da, db)
        return (yy + 4) % 4, (xx + 4) % 4

    def cp(n, sa, sb, rows, to):
        yy, xx = block(sa, sb)
        ref = out.at[yy, xx, rows]
        return remote(ref, ref, send, recv, n, place(*to))

    sends, recvs = {}, {}
    for i, d in enumerate((1, -1, 2)):
        sends["a", d] = cp(i, 0, 0, ALL, (d, 0))
        recvs["a", d] = cp(i, -d, 0, ALL, (d, 0))
    for d, half in ((1, LO), (-1, HI)):
        i = (1 - d) // 2
        for k, e in enumerate(OFFSETS):
            sends["b", e, d] = cp(4 + 4 * k + i, e, 0, ALL, (0, d))
            recvs["b", e, d] = cp(4 + 4 * k + i, e, -d, ALL, (0, d))
            sends["bb", e, d] = cp(6 + 4 * k + i, e, -d, half, (0, d))
            recvs["bb", e, d] = cp(6 + 4 * k + i, e, -2 * d, half, (0, d))
    return sends, recvs


def key_order(place, part):
    slot = lax.broadcasted_iota(jnp.int32, (128, 128), 0)
    lane = lax.broadcasted_iota(jnp.int32, (128, 128), 1)
    across = jnp.broadcast_to(f32(place), (128, 128))
    down = across.T
    position = f32(lane)
    own = jnp.where((slot % 8) // 2 == part, 1.0, 0.0)
    name = f32(slot // 8 * 2 + slot % 2)
    before = jnp.sum(jnp.where(down < position, own, 0.0), axis=0, keepdims=True)
    held = jnp.sum(jnp.where(down == position, own * (name + 1.0), 0.0), axis=0, keepdims=True) - 1.0
    own_lane = jnp.where((lane % 8) // 2 == part, 1.0, 0.0)
    rank = jnp.sum(jnp.where(across < down, own_lane, 0.0), axis=1, keepdims=True)
    order = jnp.sum(jnp.where(rank == position, own * name, 0.0), axis=0, keepdims=True)
    return jnp.concatenate([before, held, order, f32(place)], axis=0).astype(jnp.int32)


def order_kernel(place, keys):
    _, _, z, c = coords()
    keys[...] = key_order(place[...], z * 2 + c)


def share_kernel(q_ref, k_ref, v_ref, c_ref, qa, ka, va, up, down, here, qs, qr, ks, kr, vs, vr, cs, cr):
    y, x, z, c = coords()
    mine = z * 2 + c
    lo, hi = c_ref.at[LO], c_ref.at[HI]
    loads = [pltpu.make_async_copy(k_ref, ka.at[y, x], here.at[0]), pltpu.make_async_copy(v_ref, va.at[y, x], here.at[1])]
    for s in range(2):
        for h in range(4):
            loads.append(pltpu.make_async_copy(
                q_ref.at[s * SPAN:(s + 1) * SPAN, h * 128:(h + 1) * 128], qa.at[mine, s, h * SPAN:(h + 1) * SPAN],
                here.at[2 + s * 4 + h]))
    loads += [pltpu.make_async_copy(hi, up.at[0], here.at[10]), pltpu.make_async_copy(lo, down.at[0], here.at[11])]
    for load in loads:
        load.start()
    greet(True)
    to_up = pltpu.make_async_remote_copy(
        src_ref=lo, dst_ref=up.at[1], send_sem=cs.at[0], recv_sem=cr.at[0], device_id=head_at(1), device_id_type=MESH)
    to_down = pltpu.make_async_remote_copy(
        src_ref=hi, dst_ref=down.at[1], send_sem=cs.at[1], recv_sem=cr.at[1], device_id=head_at(-1), device_id_type=MESH)
    planes = [plane_gather(ka, ks, kr, True), plane_gather(va, vs, vr, False)]
    q_send, q_recv = group_share(qa, qa, lambda ref: ref, qs, qr, 0)
    for load in loads[:2]:
        load.wait()
    for s, _ in planes:
        for d in (1, -1, 2):
            s["a", d].start()
    for s, _ in planes:
        for d in (1, -1):
            s["b", 0, d].start()
    for load in loads[2:]:
        load.wait()
    q_send[0].start()
    q_send[1].start()
    to_up.start()
    to_down.start()
    for d, e in ((1, -1), (-1, 1)):
        for s, r in planes:
            r["a", d].wait_recv()
            s["b", e, 1].start()
            s["b", e, -1].start()
    for d in (1, -1):
        for s, r in planes:
            r["b", 0, d].wait_recv()
            s["bb", 0, d].start()
    for s, r in planes:
        r["a", 2].wait_recv()
        s["b", 2, 1].start()
        s["b", 2, -1].start()
    q_recv[0].wait_recv()
    q_send[2].start()
    for e in (-1, 1, 2):
        for d in (1, -1):
            for s, r in planes:
                r["b", e, d].wait_recv()
                s["bb", e, d].start()
    for e in OFFSETS:
        for d in (1, -1):
            for s, r in planes:
                r["bb", e, d].wait_recv()
    q_recv[1].wait_recv()
    q_recv[2].wait_recv()
    for s, _ in planes:
        for copy in s.values():
            copy.wait_send()
    for copy in q_send:
        copy.wait_send()
    to_up.wait()
    to_down.wait()


def stats_kernel(up, down, from_low, from_high, w_ref, o_ref, m_ref, l_ref, k_ref, _, gt, ls_ref, de_ref, kt, ga, part, levels, deltas, gs, gr, ss, sr):
    y, x, z, c = coords()
    mine = z * 2 + c
    head = lax.axis_index("head")
    greet_group()

    others = [(z, 1 - c), (1 - z, c), (1 - z, 1 - c)]

    def spread(ref, first):
        sent = [remote(ref.at[mine], ref.at[mine], ss, sr, first + n, (y, x, zz, cc)) for n, (zz, cc) in enumerate(others)]
        came = [remote(ref.at[zz * 2 + cc], ref.at[zz * 2 + cc], ss, sr, first + n, (y, x, zz, cc))
                for n, (zz, cc) in enumerate(others)]
        return sent, came

    for t in range(NQ):
        levels[mine, t:t + 1, :] = m_ref[t]
        levels[mine, NQ + t:NQ + t + 1, :] = l_ref[t]
    levels_sent, levels_came = spread(levels, 0)
    for copy in levels_sent:
        copy.start()

    def term(block, d, rows):
        cols = pl.ds(pl.multiple_of((head + d + 4) % 4 * 1024, 1024), 1024)
        return dot(block, w_ref[rows, cols], 1, 1)

    def whole(low, high):
        return jnp.concatenate([low, high], axis=0)

    pieces = [(j, s) for j in range(2) for s in range(2)]

    def share_piece(n, j, s):
        return group_share(ga, ga, lambda ref: ref.at[s, pl.ds(j * 2 * SPAN, 2 * SPAN)], gs, gr, 3 * n)

    shares = [share_piece(n, j, s) for n, (j, s) in enumerate(pieces)]
    blocks = [(whole(down[0], up[0]), 0), (whole(up[1], from_low[0]), -1), (whole(from_high[0], down[1]), 1),
              (whole(from_low[1], from_high[1]), 2)]
    for j in range(2):
        rows = slice(j * 256, (j + 1) * 256)
        grad = sum(term(block, d, rows) for block, d in blocks).astype(jnp.bfloat16)
        for s in range(2):
            part_rows = grad[s * SPAN:(s + 1) * SPAN]
            ga[mine, s, j * 2 * SPAN:(j + 1) * 2 * SPAN] = jnp.concatenate([part_rows[:, :128], part_rows[:, 128:]], axis=0)
            shares[2 * j + s][0][0].start()
            shares[2 * j + s][0][1].start()

    def inner(block, s):
        t = block * 2 + s
        down = ga[block, s].T
        gt[t] = down
        part[t] = jnp.sum(f32(down) * o_ref[t], axis=0, keepdims=True)

    for i in range(NK * SPAN // 512):
        kt[:, i * 512:(i + 1) * 512] = k_ref[i * 512:(i + 1) * 512, :].T
    for s in range(2):
        inner(mine, s)
    for sends, recvs in shares:
        recvs[1].wait_recv()
    for s in range(2):
        inner(z * 2 + 1 - c, s)
    for sends, recvs in shares:
        recvs[0].wait_recv()
        sends[2].start()
    for s in range(2):
        inner((1 - z) * 2 + c, s)
    for sends, recvs in shares:
        recvs[2].wait_recv()
    for s in range(2):
        inner((1 - z) * 2 + 1 - c, s)
    for t in range(NQ):
        deltas[mine, t:t + 1, :] = part[t]
    deltas_sent, deltas_came = spread(deltas, 3)
    for copy in deltas_sent:
        copy.start()
    for copy in levels_came:
        copy.wait_recv()
    tops = [levels[j, 0:NQ, :] for j in range(4)]
    top = jnp.maximum(jnp.maximum(tops[0], tops[1]), jnp.maximum(tops[2], tops[3]))
    scales = [jnp.exp2(m - top) for m in tops]
    total = sum(scales[j] * levels[j, NQ:2 * NQ, :] for j in range(4))
    level = top + jnp.log(total) * math.log2(math.e)
    for copy in deltas_came:
        copy.wait_recv()
    delta = sum(scales[j] * deltas[j] for j in range(4)) / total
    for t in range(NQ):
        ls_ref[t] = level[t:t + 1, :]
        de_ref[t] = delta[t:t + 1, :]
    for copy in levels_sent + deltas_sent:
        copy.wait_send()
    for sends, _ in shares:
        for copy in sends:
            copy.wait_send()


def greet_group():
    y, x, z, c = coords()
    barrier = pltpu.get_barrier_semaphore()
    near = [(y, x, 1 - z, c), (y, x, z, 1 - c), (y, x, 1 - z, 1 - c)]
    for n in near:
        pl.semaphore_signal(barrier, inc=1, device_id=device(*n), device_id_type=MESH)
    pl.semaphore_wait(barrier, len(near))


def f32(a):
    return a.astype(jnp.float32)


ORDER2 = (2, 1, -1, 0)


def plane_reduce(src, out, x_first, far1, near1, stage1, acc, near2, send, recv):
    y, x, z, c = coords()
    first = x if x_first else y
    second = y if x_first else x

    def to1(d):
        return (y, x + d, z, c) if x_first else (y + d, x, z, c)

    def to2(d):
        return (y + d, x, z, c) if x_first else (y, x + d, z, c)

    def place(d, k):
        i, j = (first + d + 4) % 4, (second + ORDER2[k] + 4) % 4
        return (j, i) if x_first else (i, j)

    def cp(s, t, n, to):
        return remote(s, t, send, recv, n, to)

    halves = ((0, 1, LO, HI, slice(0, SPAN)), (1, -1, HI, LO, slice(SPAN, 2 * SPAN)))
    sends = []

    def go(copy):
        copy.start()
        sends.append(copy)

    def begin():
        for k in range(4):
            for i, d, half, _, _ in halves:
                a, b = place(2, k)
                go(cp(src.at[a, b, half], far1.at[i, k], 6 * k + i, to1(d)))
        for k in range(4):
            for i, d, _, other, _ in halves:
                a, b = place(d, k)
                go(cp(src.at[a, b, other], near1.at[i, k, other], 6 * k + 2 + i, to1(d)))

    def relay(k):
        for i, d, half, _, hs in halves:
            cp(far1.at[i, k], far1.at[i, k], 6 * k + i, to1(d)).wait_recv()
            a, b = place(d, k)
            stage1[i, k] = (f32(src[a, b, hs]) + f32(far1[i, k])).astype(jnp.bfloat16)
            go(cp(stage1.at[i, k], near1.at[i, k, half], 6 * k + 4 + i, to1(d)))

    def turn(k):
        for i, d, half, other, _ in halves:
            cp(near1.at[i, k, other], near1.at[i, k, other], 6 * k + 2 + i, to1(d)).wait_recv()
            cp(near1.at[i, k, half], near1.at[i, k, half], 6 * k + 4 + i, to1(d)).wait_recv()
        a, b = place(0, k)
        acc[k] = (f32(src[a, b]) + f32(near1[0, k]) + f32(near1[1, k])).astype(jnp.bfloat16)
        if k < 3:
            go(cp(acc.at[k], near2.at[k], 24 + k, to2(ORDER2[k])))

    def end():
        for k in range(3):
            cp(near2.at[k], near2.at[k], 24 + k, to2(ORDER2[k])).wait_recv()
        out[...] = (f32(acc[3]) + f32(near2[0]) + f32(near2[1]) + f32(near2[2])).astype(jnp.bfloat16)

    def finish():
        for copy in sends:
            copy.wait_send()

    return begin, relay, turn, end, finish


def reduce_kernel(ds_ref, kt, dk_ref, dv_ref, qo, ko, vo, dq, q1, q2, qstage, qs, qr, *rest):
    y, x, z, c = coords()
    greet(False)
    core, chip = (y, x, z, 1 - c), (y, x, 1 - z, c)
    sums = [plane_reduce(dk_ref, ko, False, *rest[:7]), plane_reduce(dv_ref, vo, True, *rest[7:])]
    other = remote(dq.at[(1 - z) * 2 + 1 - c], q1.at[1 - z], qs, qr, 0, core)
    same = remote(dq.at[z * 2 + 1 - c], q1.at[z], qs, qr, 1, core)
    across = remote(qstage, q2, qs, qr, 2, chip)

    def query_terms(block):
        def slot(s, _):
            dq[block, s] = (dot(kt[...], ds_ref[block * 2 + s], 1, 0).T * SCALE).astype(jnp.bfloat16)
            return 0
        lax.fori_loop(0, 2, slot, 0)

    for begin, _, _, _, _ in sums:
        begin()
    query_terms((1 - z) * 2 + 1 - c)
    other.start()
    query_terms((1 - z) * 2 + c)
    for k in range(4):
        for _, relay, _, _, _ in sums:
            relay(k)
    other.wait_recv()
    qstage[...] = (f32(dq[(1 - z) * 2 + c]) + f32(q1[1 - z])).astype(jnp.bfloat16)
    across.start()
    query_terms(z * 2 + 1 - c)
    same.start()
    query_terms(z * 2 + c)
    for k in range(4):
        for _, _, turn, _, _ in sums:
            turn(k)
    for _, _, _, end, _ in sums:
        end()
    same.wait_recv()
    across.wait_recv()
    total = (f32(dq[z * 2 + c]) + f32(q1[z]) + f32(q2[...])).astype(jnp.bfloat16)
    for s in range(2):
        for h in range(4):
            qo[s * SPAN:(s + 1) * SPAN, h * 128:(h + 1) * 128] = total[s, h * SPAN:(h + 1) * SPAN]
    for _, _, _, _, finish_all in sums:
        finish_all()
    for copy in (other, same, across):
        copy.wait_send()


def sems(n):
    return [pltpu.SemaphoreType.DMA((n,)), pltpu.SemaphoreType.DMA((n,))]


def remote_params(n, limit=LOW):
    return pltpu.CompilerParams(collective_id=n, has_side_effects=True, vmem_limit_bytes=limit)


def key_table(place):
    return pl.pallas_call(
        order_kernel, out_shape=jax.ShapeDtypeStruct((4, 128), jnp.int32), in_specs=[VM], out_specs=VM,
        compiler_params=pltpu.CompilerParams(vmem_limit_bytes=LIM), cost_estimate=cost(10**10, 10**6), name="order_k",
    )(place)


def finish_kernel(*refs):
    sems = refs[-1]
    copies = [pltpu.make_async_copy(refs[i], refs[3 + i], sems.at[i]) for i in range(3)]
    for copy in copies:
        copy.start()
    for copy in copies:
        copy.wait()


def finish(*args):
    return pl.pallas_call(
        finish_kernel, out_shape=tuple(bf16(*a.shape) for a in args), in_specs=[VM] * 3, out_specs=(ANY,) * 3,
        scratch_shapes=[pltpu.SemaphoreType.DMA((3,))],
        compiler_params=pltpu.CompilerParams(vmem_limit_bytes=LIM), cost_estimate=cost(10**6, 10**6), name="finish_k",
    )(*args)


def share(*args):
    return pl.pallas_call(
        share_kernel,
        out_shape=(bf16(4, 2, COLS, 128), bf16(4, 4, 192, 128), bf16(4, 4, 192, 128), bf16(2, SPAN, 1024), bf16(2, SPAN, 1024)),
        in_specs=[ANY] * 4, out_specs=(VM,) * 5,
        scratch_shapes=[pltpu.SemaphoreType.DMA((12,))] + sems(3) + sems(20) + sems(20) + sems(2),
        compiler_params=remote_params(0), cost_estimate=cost(10**10, 8 * 10**6), name="share_k",
    )(*[pltpu.with_memory_space_constraint(a, pltpu.HBM) for a in args])


def stats(*args):
    return pl.pallas_call(
        stats_kernel,
        out_shape=(bf16(NQ, 128, COLS), single(NQ, 1, COLS), single(NQ, 1, COLS), bf16(128, KEYS)),
        in_specs=[VM] * 10, out_specs=(VM,) * 4,
        scratch_shapes=[vm(4, 2, COLS, 128), vm32(NQ, 1, COLS), vm32(4, 2 * NQ, COLS), vm32(4, NQ, COLS)] + sems(12) + sems(6),
        compiler_params=remote_params(1), cost_estimate=cost(10**9, 8 * 10**6), name="stats_k",
    )(*args)


def reduce(ds, kt, dk, dv):
    plane = [vm(2, 4, SPAN, 128), vm(2, 4, 2 * SPAN, 128), vm(2, 4, SPAN, 128), vm(4, 2 * SPAN, 128),
             vm(3, 2 * SPAN, 128)] + sems(27)
    return pl.pallas_call(
        reduce_kernel,
        out_shape=(bf16(192, 512), bf16(192, 128), bf16(192, 128)),
        in_specs=[VM] * 4, out_specs=(VM,) * 3,
        scratch_shapes=[vm(4, 2, COLS, 128), vm(2, 2, COLS, 128), vm(2, COLS, 128), vm(2, COLS, 128)] + sems(3) + plane + plane,
        compiler_params=remote_params(2), name="reduce_k",
    )(ds, kt, dk, dv)


def where():
    y, x, z, c = coords()
    return y * 4 + x, z * 2 + c


def local(placement, queries, keys, values, cotangent, out_weight):
    order = key_table(placement.reshape(1, 128))
    q_all, k_all, v_all, up, down = share(queries, keys, values, cotangent)
    from_low = lax.ppermute(up, "head", [(i, (i + 1) % 4) for i in range(4)])
    from_high = lax.ppermute(down, "head", [(i, (i + 3) % 4) for i in range(4)])
    q_all = q_all.reshape(NQ, COLS, 128)
    o, m, l, ks, vs, tab, kept, pairs_m, ones_m = fwd(where, order, q_all, k_all.reshape(KEYS, 128), v_all.reshape(KEYS, 128))
    kept = pltpu.with_memory_space_constraint(kept, pltpu.VMEM)
    gt, ls, de, kt = stats(up, down, from_low, from_high, out_weight, o, m, l, ks, kept)
    ds, dk, dv = bwd(tab, q_all, gt, vs, ls, de, kept, pairs_m, ones_m)
    ds = pltpu.with_memory_space_constraint(ds, pltpu.VMEM)
    return finish(*reduce(ds, kt, dk.reshape(4, 4, 192, 128), dv.reshape(4, 4, 192, 128)))


def solution(mesh):
    in_specs = (P(), P("ctx", "head"), P("ctx", "head"), P("ctx", "head"), P("ctx", "head"), P("head", None))
    out_specs = (P("ctx", "head"), P("ctx", "head"), P("ctx", "head"))
    return jax.shard_map(local, mesh=mesh, in_specs=in_specs, out_specs=out_specs, check_vma=False)
```

```python
import functools
import math

import jax
import jax.numpy as jnp
from jax import lax
from jax.experimental import pallas as pl
from jax.experimental.pallas import tpu as pltpu
from jax.sharding import PartitionSpec as P

SPAN = 96
SCALE = 1.0 / math.sqrt(128.0)
C2 = math.log2(math.e) * SCALE
NEG = -1e30
NQ = 8
NK = 32
CH = 512
COLS = 4 * SPAN
PAIR_A, PAIR_B, PAIR_C, PAIR_F, ONE_T, ONE_C, FULL, OWN, ORDER, PAIRS, ONES = 0, 32, 64, 96, 128, 160, 192, 200, 208, 248, 249
TABLE = 256


def dot(a, b, ca, cb):
    return lax.dot_general(a, b, (((ca,), (cb,)), ((), ())), preferred_element_type=jnp.float32)


def int_of(flag):
    return jnp.where(flag, 1, 0).astype(jnp.int32)


def make_table(keys, plane, tab, rank):
    for r in range(NK):
        tab[ORDER + r] = keys[2, r]
    spans = [keys[3, plane * 8 + t] for t in range(NQ)]
    for t in range(NQ):
        tab[FULL + t] = keys[0, spans[t]] * SPAN
        tab[OWN + t] = int_of(keys[1, spans[t]] >= 0)
        rank[sum(int_of(spans[u] < spans[t]) for u in range(NQ) if u != t)] = t

    def pair(i, counts):
        pairs, ones = counts
        a, b = rank[2 * i], rank[2 * i + 1]
        full = tab[FULL + a]
        chunks_a = (full + tab[OWN + a] * SPAN + CH - 1) // CH
        chunks_b = (tab[FULL + b] + tab[OWN + b] * SPAN + CH - 1) // CH

        def put_pair(c, _):
            tab[PAIR_A + pairs + c] = a
            tab[PAIR_B + pairs + c] = b
            tab[PAIR_C + pairs + c] = c
            tab[PAIR_F + pairs + c] = int_of((c + 1) * CH > full)
            return 0
        lax.fori_loop(0, chunks_a, put_pair, 0)

        def put_one(c, _):
            tab[ONE_T + ones + c - chunks_a] = b
            tab[ONE_C + ones + c - chunks_a] = c
            return 0
        lax.fori_loop(chunks_a, chunks_b, put_one, 0)
        return pairs + chunks_a, ones + jnp.maximum(chunks_b - chunks_a, 0)
    pairs, ones = lax.fori_loop(0, NQ // 2, pair, (jnp.int32(0), jnp.int32(0)))
    tab[PAIRS] = pairs
    tab[ONES] = ones
    tab[PAIR_A + pairs] = 0
    tab[PAIR_B + pairs] = 1
    tab[PAIR_C + pairs] = 0
    tab[PAIR_F + pairs] = 0


def limits(tab, slots):
    col = lax.broadcasted_iota(jnp.int32, (1, COLS), 1)
    sub = 32 * ((col % SPAN) // 32 + 1)
    return jnp.concatenate([tab[FULL + t] + tab[OWN + t] * sub for t in slots], axis=1)


def visible(tab, slots, chunk):
    idx = lax.broadcasted_iota(jnp.int32, (CH, COLS * len(slots)), 0)
    return idx < limits(tab, slots) - chunk * CH


def side(ref, slots, axis):
    return jnp.concatenate([ref[t] for t in slots], axis=axis) if len(slots) > 1 else ref[slots[0]]


def rows_of(chunk):
    return pl.ds(pl.multiple_of(chunk * CH, CH), CH)


def fwd_kernel(where, keys, qd, k_ref, v_ref, o_ref, m_ref, l_ref, ks, vs, tab, kept, pairs_m, ones_m,
               vt, s0, s1, x0, x1, rank):
    plane, _ = where()
    make_table(keys, plane, tab, rank)

    def sort(r, _):
        src = pl.ds(pl.multiple_of(tab[ORDER + r] * SPAN, SPAN), SPAN)
        dst = pl.ds(pl.multiple_of(r * SPAN, SPAN), SPAN)
        ks[dst, :] = k_ref[src, :]
        vs[dst, :] = v_ref[src, :]
        return 0
    lax.fori_loop(0, NK, sort, 0)
    for i in range(NK * SPAN // 512):
        vt[:, i * 512:(i + 1) * 512] = vs[i * 512:(i + 1) * 512, :].T

    def clear(t, _):
        first = (tab[FULL + t] + tab[OWN + t] * SPAN + CH - 1) // CH

        def unseen(chunk, _):
            kept[t, rows_of(chunk), :] = jnp.zeros((CH, COLS), jnp.bfloat16)
            return 0
        return lax.fori_loop(first, KEYS // CH, unseen, 0)
    lax.fori_loop(0, NQ, clear, 0)
    o_ref[...] = jnp.zeros_like(o_ref)
    m_ref[...] = jnp.full(m_ref.shape, NEG, jnp.float32)
    l_ref[...] = jnp.zeros_like(l_ref)

    def scores(slots, chunk):
        return dot(ks[rows_of(chunk), :], side(qd, slots, 0), 1, 1) * C2

    def accumulate(slots, chunk, s, top, kept_m, n):
        m = side(m_ref, slots, 1)
        m2 = jnp.maximum(m, top)
        a = jnp.exp2(m - m2)
        p = jnp.exp2(s - m2)
        l2 = side(l_ref, slots, 1) * a + jnp.sum(p, axis=0, keepdims=True)
        pb = p.astype(jnp.bfloat16)
        kept_m[n] = m2
        o = dot(vt[:, rows_of(chunk)], pb, 1, 0)
        for i, t in enumerate(slots):
            at = slice(i * COLS, (i + 1) * COLS)
            kept[t, rows_of(chunk), :] = pb[:, at]
            m_ref[t] = m2[:, at]
            l_ref[t] = l2[:, at]
            o_ref[t] = o_ref[t] * a[:, at] + o[:, at]

    def item(n):
        return [tab[PAIR_A + n], tab[PAIR_B + n]], tab[PAIR_C + n]

    def produce(n, buf, top):
        slots, chunk = item(n)
        s = scores(slots, chunk)
        buf[...] = s
        top[...] = jnp.max(s, axis=0, keepdims=True)

    def fix(n, buf, top):
        @pl.when(tab[PAIR_F + n] == 1)
        def _():
            slots, chunk = item(n)
            s = jnp.where(visible(tab, slots, chunk), buf[...], NEG)
            buf[...] = s
            top[...] = jnp.max(s, axis=0, keepdims=True)

    def consume(n, buf, top):
        slots, chunk = item(n)
        accumulate(slots, chunk, buf[...], top[...], pairs_m, n)

    count = tab[PAIRS]

    @pl.when(count > 0)
    def _():
        produce(0, s0, x0)
        fix(0, s0, x0)

    def two(i, _):
        plain = tab[PAIR_F + 2 * i + 1] + tab[PAIR_F + 2 * i + 2] == 0

        def items(fixed):
            produce(2 * i + 1, s1, x1)
            consume(2 * i, s0, x0)
            if fixed:
                fix(2 * i + 1, s1, x1)
            produce(2 * i + 2, s0, x0)
            consume(2 * i + 1, s1, x1)
            if fixed:
                fix(2 * i + 2, s0, x0)

        @pl.when(plain)
        def _():
            items(False)

        @pl.when(jnp.logical_not(plain))
        def _():
            items(True)
        return 0
    lax.fori_loop(0, count // 2, two, 0)

    @pl.when(count % 2 == 1)
    def _():
        consume(count - 1, s0, x0)

    def one(n, _):
        slots, chunk = [tab[ONE_T + n]], tab[ONE_C + n]
        s = jnp.where(visible(tab, slots, chunk), scores(slots, chunk), NEG)
        accumulate(slots, chunk, s, jnp.max(s, axis=0, keepdims=True), ones_m, n)
        return 0
    several(0, tab[ONES], 2, one)


def several(first, count, size, body):
    def group(i, _):
        for j in range(size):
            body(first + i * size + j, 0)
        return 0
    groups = (count - first) // size
    lax.fori_loop(0, groups, group, 0)
    lax.fori_loop(first + groups * size, count, body, 0)


def bwd_kernel(tab, qd, gt, vs, ls_ref, de_ref, kept, pairs_m, ones_m, ds_ref, dk_ref, dv_ref, dks, dvs):
    pairs, ones = tab[PAIRS], tab[ONES]
    dks[...] = jnp.zeros_like(dks)
    dvs[...] = jnp.zeros_like(dvs)

    def step(slots, chunk, m):
        at = rows_of(chunk)
        part = jnp.exp2(m - side(ls_ref, slots, 1))
        gs = (side(gt, slots, 1).astype(jnp.float32) * part).astype(jnp.bfloat16)
        p = jnp.concatenate([kept[t, at, :] for t in slots], axis=1)
        dp = dot(vs[at, :], gs, 1, 0)
        ds = p * (dp - side(de_ref, slots, 1) * part).astype(jnp.bfloat16)
        dvs[at, :] += dot(p, gs, 1, 1)
        dks[at, :] += dot(ds, side(qd, slots, 0), 1, 0)
        for i, t in enumerate(slots):
            ds_ref[t, at, :] = ds[:, i * COLS:(i + 1) * COLS]

    def pair(n, _):
        step([tab[PAIR_A + n], tab[PAIR_B + n]], tab[PAIR_C + n], pairs_m[n])
        return 0
    several(0, pairs, 4, pair)

    def one(n, _):
        step([tab[ONE_T + n]], tab[ONE_C + n], ones_m[n])
        return 0
    several(0, ones, 2, one)

    def scatter(r, _):
        src = pl.ds(pl.multiple_of(r * SPAN, SPAN), SPAN)
        dst = pl.ds(pl.multiple_of(tab[ORDER + r] * SPAN, SPAN), SPAN)
        dk_ref[dst, :] = (dks[src, :] * SCALE).astype(jnp.bfloat16)
        dv_ref[dst, :] = dvs[src, :].astype(jnp.bfloat16)
        return 0
    lax.fori_loop(0, NK, scatter, 0)


VM = pl.BlockSpec(memory_space=pltpu.VMEM)
SM = pl.BlockSpec(memory_space=pltpu.SMEM)
ANY = pl.BlockSpec(memory_space=pl.ANY)
LIM = 18 * 1024 * 1024
LOW = 16 * 1024 * 1024
KEYS = NK * SPAN


def bf16(*shape):
    return jax.ShapeDtypeStruct(shape, jnp.bfloat16)


def single(*shape):
    return jax.ShapeDtypeStruct(shape, jnp.float32)


def vm(*shape):
    return pltpu.VMEM(shape, jnp.bfloat16)


def vm32(*shape):
    return pltpu.VMEM(shape, jnp.float32)


def cost(flops, nbytes):
    return pl.CostEstimate(flops=flops, bytes_accessed=nbytes, transcendentals=0)


def fwd(where, keys, q, k, v):
    return pl.pallas_call(
        functools.partial(fwd_kernel, where),
        out_shape=(single(NQ, 128, COLS), single(NQ, 1, COLS), single(NQ, 1, COLS), bf16(KEYS, 128), bf16(KEYS, 128),
                   jax.ShapeDtypeStruct((TABLE,), jnp.int32), vm(NQ, KEYS, COLS), single(24, 1, 2 * COLS), single(24, 1, COLS)),
        in_specs=[SM, VM, VM, VM], out_specs=(VM,) * 5 + (SM, VM, VM, VM),
        scratch_shapes=[vm(128, KEYS), vm32(CH, 2 * COLS), vm32(CH, 2 * COLS), vm32(1, 2 * COLS), vm32(1, 2 * COLS),
                        pltpu.SMEM((NQ,), jnp.int32)],
        compiler_params=pltpu.CompilerParams(vmem_limit_bytes=LIM), cost_estimate=cost(10**10, 8 * 10**6), name="fwd_k",
    )(keys, q, k, v)


def bwd(tab, q, g, v, ls, de, kept, pairs_m, ones_m):
    return pl.pallas_call(
        bwd_kernel,
        out_shape=(vm(NQ, KEYS, COLS), bf16(KEYS, 128), bf16(KEYS, 128)),
        in_specs=[SM] + [VM] * 8, out_specs=(VM, VM, VM), input_output_aliases={6: 0},
        scratch_shapes=[vm32(KEYS, 128), vm32(KEYS, 128)],
        compiler_params=pltpu.CompilerParams(vmem_limit_bytes=LIM), cost_estimate=cost(2 * 10**10, 8 * 10**6), name="bwd_k",
    )(tab, q, g, v, ls, de, kept, pairs_m, ones_m)

MESH = pl.DeviceIdType.MESH
LO, HI = pl.ds(0, SPAN), pl.ds(SPAN, SPAN)
ALL = pl.ds(0, 2 * SPAN)
OFFSETS = (0, -1, 1, 2)


def coords():
    me = lax.axis_index("ctx")
    return me // 16, (me // 4) % 4, (me // 2) % 2, me % 2


def device(y, x, z, c):
    return {"ctx": ((y + 4) % 4 * 4 + (x + 4) % 4) * 4 + z * 2 + c}


def head_at(d):
    return {"head": (lax.axis_index("head") + d + 4) % 4}


def greet(heads):
    y, x, z, c = coords()
    barrier = pltpu.get_barrier_semaphore()
    near = [(y, x, 1 - z, c), (y, x, z, 1 - c)]
    for d in (1, -1, 2):
        near += [(y, x + d, z, c), (y + d, x, z, c)]
    ids = [device(*n) for n in near]
    if heads:
        ids += [head_at(1), head_at(-1)]
    for n in ids:
        pl.semaphore_signal(barrier, inc=1, device_id=n, device_id_type=MESH)
    pl.semaphore_wait(barrier, len(ids))


def remote(src, dst, send, recv, n, to):
    return pltpu.make_async_remote_copy(
        src_ref=src, dst_ref=dst, send_sem=send.at[n], recv_sem=recv.at[n], device_id=device(*to), device_id_type=MESH
    )


def group_share(own, out, pick, send, recv, first):
    y, x, z, c = coords()
    core, chip = (y, x, z, 1 - c), (y, x, 1 - z, c)
    mine, far, beside, across = z * 2 + c, (1 - z) * 2 + c, z * 2 + 1 - c, (1 - z) * 2 + 1 - c

    def cp(src, block, n, to):
        return remote(pick(src.at[block]), pick(out.at[block]), send, recv, first + n, to)

    sends = cp(own, mine, 0, chip), cp(own, mine, 1, core), cp(out, far, 2, core)
    recvs = cp(out, far, 0, chip), cp(out, beside, 1, core), cp(out, across, 2, core)
    return sends, recvs


def plane_gather(out, send, recv, x_first):
    y, x, z, c = coords()

    def place(da, db):
        dy, dx = (db, da) if x_first else (da, db)
        return (y + dy, x + dx, z, c)

    def block(da, db):
        yy, xx, _, _ = place(da, db)
        return (yy + 4) % 4, (xx + 4) % 4

    def cp(n, sa, sb, rows, to):
        yy, xx = block(sa, sb)
        ref = out.at[yy, xx, rows]
        return remote(ref, ref, send, recv, n, place(*to))

    sends, recvs = {}, {}
    for i, d in enumerate((1, -1, 2)):
        sends["a", d] = cp(i, 0, 0, ALL, (d, 0))
        recvs["a", d] = cp(i, -d, 0, ALL, (d, 0))
    for d, half in ((1, LO), (-1, HI)):
        i = (1 - d) // 2
        for k, e in enumerate(OFFSETS):
            sends["b", e, d] = cp(4 + 4 * k + i, e, 0, ALL, (0, d))
            recvs["b", e, d] = cp(4 + 4 * k + i, e, -d, ALL, (0, d))
            sends["bb", e, d] = cp(6 + 4 * k + i, e, -d, half, (0, d))
            recvs["bb", e, d] = cp(6 + 4 * k + i, e, -2 * d, half, (0, d))
    return sends, recvs


def key_order(place, part):
    slot = lax.broadcasted_iota(jnp.int32, (128, 128), 0)
    lane = lax.broadcasted_iota(jnp.int32, (128, 128), 1)
    across = jnp.broadcast_to(f32(place), (128, 128))
    down = across.T
    position = f32(lane)
    own = jnp.where((slot % 8) // 2 == part, 1.0, 0.0)
    name = f32(slot // 8 * 2 + slot % 2)
    before = jnp.sum(jnp.where(down < position, own, 0.0), axis=0, keepdims=True)
    held = jnp.sum(jnp.where(down == position, own * (name + 1.0), 0.0), axis=0, keepdims=True) - 1.0
    own_lane = jnp.where((lane % 8) // 2 == part, 1.0, 0.0)
    rank = jnp.sum(jnp.where(across < down, own_lane, 0.0), axis=1, keepdims=True)
    order = jnp.sum(jnp.where(rank == position, own * name, 0.0), axis=0, keepdims=True)
    return jnp.concatenate([before, held, order, f32(place)], axis=0).astype(jnp.int32)


def order_kernel(place, keys):
    _, _, z, c = coords()
    keys[...] = key_order(place[...], z * 2 + c)


def share_kernel(q_ref, k_ref, v_ref, c_ref, qa, ka, va, up, down, here, qs, qr, ks, kr, vs, vr, cs, cr):
    y, x, z, c = coords()
    mine = z * 2 + c
    lo, hi = c_ref.at[LO], c_ref.at[HI]
    loads = [pltpu.make_async_copy(k_ref, ka.at[y, x], here.at[0]), pltpu.make_async_copy(v_ref, va.at[y, x], here.at[1])]
    for s in range(2):
        for h in range(4):
            loads.append(pltpu.make_async_copy(
                q_ref.at[s * SPAN:(s + 1) * SPAN, h * 128:(h + 1) * 128], qa.at[mine, s, h * SPAN:(h + 1) * SPAN],
                here.at[2 + s * 4 + h]))
    loads += [pltpu.make_async_copy(hi, up.at[0], here.at[10]), pltpu.make_async_copy(lo, down.at[0], here.at[11])]
    for load in loads:
        load.start()
    greet(True)
    to_up = pltpu.make_async_remote_copy(
        src_ref=lo, dst_ref=up.at[1], send_sem=cs.at[0], recv_sem=cr.at[0], device_id=head_at(1), device_id_type=MESH)
    to_down = pltpu.make_async_remote_copy(
        src_ref=hi, dst_ref=down.at[1], send_sem=cs.at[1], recv_sem=cr.at[1], device_id=head_at(-1), device_id_type=MESH)
    planes = [plane_gather(ka, ks, kr, True), plane_gather(va, vs, vr, False)]
    q_send, q_recv = group_share(qa, qa, lambda ref: ref, qs, qr, 0)
    for load in loads[:2]:
        load.wait()
    for s, _ in planes:
        for d in (1, -1, 2):
            s["a", d].start()
    for s, _ in planes:
        for d in (1, -1):
            s["b", 0, d].start()
    for load in loads[2:]:
        load.wait()
    q_send[0].start()
    q_send[1].start()
    to_up.start()
    to_down.start()
    for d, e in ((1, -1), (-1, 1)):
        for s, r in planes:
            r["a", d].wait_recv()
            s["b", e, 1].start()
            s["b", e, -1].start()
    for d in (1, -1):
        for s, r in planes:
            r["b", 0, d].wait_recv()
            s["bb", 0, d].start()
    for s, r in planes:
        r["a", 2].wait_recv()
        s["b", 2, 1].start()
        s["b", 2, -1].start()
    q_recv[0].wait_recv()
    q_send[2].start()
    for e in (-1, 1, 2):
        for d in (1, -1):
            for s, r in planes:
                r["b", e, d].wait_recv()
                s["bb", e, d].start()
    for e in OFFSETS:
        for d in (1, -1):
            for s, r in planes:
                r["bb", e, d].wait_recv()
    q_recv[1].wait_recv()
    q_recv[2].wait_recv()
    for s, _ in planes:
        for copy in s.values():
            copy.wait_send()
    for copy in q_send:
        copy.wait_send()
    to_up.wait()
    to_down.wait()


def stats_kernel(up, down, from_low, from_high, w_ref, o_ref, m_ref, l_ref, k_ref, _, gt, ls_ref, de_ref, kt, ga, part, levels, deltas, gs, gr, ss, sr):
    y, x, z, c = coords()
    mine = z * 2 + c
    head = lax.axis_index("head")
    greet_group()

    others = [(z, 1 - c), (1 - z, c), (1 - z, 1 - c)]

    def spread(ref, first):
        sent = [remote(ref.at[mine], ref.at[mine], ss, sr, first + n, (y, x, zz, cc)) for n, (zz, cc) in enumerate(others)]
        came = [remote(ref.at[zz * 2 + cc], ref.at[zz * 2 + cc], ss, sr, first + n, (y, x, zz, cc))
                for n, (zz, cc) in enumerate(others)]
        return sent, came

    for t in range(NQ):
        levels[mine, t:t + 1, :] = m_ref[t]
        levels[mine, NQ + t:NQ + t + 1, :] = l_ref[t]
    levels_sent, levels_came = spread(levels, 0)
    for copy in levels_sent:
        copy.start()

    def term(block, d, rows):
        cols = pl.ds(pl.multiple_of((head + d + 4) % 4 * 1024, 1024), 1024)
        return dot(block, w_ref[rows, cols], 1, 1)

    def whole(low, high):
        return jnp.concatenate([low, high], axis=0)

    pieces = [(j, s) for j in range(2) for s in range(2)]

    def share_piece(n, j, s):
        return group_share(ga, ga, lambda ref: ref.at[s, pl.ds(j * 2 * SPAN, 2 * SPAN)], gs, gr, 3 * n)

    shares = [share_piece(n, j, s) for n, (j, s) in enumerate(pieces)]
    blocks = [(whole(down[0], up[0]), 0), (whole(up[1], from_low[0]), -1), (whole(from_high[0], down[1]), 1),
              (whole(from_low[1], from_high[1]), 2)]
    for j in range(2):
        rows = slice(j * 256, (j + 1) * 256)
        grad = sum(term(block, d, rows) for block, d in blocks).astype(jnp.bfloat16)
        for s in range(2):
            part_rows = grad[s * SPAN:(s + 1) * SPAN]
            ga[mine, s, j * 2 * SPAN:(j + 1) * 2 * SPAN] = jnp.concatenate([part_rows[:, :128], part_rows[:, 128:]], axis=0)
            shares[2 * j + s][0][0].start()
            shares[2 * j + s][0][1].start()

    def inner(block, s):
        t = block * 2 + s
        down = ga[block, s].T
        gt[t] = down
        part[t] = jnp.sum(f32(down) * o_ref[t], axis=0, keepdims=True)

    for i in range(NK * SPAN // 512):
        kt[:, i * 512:(i + 1) * 512] = k_ref[i * 512:(i + 1) * 512, :].T
    for s in range(2):
        inner(mine, s)
    for sends, recvs in shares:
        recvs[1].wait_recv()
    for s in range(2):
        inner(z * 2 + 1 - c, s)
    for sends, recvs in shares:
        recvs[0].wait_recv()
        sends[2].start()
    for s in range(2):
        inner((1 - z) * 2 + c, s)
    for sends, recvs in shares:
        recvs[2].wait_recv()
    for s in range(2):
        inner((1 - z) * 2 + 1 - c, s)
    for t in range(NQ):
        deltas[mine, t:t + 1, :] = part[t]
    deltas_sent, deltas_came = spread(deltas, 3)
    for copy in deltas_sent:
        copy.start()
    for copy in levels_came:
        copy.wait_recv()
    tops = [levels[j, 0:NQ, :] for j in range(4)]
    top = jnp.maximum(jnp.maximum(tops[0], tops[1]), jnp.maximum(tops[2], tops[3]))
    scales = [jnp.exp2(m - top) for m in tops]
    total = sum(scales[j] * levels[j, NQ:2 * NQ, :] for j in range(4))
    level = top + jnp.log(total) * math.log2(math.e)
    for copy in deltas_came:
        copy.wait_recv()
    delta = sum(scales[j] * deltas[j] for j in range(4)) / total
    for t in range(NQ):
        ls_ref[t] = level[t:t + 1, :]
        de_ref[t] = delta[t:t + 1, :]
    for copy in levels_sent + deltas_sent:
        copy.wait_send()
    for sends, _ in shares:
        for copy in sends:
            copy.wait_send()


def greet_group():
    y, x, z, c = coords()
    barrier = pltpu.get_barrier_semaphore()
    near = [(y, x, 1 - z, c), (y, x, z, 1 - c), (y, x, 1 - z, 1 - c)]
    for n in near:
        pl.semaphore_signal(barrier, inc=1, device_id=device(*n), device_id_type=MESH)
    pl.semaphore_wait(barrier, len(near))


def f32(a):
    return a.astype(jnp.float32)


ORDER2 = (2, 1, -1, 0)


def plane_reduce(src, out, x_first, far1, near1, stage1, acc, near2, send, recv):
    y, x, z, c = coords()
    first = x if x_first else y
    second = y if x_first else x

    def to1(d):
        return (y, x + d, z, c) if x_first else (y + d, x, z, c)

    def to2(d):
        return (y + d, x, z, c) if x_first else (y, x + d, z, c)

    def place(d, k):
        i, j = (first + d + 4) % 4, (second + ORDER2[k] + 4) % 4
        return (j, i) if x_first else (i, j)

    def cp(s, t, n, to):
        return remote(s, t, send, recv, n, to)

    halves = ((0, 1, LO, HI, slice(0, SPAN)), (1, -1, HI, LO, slice(SPAN, 2 * SPAN)))
    sends = []

    def go(copy):
        copy.start()
        sends.append(copy)

    def begin():
        for k in range(4):
            for i, d, half, _, _ in halves:
                a, b = place(2, k)
                go(cp(src.at[a, b, half], far1.at[i, k], 6 * k + i, to1(d)))
        for k in range(4):
            for i, d, _, other, _ in halves:
                a, b = place(d, k)
                go(cp(src.at[a, b, other], near1.at[i, k, other], 6 * k + 2 + i, to1(d)))

    def relay(k):
        for i, d, half, _, hs in halves:
            cp(far1.at[i, k], far1.at[i, k], 6 * k + i, to1(d)).wait_recv()
            a, b = place(d, k)
            stage1[i, k] = (f32(src[a, b, hs]) + f32(far1[i, k])).astype(jnp.bfloat16)
            go(cp(stage1.at[i, k], near1.at[i, k, half], 6 * k + 4 + i, to1(d)))

    def turn(k):
        for i, d, half, other, _ in halves:
            cp(near1.at[i, k, other], near1.at[i, k, other], 6 * k + 2 + i, to1(d)).wait_recv()
            cp(near1.at[i, k, half], near1.at[i, k, half], 6 * k + 4 + i, to1(d)).wait_recv()
        a, b = place(0, k)
        acc[k] = (f32(src[a, b]) + f32(near1[0, k]) + f32(near1[1, k])).astype(jnp.bfloat16)
        if k < 3:
            go(cp(acc.at[k], near2.at[k], 24 + k, to2(ORDER2[k])))

    def end():
        for k in range(3):
            cp(near2.at[k], near2.at[k], 24 + k, to2(ORDER2[k])).wait_recv()
        out[...] = (f32(acc[3]) + f32(near2[0]) + f32(near2[1]) + f32(near2[2])).astype(jnp.bfloat16)

    def finish():
        for copy in sends:
            copy.wait_send()

    return begin, relay, turn, end, finish


def reduce_kernel(ds_ref, kt, dk_ref, dv_ref, qo, ko, vo, dq, q1, q2, qstage, qs, qr, *rest):
    y, x, z, c = coords()
    greet(False)
    core, chip = (y, x, z, 1 - c), (y, x, 1 - z, c)
    sums = [plane_reduce(dk_ref, ko, False, *rest[:7]), plane_reduce(dv_ref, vo, True, *rest[7:])]
    other = remote(dq.at[(1 - z) * 2 + 1 - c], q1.at[1 - z], qs, qr, 0, core)
    same = remote(dq.at[z * 2 + 1 - c], q1.at[z], qs, qr, 1, core)
    across = remote(qstage, q2, qs, qr, 2, chip)

    def query_terms(block):
        def slot(s, _):
            dq[block, s] = (dot(kt[...], ds_ref[block * 2 + s], 1, 0).T * SCALE).astype(jnp.bfloat16)
            return 0
        lax.fori_loop(0, 2, slot, 0)

    for begin, _, _, _, _ in sums:
        begin()
    query_terms((1 - z) * 2 + 1 - c)
    other.start()
    query_terms((1 - z) * 2 + c)
    for k in range(4):
        for _, relay, _, _, _ in sums:
            relay(k)
    other.wait_recv()
    qstage[...] = (f32(dq[(1 - z) * 2 + c]) + f32(q1[1 - z])).astype(jnp.bfloat16)
    across.start()
    query_terms(z * 2 + 1 - c)
    same.start()
    query_terms(z * 2 + c)
    for k in range(4):
        for _, _, turn, _, _ in sums:
            turn(k)
    for _, _, _, end, _ in sums:
        end()
    same.wait_recv()
    across.wait_recv()
    total = (f32(dq[z * 2 + c]) + f32(q1[z]) + f32(q2[...])).astype(jnp.bfloat16)
    for s in range(2):
        for h in range(4):
            qo[s * SPAN:(s + 1) * SPAN, h * 128:(h + 1) * 128] = total[s, h * SPAN:(h + 1) * SPAN]
    for _, _, _, _, finish_all in sums:
        finish_all()
    for copy in (other, same, across):
        copy.wait_send()


def sems(n):
    return [pltpu.SemaphoreType.DMA((n,)), pltpu.SemaphoreType.DMA((n,))]


def remote_params(n, limit=LOW):
    return pltpu.CompilerParams(collective_id=n, has_side_effects=True, vmem_limit_bytes=limit)


def key_table(place):
    return pl.pallas_call(
        order_kernel, out_shape=jax.ShapeDtypeStruct((4, 128), jnp.int32), in_specs=[VM], out_specs=VM,
        compiler_params=pltpu.CompilerParams(vmem_limit_bytes=LIM), cost_estimate=cost(10**10, 10**6), name="order_k",
    )(place)


def finish_kernel(*refs):
    sems = refs[-1]
    copies = [pltpu.make_async_copy(refs[i], refs[3 + i], sems.at[i]) for i in range(3)]
    for copy in copies:
        copy.start()
    for copy in copies:
        copy.wait()


def finish(*args):
    return pl.pallas_call(
        finish_kernel, out_shape=tuple(bf16(*a.shape) for a in args), in_specs=[VM] * 3, out_specs=(ANY,) * 3,
        scratch_shapes=[pltpu.SemaphoreType.DMA((3,))],
        compiler_params=pltpu.CompilerParams(vmem_limit_bytes=LIM), cost_estimate=cost(10**6, 10**6), name="finish_k",
    )(*args)


def share(*args):
    return pl.pallas_call(
        share_kernel,
        out_shape=(bf16(4, 2, COLS, 128), bf16(4, 4, 192, 128), bf16(4, 4, 192, 128), bf16(2, SPAN, 1024), bf16(2, SPAN, 1024)),
        in_specs=[ANY] * 4, out_specs=(VM,) * 5,
        scratch_shapes=[pltpu.SemaphoreType.DMA((12,))] + sems(3) + sems(20) + sems(20) + sems(2),
        compiler_params=remote_params(0), cost_estimate=cost(10**10, 8 * 10**6), name="share_k",
    )(*[pltpu.with_memory_space_constraint(a, pltpu.HBM) for a in args])


def stats(*args):
    return pl.pallas_call(
        stats_kernel,
        out_shape=(bf16(NQ, 128, COLS), single(NQ, 1, COLS), single(NQ, 1, COLS), bf16(128, KEYS)),
        in_specs=[VM] * 10, out_specs=(VM,) * 4,
        scratch_shapes=[vm(4, 2, COLS, 128), vm32(NQ, 1, COLS), vm32(4, 2 * NQ, COLS), vm32(4, NQ, COLS)] + sems(12) + sems(6),
        compiler_params=remote_params(1), cost_estimate=cost(10**9, 8 * 10**6), name="stats_k",
    )(*args)


def reduce(ds, kt, dk, dv):
    plane = [vm(2, 4, SPAN, 128), vm(2, 4, 2 * SPAN, 128), vm(2, 4, SPAN, 128), vm(4, 2 * SPAN, 128),
             vm(3, 2 * SPAN, 128)] + sems(27)
    return pl.pallas_call(
        reduce_kernel,
        out_shape=(bf16(192, 512), bf16(192, 128), bf16(192, 128)),
        in_specs=[VM] * 4, out_specs=(VM,) * 3,
        scratch_shapes=[vm(4, 2, COLS, 128), vm(2, 2, COLS, 128), vm(2, COLS, 128), vm(2, COLS, 128)] + sems(3) + plane + plane,
        compiler_params=remote_params(2), name="reduce_k",
    )(ds, kt, dk, dv)


def where():
    y, x, z, c = coords()
    return y * 4 + x, z * 2 + c


def local(placement, queries, keys, values, cotangent, out_weight):
    order = key_table(placement.reshape(1, 128))
    q_all, k_all, v_all, up, down = share(queries, keys, values, cotangent)
    from_low = lax.ppermute(up, "head", [(i, (i + 1) % 4) for i in range(4)])
    from_high = lax.ppermute(down, "head", [(i, (i + 3) % 4) for i in range(4)])
    q_all = q_all.reshape(NQ, COLS, 128)
    o, m, l, ks, vs, tab, kept, pairs_m, ones_m = fwd(where, order, q_all, k_all.reshape(KEYS, 128), v_all.reshape(KEYS, 128))
    kept = pltpu.with_memory_space_constraint(kept, pltpu.VMEM)
    gt, ls, de, kt = stats(up, down, from_low, from_high, out_weight, o, m, l, ks, kept)
    ds, dk, dv = bwd(tab, q_all, gt, vs, ls, de, kept, pairs_m, ones_m)
    ds = pltpu.with_memory_space_constraint(ds, pltpu.VMEM)
    return finish(*reduce(ds, kt, dk.reshape(4, 4, 192, 128), dv.reshape(4, 4, 192, 128)))


def solution(mesh):
    in_specs = (P(), P("ctx", "head"), P("ctx", "head"), P("ctx", "head"), P("ctx", "head"), P("head", None))
    out_specs = (P("ctx", "head"), P("ctx", "head"), P("ctx", "head"))
    return jax.shard_map(local, mesh=mesh, in_specs=in_specs, out_specs=out_specs, check_vma=False)
```

```python
import functools
import math

import jax
import jax.numpy as jnp
from jax import lax
from jax.experimental import pallas as pl
from jax.experimental.pallas import tpu as pltpu
from jax.sharding import PartitionSpec as P

SPAN = 96
SCALE = 1.0 / math.sqrt(128.0)
C2 = math.log2(math.e) * SCALE
NEG = -1e30
NQ = 8
NK = 32
CH = 512
COLS = 4 * SPAN
PAIR_A, PAIR_B, PAIR_C, PAIR_F, ONE_T, ONE_C, FULL, OWN, ORDER, PAIRS, ONES = 0, 32, 64, 96, 128, 160, 192, 200, 208, 248, 249
TABLE = 256


def dot(a, b, ca, cb):
    return lax.dot_general(a, b, (((ca,), (cb,)), ((), ())), preferred_element_type=jnp.float32)


def int_of(flag):
    return jnp.where(flag, 1, 0).astype(jnp.int32)


def make_table(keys, plane, tab, rank):
    for r in range(NK):
        tab[ORDER + r] = keys[2, r]
    spans = [keys[3, plane * 8 + t] for t in range(NQ)]
    for t in range(NQ):
        tab[FULL + t] = keys[0, spans[t]] * SPAN
        tab[OWN + t] = int_of(keys[1, spans[t]] >= 0)
        rank[sum(int_of(spans[u] < spans[t]) for u in range(NQ) if u != t)] = t

    def pair(i, counts):
        pairs, ones = counts
        a, b = rank[2 * i], rank[2 * i + 1]
        full = tab[FULL + a]
        chunks_a = (full + tab[OWN + a] * SPAN + CH - 1) // CH
        chunks_b = (tab[FULL + b] + tab[OWN + b] * SPAN + CH - 1) // CH

        def put_pair(c, _):
            tab[PAIR_A + pairs + c] = a
            tab[PAIR_B + pairs + c] = b
            tab[PAIR_C + pairs + c] = c
            tab[PAIR_F + pairs + c] = int_of((c + 1) * CH > full)
            return 0
        lax.fori_loop(0, chunks_a, put_pair, 0)

        def put_one(c, _):
            tab[ONE_T + ones + c - chunks_a] = b
            tab[ONE_C + ones + c - chunks_a] = c
            return 0
        lax.fori_loop(chunks_a, chunks_b, put_one, 0)
        return pairs + chunks_a, ones + jnp.maximum(chunks_b - chunks_a, 0)
    pairs, ones = lax.fori_loop(0, NQ // 2, pair, (jnp.int32(0), jnp.int32(0)))
    tab[PAIRS] = pairs
    tab[ONES] = ones
    tab[PAIR_A + pairs] = 0
    tab[PAIR_B + pairs] = 1
    tab[PAIR_C + pairs] = 0
    tab[PAIR_F + pairs] = 0


def limits(tab, slots):
    col = lax.broadcasted_iota(jnp.int32, (1, COLS), 1)
    sub = 32 * ((col % SPAN) // 32 + 1)
    return jnp.concatenate([tab[FULL + t] + tab[OWN + t] * sub for t in slots], axis=1)


def visible(tab, slots, chunk):
    idx = lax.broadcasted_iota(jnp.int32, (CH, COLS * len(slots)), 0)
    return idx < limits(tab, slots) - chunk * CH


def side(ref, slots, axis):
    return jnp.concatenate([ref[t] for t in slots], axis=axis) if len(slots) > 1 else ref[slots[0]]


def rows_of(chunk):
    return pl.ds(pl.multiple_of(chunk * CH, CH), CH)


def fwd_kernel(where, keys, qd, k_ref, v_ref, o_ref, m_ref, l_ref, ks, vs, tab, kept, pairs_m, ones_m,
               vt, s0, s1, x0, x1, rank):
    plane, _ = where()
    make_table(keys, plane, tab, rank)

    def sort(r, _):
        src = pl.ds(pl.multiple_of(tab[ORDER + r] * SPAN, SPAN), SPAN)
        dst = pl.ds(pl.multiple_of(r * SPAN, SPAN), SPAN)
        ks[dst, :] = k_ref[src, :]
        vs[dst, :] = v_ref[src, :]
        return 0
    lax.fori_loop(0, NK, sort, 0)
    for i in range(NK * SPAN // 512):
        vt[:, i * 512:(i + 1) * 512] = vs[i * 512:(i + 1) * 512, :].T

    def clear(t, _):
        first = (tab[FULL + t] + tab[OWN + t] * SPAN + CH - 1) // CH

        def unseen(chunk, _):
            kept[t, rows_of(chunk), :] = jnp.zeros((CH, COLS), jnp.bfloat16)
            return 0
        return lax.fori_loop(first, KEYS // CH, unseen, 0)
    lax.fori_loop(0, NQ, clear, 0)
    o_ref[...] = jnp.zeros_like(o_ref)
    m_ref[...] = jnp.full(m_ref.shape, NEG, jnp.float32)
    l_ref[...] = jnp.zeros_like(l_ref)

    def scores(slots, chunk):
        return dot(ks[rows_of(chunk), :], side(qd, slots, 0), 1, 1) * C2

    def accumulate(slots, chunk, s, top, kept_m, n):
        m = side(m_ref, slots, 1)
        m2 = jnp.maximum(m, top)
        a = jnp.exp2(m - m2)
        p = jnp.exp2(s - m2)
        l2 = side(l_ref, slots, 1) * a + jnp.sum(p, axis=0, keepdims=True)
        pb = p.astype(jnp.bfloat16)
        kept_m[n] = m2
        o = dot(vt[:, rows_of(chunk)], pb, 1, 0)
        for i, t in enumerate(slots):
            at = slice(i * COLS, (i + 1) * COLS)
            kept[t, rows_of(chunk), :] = pb[:, at]
            m_ref[t] = m2[:, at]
            l_ref[t] = l2[:, at]
            o_ref[t] = o_ref[t] * a[:, at] + o[:, at]

    def item(n):
        return [tab[PAIR_A + n], tab[PAIR_B + n]], tab[PAIR_C + n]

    def produce(n, buf, top):
        slots, chunk = item(n)
        s = scores(slots, chunk)
        buf[...] = s
        top[...] = jnp.max(s, axis=0, keepdims=True)

    def fix(n, buf, top):
        @pl.when(tab[PAIR_F + n] == 1)
        def _():
            slots, chunk = item(n)
            s = jnp.where(visible(tab, slots, chunk), buf[...], NEG)
            buf[...] = s
            top[...] = jnp.max(s, axis=0, keepdims=True)

    def consume(n, buf, top):
        slots, chunk = item(n)
        accumulate(slots, chunk, buf[...], top[...], pairs_m, n)

    count = tab[PAIRS]

    @pl.when(count > 0)
    def _():
        produce(0, s0, x0)
        fix(0, s0, x0)

    def two(i, _):
        plain = tab[PAIR_F + 2 * i + 1] + tab[PAIR_F + 2 * i + 2] == 0

        def items(fixed):
            produce(2 * i + 1, s1, x1)
            consume(2 * i, s0, x0)
            if fixed:
                fix(2 * i + 1, s1, x1)
            produce(2 * i + 2, s0, x0)
            consume(2 * i + 1, s1, x1)
            if fixed:
                fix(2 * i + 2, s0, x0)

        @pl.when(plain)
        def _():
            items(False)

        @pl.when(jnp.logical_not(plain))
        def _():
            items(True)
        return 0
    lax.fori_loop(0, count // 2, two, 0)

    @pl.when(count % 2 == 1)
    def _():
        consume(count - 1, s0, x0)

    def one(n, _):
        slots, chunk = [tab[ONE_T + n]], tab[ONE_C + n]
        s = jnp.where(visible(tab, slots, chunk), scores(slots, chunk), NEG)
        accumulate(slots, chunk, s, jnp.max(s, axis=0, keepdims=True), ones_m, n)
        return 0
    several(0, tab[ONES], 2, one)


def several(first, count, size, body):
    def group(i, _):
        for j in range(size):
            body(first + i * size + j, 0)
        return 0
    groups = (count - first) // size
    lax.fori_loop(0, groups, group, 0)
    lax.fori_loop(first + groups * size, count, body, 0)


def bwd_kernel(tab, qd, gt, vs, ls_ref, de_ref, kept, pairs_m, ones_m, ds_ref, dk_ref, dv_ref, dks, dvs):
    pairs, ones = tab[PAIRS], tab[ONES]
    dks[...] = jnp.zeros_like(dks)
    dvs[...] = jnp.zeros_like(dvs)

    def step(slots, chunk, m):
        at = rows_of(chunk)
        part = jnp.exp2(m - side(ls_ref, slots, 1))
        gs = (side(gt, slots, 1).astype(jnp.float32) * part).astype(jnp.bfloat16)
        p = jnp.concatenate([kept[t, at, :] for t in slots], axis=1)
        dp = dot(vs[at, :], gs, 1, 0)
        ds = p * (dp - side(de_ref, slots, 1) * part).astype(jnp.bfloat16)
        dvs[at, :] += dot(p, gs, 1, 1)
        dks[at, :] += dot(ds, side(qd, slots, 0), 1, 0)
        for i, t in enumerate(slots):
            ds_ref[t, at, :] = ds[:, i * COLS:(i + 1) * COLS]

    def pair(n, _):
        step([tab[PAIR_A + n], tab[PAIR_B + n]], tab[PAIR_C + n], pairs_m[n])
        return 0
    several(0, pairs, 4, pair)

    def one(n, _):
        step([tab[ONE_T + n]], tab[ONE_C + n], ones_m[n])
        return 0
    several(0, ones, 2, one)

    def scatter(r, _):
        src = pl.ds(pl.multiple_of(r * SPAN, SPAN), SPAN)
        dst = pl.ds(pl.multiple_of(tab[ORDER + r] * SPAN, SPAN), SPAN)
        dk_ref[dst, :] = (dks[src, :] * SCALE).astype(jnp.bfloat16)
        dv_ref[dst, :] = dvs[src, :].astype(jnp.bfloat16)
        return 0
    lax.fori_loop(0, NK, scatter, 0)


VM = pl.BlockSpec(memory_space=pltpu.VMEM)
SM = pl.BlockSpec(memory_space=pltpu.SMEM)
ANY = pl.BlockSpec(memory_space=pl.ANY)
LIM = 18 * 1024 * 1024
LOW = 16 * 1024 * 1024
KEYS = NK * SPAN


def bf16(*shape):
    return jax.ShapeDtypeStruct(shape, jnp.bfloat16)


def single(*shape):
    return jax.ShapeDtypeStruct(shape, jnp.float32)


def vm(*shape):
    return pltpu.VMEM(shape, jnp.bfloat16)


def vm32(*shape):
    return pltpu.VMEM(shape, jnp.float32)


def cost(flops, nbytes):
    return pl.CostEstimate(flops=flops, bytes_accessed=nbytes, transcendentals=0)


def fwd(where, keys, q, k, v):
    return pl.pallas_call(
        functools.partial(fwd_kernel, where),
        out_shape=(single(NQ, 128, COLS), single(NQ, 1, COLS), single(NQ, 1, COLS), bf16(KEYS, 128), bf16(KEYS, 128),
                   jax.ShapeDtypeStruct((TABLE,), jnp.int32), vm(NQ, KEYS, COLS), single(24, 1, 2 * COLS), single(24, 1, COLS)),
        in_specs=[SM, VM, VM, VM], out_specs=(VM,) * 5 + (SM, VM, VM, VM),
        scratch_shapes=[vm(128, KEYS), vm32(CH, 2 * COLS), vm32(CH, 2 * COLS), vm32(1, 2 * COLS), vm32(1, 2 * COLS),
                        pltpu.SMEM((NQ,), jnp.int32)],
        compiler_params=pltpu.CompilerParams(vmem_limit_bytes=LIM), cost_estimate=cost(10**10, 8 * 10**6), name="fwd_k",
    )(keys, q, k, v)


def bwd(tab, q, g, v, ls, de, kept, pairs_m, ones_m):
    return pl.pallas_call(
        bwd_kernel,
        out_shape=(vm(NQ, KEYS, COLS), bf16(KEYS, 128), bf16(KEYS, 128)),
        in_specs=[SM] + [VM] * 8, out_specs=(VM, VM, VM), input_output_aliases={6: 0},
        scratch_shapes=[vm32(KEYS, 128), vm32(KEYS, 128)],
        compiler_params=pltpu.CompilerParams(vmem_limit_bytes=LIM), cost_estimate=cost(2 * 10**10, 8 * 10**6), name="bwd_k",
    )(tab, q, g, v, ls, de, kept, pairs_m, ones_m)

MESH = pl.DeviceIdType.MESH
LO, HI = pl.ds(0, SPAN), pl.ds(SPAN, SPAN)
ALL = pl.ds(0, 2 * SPAN)
OFFSETS = (0, -1, 1, 2)


def coords():
    me = lax.axis_index("ctx")
    return me // 16, (me // 4) % 4, (me // 2) % 2, me % 2


def device(y, x, z, c):
    return {"ctx": ((y + 4) % 4 * 4 + (x + 4) % 4) * 4 + z * 2 + c}


def head_at(d):
    return {"head": (lax.axis_index("head") + d + 4) % 4}


def greet(heads):
    y, x, z, c = coords()
    barrier = pltpu.get_barrier_semaphore()
    near = [(y, x, 1 - z, c), (y, x, z, 1 - c)]
    for d in (1, -1, 2):
        near += [(y, x + d, z, c), (y + d, x, z, c)]
    ids = [device(*n) for n in near]
    if heads:
        ids += [head_at(1), head_at(-1)]
    for n in ids:
        pl.semaphore_signal(barrier, inc=1, device_id=n, device_id_type=MESH)
    pl.semaphore_wait(barrier, len(ids))


def remote(src, dst, send, recv, n, to):
    return pltpu.make_async_remote_copy(
        src_ref=src, dst_ref=dst, send_sem=send.at[n], recv_sem=recv.at[n], device_id=device(*to), device_id_type=MESH
    )


def group_share(own, out, pick, send, recv, first):
    y, x, z, c = coords()
    core, chip = (y, x, z, 1 - c), (y, x, 1 - z, c)
    mine, far, beside, across = z * 2 + c, (1 - z) * 2 + c, z * 2 + 1 - c, (1 - z) * 2 + 1 - c

    def cp(src, block, n, to):
        return remote(pick(src.at[block]), pick(out.at[block]), send, recv, first + n, to)

    sends = cp(own, mine, 0, chip), cp(own, mine, 1, core), cp(out, far, 2, core)
    recvs = cp(out, far, 0, chip), cp(out, beside, 1, core), cp(out, across, 2, core)
    return sends, recvs


def plane_gather(out, send, recv, x_first):
    y, x, z, c = coords()

    def place(da, db):
        dy, dx = (db, da) if x_first else (da, db)
        return (y + dy, x + dx, z, c)

    def block(da, db):
        yy, xx, _, _ = place(da, db)
        return (yy + 4) % 4, (xx + 4) % 4

    def cp(n, sa, sb, rows, to):
        yy, xx = block(sa, sb)
        ref = out.at[yy, xx, rows]
        return remote(ref, ref, send, recv, n, place(*to))

    sends, recvs = {}, {}
    for i, d in enumerate((1, -1, 2)):
        sends["a", d] = cp(i, 0, 0, ALL, (d, 0))
        recvs["a", d] = cp(i, -d, 0, ALL, (d, 0))
    for d, half in ((1, LO), (-1, HI)):
        i = (1 - d) // 2
        for k, e in enumerate(OFFSETS):
            sends["b", e, d] = cp(4 + 4 * k + i, e, 0, ALL, (0, d))
            recvs["b", e, d] = cp(4 + 4 * k + i, e, -d, ALL, (0, d))
            sends["bb", e, d] = cp(6 + 4 * k + i, e, -d, half, (0, d))
            recvs["bb", e, d] = cp(6 + 4 * k + i, e, -2 * d, half, (0, d))
    return sends, recvs


def key_order(place, part):
    slot = lax.broadcasted_iota(jnp.int32, (128, 128), 0)
    lane = lax.broadcasted_iota(jnp.int32, (128, 128), 1)
    across = jnp.broadcast_to(f32(place), (128, 128))
    down = across.T
    position = f32(lane)
    own = jnp.where((slot % 8) // 2 == part, 1.0, 0.0)
    name = f32(slot // 8 * 2 + slot % 2)
    before = jnp.sum(jnp.where(down < position, own, 0.0), axis=0, keepdims=True)
    held = jnp.sum(jnp.where(down == position, own * (name + 1.0), 0.0), axis=0, keepdims=True) - 1.0
    own_lane = jnp.where((lane % 8) // 2 == part, 1.0, 0.0)
    rank = jnp.sum(jnp.where(across < down, own_lane, 0.0), axis=1, keepdims=True)
    order = jnp.sum(jnp.where(rank == position, own * name, 0.0), axis=0, keepdims=True)
    return jnp.concatenate([before, held, order, f32(place)], axis=0).astype(jnp.int32)


def order_kernel(place, keys):
    _, _, z, c = coords()
    keys[...] = key_order(place[...], z * 2 + c)


def share_kernel(q_ref, k_ref, v_ref, c_ref, qa, ka, va, up, down, here, qs, qr, ks, kr, vs, vr, cs, cr):
    y, x, z, c = coords()
    mine = z * 2 + c
    lo, hi = c_ref.at[LO], c_ref.at[HI]
    loads = [pltpu.make_async_copy(k_ref, ka.at[y, x], here.at[0]), pltpu.make_async_copy(v_ref, va.at[y, x], here.at[1])]
    for s in range(2):
        for h in range(4):
            loads.append(pltpu.make_async_copy(
                q_ref.at[s * SPAN:(s + 1) * SPAN, h * 128:(h + 1) * 128], qa.at[mine, s, h * SPAN:(h + 1) * SPAN],
                here.at[2 + s * 4 + h]))
    loads += [pltpu.make_async_copy(hi, up.at[0], here.at[10]), pltpu.make_async_copy(lo, down.at[0], here.at[11])]
    for load in loads:
        load.start()
    greet(True)
    to_up = pltpu.make_async_remote_copy(
        src_ref=lo, dst_ref=up.at[1], send_sem=cs.at[0], recv_sem=cr.at[0], device_id=head_at(1), device_id_type=MESH)
    to_down = pltpu.make_async_remote_copy(
        src_ref=hi, dst_ref=down.at[1], send_sem=cs.at[1], recv_sem=cr.at[1], device_id=head_at(-1), device_id_type=MESH)
    to_up.start()
    to_down.start()
    planes = [plane_gather(ka, ks, kr, True), plane_gather(va, vs, vr, False)]
    q_send, q_recv = group_share(qa, qa, lambda ref: ref, qs, qr, 0)
    for load in loads[:2]:
        load.wait()
    for s, _ in planes:
        for d in (1, -1, 2):
            s["a", d].start()
    for s, _ in planes:
        for d in (1, -1):
            s["b", 0, d].start()
    for load in loads[2:]:
        load.wait()
    q_send[0].start()
    q_send[1].start()
    for d, e in ((1, -1), (-1, 1)):
        for s, r in planes:
            r["a", d].wait_recv()
            s["b", e, 1].start()
            s["b", e, -1].start()
    for d in (1, -1):
        for s, r in planes:
            r["b", 0, d].wait_recv()
            s["bb", 0, d].start()
    for s, r in planes:
        r["a", 2].wait_recv()
        s["b", 2, 1].start()
        s["b", 2, -1].start()
    q_recv[0].wait_recv()
    q_send[2].start()
    for e in (-1, 1, 2):
        for d in (1, -1):
            for s, r in planes:
                r["b", e, d].wait_recv()
                s["bb", e, d].start()
    for e in OFFSETS:
        for d in (1, -1):
            for s, r in planes:
                r["bb", e, d].wait_recv()
    q_recv[1].wait_recv()
    q_recv[2].wait_recv()
    for s, _ in planes:
        for copy in s.values():
            copy.wait_send()
    for copy in q_send:
        copy.wait_send()
    to_up.wait()
    to_down.wait()


def stats_kernel(up, down, from_low, from_high, w_ref, o_ref, m_ref, l_ref, k_ref, _, gt, ls_ref, de_ref, kt, ga, part, levels, deltas, gs, gr, ss, sr):
    y, x, z, c = coords()
    mine = z * 2 + c
    head = lax.axis_index("head")
    greet_group()

    others = [(z, 1 - c), (1 - z, c), (1 - z, 1 - c)]

    def spread(ref, first):
        sent = [remote(ref.at[mine], ref.at[mine], ss, sr, first + n, (y, x, zz, cc)) for n, (zz, cc) in enumerate(others)]
        came = [remote(ref.at[zz * 2 + cc], ref.at[zz * 2 + cc], ss, sr, first + n, (y, x, zz, cc))
                for n, (zz, cc) in enumerate(others)]
        return sent, came

    for t in range(NQ):
        levels[mine, t:t + 1, :] = m_ref[t]
        levels[mine, NQ + t:NQ + t + 1, :] = l_ref[t]
    levels_sent, levels_came = spread(levels, 0)
    for copy in levels_sent:
        copy.start()

    def term(block, d, rows):
        cols = pl.ds(pl.multiple_of((head + d + 4) % 4 * 1024, 1024), 1024)
        return dot(block, w_ref[rows, cols], 1, 1)

    def whole(low, high):
        return jnp.concatenate([low, high], axis=0)

    pieces = [(j, s) for j in range(2) for s in range(2)]

    def share_piece(n, j, s):
        return group_share(ga, ga, lambda ref: ref.at[s, pl.ds(j * 2 * SPAN, 2 * SPAN)], gs, gr, 3 * n)

    shares = [share_piece(n, j, s) for n, (j, s) in enumerate(pieces)]
    blocks = [(whole(down[0], up[0]), 0), (whole(up[1], from_low[0]), -1), (whole(from_high[0], down[1]), 1),
              (whole(from_low[1], from_high[1]), 2)]
    for j in range(2):
        rows = slice(j * 256, (j + 1) * 256)
        grad = sum(term(block, d, rows) for block, d in blocks).astype(jnp.bfloat16)
        for s in range(2):
            part_rows = grad[s * SPAN:(s + 1) * SPAN]
            ga[mine, s, j * 2 * SPAN:(j + 1) * 2 * SPAN] = jnp.concatenate([part_rows[:, :128], part_rows[:, 128:]], axis=0)
            shares[2 * j + s][0][0].start()
            shares[2 * j + s][0][1].start()

    def inner(block, s):
        t = block * 2 + s
        down = ga[block, s].T
        gt[t] = down
        part[t] = jnp.sum(f32(down) * o_ref[t], axis=0, keepdims=True)

    for i in range(NK * SPAN // 512):
        kt[:, i * 512:(i + 1) * 512] = k_ref[i * 512:(i + 1) * 512, :].T
    for s in range(2):
        inner(mine, s)
    for sends, recvs in shares:
        recvs[1].wait_recv()
    for s in range(2):
        inner(z * 2 + 1 - c, s)
    for sends, recvs in shares:
        recvs[0].wait_recv()
        sends[2].start()
    for s in range(2):
        inner((1 - z) * 2 + c, s)
    for sends, recvs in shares:
        recvs[2].wait_recv()
    for s in range(2):
        inner((1 - z) * 2 + 1 - c, s)
    for t in range(NQ):
        deltas[mine, t:t + 1, :] = part[t]
    deltas_sent, deltas_came = spread(deltas, 3)
    for copy in deltas_sent:
        copy.start()
    for copy in levels_came:
        copy.wait_recv()
    tops = [levels[j, 0:NQ, :] for j in range(4)]
    top = jnp.maximum(jnp.maximum(tops[0], tops[1]), jnp.maximum(tops[2], tops[3]))
    scales = [jnp.exp2(m - top) for m in tops]
    total = sum(scales[j] * levels[j, NQ:2 * NQ, :] for j in range(4))
    level = top + jnp.log(total) * math.log2(math.e)
    for copy in deltas_came:
        copy.wait_recv()
    delta = sum(scales[j] * deltas[j] for j in range(4)) / total
    for t in range(NQ):
        ls_ref[t] = level[t:t + 1, :]
        de_ref[t] = delta[t:t + 1, :]
    for copy in levels_sent + deltas_sent:
        copy.wait_send()
    for sends, _ in shares:
        for copy in sends:
            copy.wait_send()


def greet_group():
    y, x, z, c = coords()
    barrier = pltpu.get_barrier_semaphore()
    near = [(y, x, 1 - z, c), (y, x, z, 1 - c), (y, x, 1 - z, 1 - c)]
    for n in near:
        pl.semaphore_signal(barrier, inc=1, device_id=device(*n), device_id_type=MESH)
    pl.semaphore_wait(barrier, len(near))


def f32(a):
    return a.astype(jnp.float32)


ORDER2 = (2, 1, -1, 0)


def plane_reduce(src, out, x_first, far1, near1, stage1, acc, near2, send, recv):
    y, x, z, c = coords()
    first = x if x_first else y
    second = y if x_first else x

    def to1(d):
        return (y, x + d, z, c) if x_first else (y + d, x, z, c)

    def to2(d):
        return (y + d, x, z, c) if x_first else (y, x + d, z, c)

    def place(d, k):
        i, j = (first + d + 4) % 4, (second + ORDER2[k] + 4) % 4
        return (j, i) if x_first else (i, j)

    def cp(s, t, n, to):
        return remote(s, t, send, recv, n, to)

    halves = ((0, 1, LO, HI, slice(0, SPAN)), (1, -1, HI, LO, slice(SPAN, 2 * SPAN)))
    sends = []

    def go(copy):
        copy.start()
        sends.append(copy)

    def begin():
        for k in range(4):
            for i, d, half, _, _ in halves:
                a, b = place(2, k)
                go(cp(src.at[a, b, half], far1.at[i, k], 6 * k + i, to1(d)))
        for k in range(4):
            for i, d, _, other, _ in halves:
                a, b = place(d, k)
                go(cp(src.at[a, b, other], near1.at[i, k, other], 6 * k + 2 + i, to1(d)))

    def relay(k):
        for i, d, half, _, hs in halves:
            cp(far1.at[i, k], far1.at[i, k], 6 * k + i, to1(d)).wait_recv()
            a, b = place(d, k)
            stage1[i, k] = (f32(src[a, b, hs]) + f32(far1[i, k])).astype(jnp.bfloat16)
            go(cp(stage1.at[i, k], near1.at[i, k, half], 6 * k + 4 + i, to1(d)))

    def turn(k):
        for i, d, half, other, _ in halves:
            cp(near1.at[i, k, other], near1.at[i, k, other], 6 * k + 2 + i, to1(d)).wait_recv()
            cp(near1.at[i, k, half], near1.at[i, k, half], 6 * k + 4 + i, to1(d)).wait_recv()
        a, b = place(0, k)
        acc[k] = (f32(src[a, b]) + f32(near1[0, k]) + f32(near1[1, k])).astype(jnp.bfloat16)
        if k < 3:
            go(cp(acc.at[k], near2.at[k], 24 + k, to2(ORDER2[k])))

    def end():
        for k in range(3):
            cp(near2.at[k], near2.at[k], 24 + k, to2(ORDER2[k])).wait_recv()
        out[...] = (f32(acc[3]) + f32(near2[0]) + f32(near2[1]) + f32(near2[2])).astype(jnp.bfloat16)

    def finish():
        for copy in sends:
            copy.wait_send()

    return begin, relay, turn, end, finish


def reduce_kernel(ds_ref, kt, dk_ref, dv_ref, qo, ko, vo, dq, q1, q2, qstage, qs, qr, *rest):
    y, x, z, c = coords()
    greet(False)
    core, chip = (y, x, z, 1 - c), (y, x, 1 - z, c)
    sums = [plane_reduce(dk_ref, ko, False, *rest[:7]), plane_reduce(dv_ref, vo, True, *rest[7:])]
    other = remote(dq.at[(1 - z) * 2 + 1 - c], q1.at[1 - z], qs, qr, 0, core)
    same = remote(dq.at[z * 2 + 1 - c], q1.at[z], qs, qr, 1, core)
    across = remote(qstage, q2, qs, qr, 2, chip)

    def query_terms(block):
        def slot(s, _):
            dq[block, s] = (dot(kt[...], ds_ref[block * 2 + s], 1, 0).T * SCALE).astype(jnp.bfloat16)
            return 0
        lax.fori_loop(0, 2, slot, 0)

    for begin, _, _, _, _ in sums:
        begin()
    query_terms((1 - z) * 2 + 1 - c)
    other.start()
    query_terms((1 - z) * 2 + c)
    for k in range(4):
        for _, relay, _, _, _ in sums:
            relay(k)
    other.wait_recv()
    qstage[...] = (f32(dq[(1 - z) * 2 + c]) + f32(q1[1 - z])).astype(jnp.bfloat16)
    across.start()
    query_terms(z * 2 + 1 - c)
    same.start()
    query_terms(z * 2 + c)
    for k in range(4):
        for _, _, turn, _, _ in sums:
            turn(k)
    for _, _, _, end, _ in sums:
        end()
    same.wait_recv()
    across.wait_recv()
    total = (f32(dq[z * 2 + c]) + f32(q1[z]) + f32(q2[...])).astype(jnp.bfloat16)
    for s in range(2):
        for h in range(4):
            qo[s * SPAN:(s + 1) * SPAN, h * 128:(h + 1) * 128] = total[s, h * SPAN:(h + 1) * SPAN]
    for _, _, _, _, finish_all in sums:
        finish_all()
    for copy in (other, same, across):
        copy.wait_send()


def sems(n):
    return [pltpu.SemaphoreType.DMA((n,)), pltpu.SemaphoreType.DMA((n,))]


def remote_params(n, limit=LOW):
    return pltpu.CompilerParams(collective_id=n, has_side_effects=True, vmem_limit_bytes=limit)


def key_table(place):
    return pl.pallas_call(
        order_kernel, out_shape=jax.ShapeDtypeStruct((4, 128), jnp.int32), in_specs=[VM], out_specs=VM,
        compiler_params=pltpu.CompilerParams(vmem_limit_bytes=LIM), cost_estimate=cost(10**10, 10**6), name="order_k",
    )(place)


def finish_kernel(*refs):
    sems = refs[-1]
    copies = [pltpu.make_async_copy(refs[i], refs[3 + i], sems.at[i]) for i in range(3)]
    for copy in copies:
        copy.start()
    for copy in copies:
        copy.wait()


def finish(*args):
    return pl.pallas_call(
        finish_kernel, out_shape=tuple(bf16(*a.shape) for a in args), in_specs=[VM] * 3, out_specs=(ANY,) * 3,
        scratch_shapes=[pltpu.SemaphoreType.DMA((3,))],
        compiler_params=pltpu.CompilerParams(vmem_limit_bytes=LIM), cost_estimate=cost(10**6, 10**6), name="finish_k",
    )(*args)


def share(*args):
    return pl.pallas_call(
        share_kernel,
        out_shape=(bf16(4, 2, COLS, 128), bf16(4, 4, 192, 128), bf16(4, 4, 192, 128), bf16(2, SPAN, 1024), bf16(2, SPAN, 1024)),
        in_specs=[ANY] * 4, out_specs=(VM,) * 5,
        scratch_shapes=[pltpu.SemaphoreType.DMA((12,))] + sems(3) + sems(20) + sems(20) + sems(2),
        compiler_params=remote_params(0), cost_estimate=cost(10**10, 8 * 10**6), name="share_k",
    )(*[pltpu.with_memory_space_constraint(a, pltpu.HBM) for a in args])


def stats(*args):
    return pl.pallas_call(
        stats_kernel,
        out_shape=(bf16(NQ, 128, COLS), single(NQ, 1, COLS), single(NQ, 1, COLS), bf16(128, KEYS)),
        in_specs=[VM] * 10, out_specs=(VM,) * 4,
        scratch_shapes=[vm(4, 2, COLS, 128), vm32(NQ, 1, COLS), vm32(4, 2 * NQ, COLS), vm32(4, NQ, COLS)] + sems(12) + sems(6),
        compiler_params=remote_params(1), cost_estimate=cost(10**9, 8 * 10**6), name="stats_k",
    )(*args)


def reduce(ds, kt, dk, dv):
    plane = [vm(2, 4, SPAN, 128), vm(2, 4, 2 * SPAN, 128), vm(2, 4, SPAN, 128), vm(4, 2 * SPAN, 128),
             vm(3, 2 * SPAN, 128)] + sems(27)
    return pl.pallas_call(
        reduce_kernel,
        out_shape=(bf16(192, 512), bf16(192, 128), bf16(192, 128)),
        in_specs=[VM] * 4, out_specs=(VM,) * 3,
        scratch_shapes=[vm(4, 2, COLS, 128), vm(2, 2, COLS, 128), vm(2, COLS, 128), vm(2, COLS, 128)] + sems(3) + plane + plane,
        compiler_params=remote_params(2), name="reduce_k",
    )(ds, kt, dk, dv)


def where():
    y, x, z, c = coords()
    return y * 4 + x, z * 2 + c


def local(placement, queries, keys, values, cotangent, out_weight):
    order = key_table(placement.reshape(1, 128))
    q_all, k_all, v_all, up, down = share(queries, keys, values, cotangent)
    from_low = lax.ppermute(up, "head", [(i, (i + 1) % 4) for i in range(4)])
    from_high = lax.ppermute(down, "head", [(i, (i + 3) % 4) for i in range(4)])
    q_all = q_all.reshape(NQ, COLS, 128)
    o, m, l, ks, vs, tab, kept, pairs_m, ones_m = fwd(where, order, q_all, k_all.reshape(KEYS, 128), v_all.reshape(KEYS, 128))
    kept = pltpu.with_memory_space_constraint(kept, pltpu.VMEM)
    gt, ls, de, kt = stats(up, down, from_low, from_high, out_weight, o, m, l, ks, kept)
    ds, dk, dv = bwd(tab, q_all, gt, vs, ls, de, kept, pairs_m, ones_m)
    ds = pltpu.with_memory_space_constraint(ds, pltpu.VMEM)
    return finish(*reduce(ds, kt, dk.reshape(4, 4, 192, 128), dv.reshape(4, 4, 192, 128)))


def solution(mesh):
    in_specs = (P(), P("ctx", "head"), P("ctx", "head"), P("ctx", "head"), P("ctx", "head"), P("head", None))
    out_specs = (P("ctx", "head"), P("ctx", "head"), P("ctx", "head"))
    return jax.shard_map(local, mesh=mesh, in_specs=in_specs, out_specs=out_specs, check_vma=False)
```
